32 devices in a mesh: parts: 2 (over y), table: 4 (over z), bal: 2 (over x), mp: 2 (over core).
Axes of the slice: x: 2, y: 2, z: 4, core: 2. Of those that a mesh axis runs over, the one named last changes fastest.
Arguments:
- table_rows: bfloat16 [8192, 512], P('table'), may hold values from -127 to 127
- row_scale: float32 [8192], P('table'), may hold values from 0.004 to 0.04
- hist_ids: int32 [64, 256], P('parts'), parts along dimension 0, may hold values from 0 to 8191, as said below
- lengths: int32 [64], P(('parts', 'table')), parts along dimension 0, may hold values from 32 to 256, as said below
- plan: int32 [64], P('parts'), parts along dimension 0, may hold values from 0 to 7, as said below
- time_bucket: int32 [64, 256], P(('parts', 'table')), parts along dimension 0, may hold values from 0 to 15
- embed_proj: bfloat16 [512, 1024], P(None, 'table'), may hold values from -0.25 to 0.25
- in_gain: float32 [1024], replicated, may hold values from 0.1 to 1.9
- qkvu_proj: bfloat16 [4, 1024, 1024], P(None, 'table', 'mp'), may hold values from -0.1875 to 0.1875
- out_gain: float32 [1024], P('mp'), may hold values from 0.1 to 1.9
- out_proj: bfloat16 [1024, 1024], P('mp', 'table'), may hold values from -0.1875 to 0.1875
- pos_bias: float32 [8, 32], P('mp'), may hold values from -4 to 4
- time_bias: float32 [8, 16], P('mp'), may hold values from -4 to 4
Outputs:
- layer_out: bfloat16 [64, 256, 1024], P(('parts', 'table', 'bal'), None, 'mp'), parts along dimension 0
The draws below stay inside these ranges and needn't reach their ends.
There are 2 independent parts, one for each index of `parts`. The reference program is written for one: setup_inputs(seed, part) draws one part's arguments, and reference() takes and returns one part's arrays. A program takes and returns all parts, laid end to end along the dimension named above; an argument that names none is the same for every part. Nothing has to cross between parts.
Inputs may be any that keep to these rules, and one draw needn't show every extreme that they name: Within each group of 8 consecutive users, plan is a permutation of 0 to 7; slot s belongs to bal index s // 4. `lengths`: every group of 8 consecutive users has a user of length 256. `hist_ids`: take the 4 users whose slots belong to one bal index of a group, and the first or the second 128 positions of their histories: at most 256 of these ids lie in one table shard (id // 2048), and exactly 256 in some shard.
All inputs are finite; a program needn't handle non-finite values.
Results may differ from the reference program's by a relative error of at most 0.0074.
Values may be sent and summed in bfloat16 or wider, within the bound.
No kernel may reach another device: no remote copies, remote signals or barrier semaphores. Data moves between devices by JAX's collectives and lax.ppermute only.
A program may use at most 320 MiB of HBM per device.

```python
import math
import jax
import jax.numpy as jnp
from jax import lax

E = 512
D = 1024
H = 8
DH = 128
POS_BUCKETS = 32
TIME_BUCKETS = 16
L = 256
U_PAIR = 4
ROWS_DEV = 2048
GROUP = 8
USERS = 32
HALF = 128
ITEMS = 8192
N_TABLE = 4
N_BAL = 2


def shared_draw(key):
    k_len, k_top, k_tie, k_hot, k_off, k_pos, k_row = jax.random.split(key, 7)
    cols = jnp.arange(GROUP, dtype=jnp.int32)[None, :]
    lens = jax.random.randint(k_len, (N_TABLE, GROUP), L // 8, L + 1)
    top = jax.random.randint(k_top, (N_TABLE, 1), 0, GROUP)
    lens = jnp.where(cols == top, L, lens)
    noise = jax.random.randint(k_tie, (N_TABLE, GROUP), 0, 1 << 20) * GROUP + cols
    jitter = jnp.argsort(jnp.argsort(noise, axis=1), axis=1).astype(jnp.int32)
    order = jnp.argsort(-(lens * GROUP + jitter), axis=1)
    ranks = jnp.arange(GROUP, dtype=jnp.int32)
    rounds = ranks // N_BAL
    within = ranks % N_BAL
    pair = jnp.where(rounds % 2 == 0, within, N_BAL - 1 - within)
    slot_of_rank = jnp.broadcast_to(pair * U_PAIR + rounds, (N_TABLE, GROUP)).astype(jnp.int32)
    plan = jnp.zeros((N_TABLE, GROUP), jnp.int32).at[jnp.arange(N_TABLE)[:, None], order].set(slot_of_rank)
    pair_of_user = plan // U_PAIR
    hot = jax.random.randint(k_hot, (N_TABLE, N_BAL, 2), 0, N_TABLE)
    hot = hot.at[0, 0, 0].set(N_TABLE - 1).at[0, 0, 1].set(0)
    hot_user = hot[jnp.arange(N_TABLE)[:, None], pair_of_user]
    capd = L // N_TABLE
    steps = jnp.arange(HALF, dtype=jnp.int32)[None, None, None, :]
    offset = jax.random.randint(k_off, (N_TABLE, GROUP, 2, 1), 0, N_TABLE - 1)
    other = (steps - capd + offset) % (N_TABLE - 1)
    other = other + (other >= hot_user[..., None]).astype(jnp.int32)
    base = jnp.where(steps < capd, hot_user[..., None], other)
    mix = jax.random.randint(k_pos, (N_TABLE, GROUP, 2, HALF), 0, 1 << 20) * HALF + steps
    perm = jnp.argsort(mix, axis=-1)
    shard = jnp.take_along_axis(base, perm, axis=-1).reshape(USERS * L)
    rows = jax.random.randint(k_row, (USERS * L,), 0, ROWS_DEV)
    highest = jnp.argmax(shard)
    lowest = jnp.argmin(shard)
    rows = rows.at[highest].set(ROWS_DEV - 1).at[lowest].set(0)
    ids = (shard * ROWS_DEV + rows).reshape(USERS, L).astype(jnp.int32)
    return (lens.reshape(USERS).astype(jnp.int32), plan.reshape(USERS), ids)


def draw_hist_ids(key, part):
    lens, plan, ids = shared_draw(key)
    return ids


def draw_lengths(key, part):
    lens, plan, ids = shared_draw(key)
    return lens


def draw_plan(key, part):
    lens, plan, ids = shared_draw(key)
    return plan


def plant(drawn, rng, low, top_value):
    extent = drawn.shape
    spot = [jax.random.randint(jax.random.fold_in(rng, axis), (), 0, extent[axis]) for axis in range(len(extent))]
    drawn = drawn.at[tuple(spot)].set(low)
    longest = extent.index(max(extent))
    spot[longest] = (spot[longest] + 1) % extent[longest]
    return drawn.at[tuple(spot)].set(top_value)


def block_scale(key, extent, cuts, least, top_value):
    factor_of = 1.0
    for dim, parts in cuts:
        draws = jax.random.uniform(jax.random.fold_in(jax.random.fold_in(key, 6), dim), (parts,), jnp.float32, least / len(cuts), top_value / len(cuts))
        factor_of = factor_of * jnp.repeat(jnp.exp(draws), extent[dim] // parts).reshape((-1,) + (1,) * (len(extent) - 1 - dim))
    return factor_of


def gaussian(key, extent, spread, limit, cuts=(), kind=jnp.bfloat16):
    loudness = block_scale(key, extent, cuts, -0.22, 0.18) if cuts else 1.0
    entries = jax.random.normal(key, extent, jnp.float32) * spread * loudness
    return jnp.minimum(jnp.maximum(entries, -limit), limit).astype(kind)


def setup_inputs(seed: int = 0, part: int = 0) -> dict:
    streams_of = jax.random.split(jax.random.key(seed), 14)
    own_keys = jax.random.split(jax.random.fold_in(streams_of[13], part), 14)
    return {
        "table_rows": gaussian(streams_of[0], (ITEMS, E), 40.0, 127.0, ((0, 4),)),
        "row_scale": jnp.clip(jnp.exp(math.log(0.04) - 2.30258502 * jax.random.uniform(streams_of[1], (ITEMS,), jnp.float32) ** block_scale(streams_of[1], (ITEMS,), ((0, 4),), -0.2, 0.2)), 0.004, 0.04),
        "hist_ids": draw_hist_ids(jax.random.fold_in(jax.random.fold_in(streams_of[13], part), 71), part),
        "lengths": draw_lengths(jax.random.fold_in(jax.random.fold_in(streams_of[13], part), 71), part),
        "plan": draw_plan(jax.random.fold_in(jax.random.fold_in(streams_of[13], part), 71), part),
        "time_bucket": plant(jax.random.randint(own_keys[5], (USERS, L), 0, TIME_BUCKETS), jax.random.fold_in(own_keys[5], 1), 0, TIME_BUCKETS - 1).astype(jnp.int32),
        "embed_proj": gaussian(streams_of[6], (E, D), E ** -0.5, 0.25, ((1, 4),)),
        "in_gain": jnp.clip(1.0 + 0.18 * jax.random.normal(streams_of[7], (D,), jnp.float32), 0.1, 1.9),
        "qkvu_proj": gaussian(streams_of[8], (4, D, H * DH), D ** -0.5, 0.1875, ((1, 4), (2, 2))),
        "out_gain": jnp.clip(1.0 + 0.18 * jax.random.normal(streams_of[9], (H * DH,), jnp.float32), 0.1, 1.9),
        "out_proj": gaussian(streams_of[10], (H * DH, D), (H * DH) ** -0.5, 0.1875, ((0, 2), (1, 4))),
        "pos_bias": gaussian(streams_of[11], (H, POS_BUCKETS), 1.0, 4.0, ((0, 2),), jnp.float32),
        "time_bias": gaussian(streams_of[12], (H, TIME_BUCKETS), 1.0, 4.0, ((0, 2),), jnp.float32),
    }


epsilon = 1e-05

def distance_bucket(length, buckets):
    pos = jnp.arange(length, dtype=jnp.int32)
    dist = jnp.maximum(pos[:, None] - pos[None, :], 0)
    count = jnp.zeros_like(dist)
    for power in range(4, 20):
        count = count + (dist >= 2 ** power).astype(jnp.int32)
    return jnp.minimum(jnp.where(dist < 16, dist, 15 + count), buckets - 1)

def reference(table_rows, row_scale, hist_ids, lengths, plan, time_bucket, embed_proj, in_gain, qkvu_proj, out_gain, out_proj, pos_bias, time_bias):
    rows = (table_rows.astype(jnp.float32) * row_scale[:, None]).astype(jnp.bfloat16)
    index = jnp.arange(USERS, dtype=jnp.int32)
    final = index // GROUP * GROUP + plan
    source = jnp.zeros((USERS,), jnp.int32).at[final].set(index)
    bucket = distance_bucket(L, POS_BUCKETS)
    pos = jnp.arange(L, dtype=jnp.int32)
    causal = pos[None, :] <= pos[:, None]
    pos_term = pos_bias[:, bucket]
    width = H * DH

    def one_user(item):
        ids, length, events = item
        emb = rows[ids]
        x = jnp.dot(emb, embed_proj, preferred_element_type=jnp.float32).astype(jnp.bfloat16)
        xf = x.astype(jnp.float32)
        mean = lax.optimization_barrier(jnp.mean(xf, axis=1, keepdims=True))
        var = lax.optimization_barrier(jnp.mean((xf - mean) ** 2, axis=1, keepdims=True))
        xn = ((xf - mean) * lax.rsqrt(var + epsilon) * in_gain).astype(jnp.bfloat16)
        proj = jnp.einsum('td,cde->cte', xn.astype(jnp.float32), qkvu_proj.astype(jnp.float32))
        act = jax.nn.silu(proj).astype(jnp.bfloat16)
        upart = act[0]
        vpart = act[1].reshape(L, H, DH).astype(jnp.float32)
        qpart = act[2].reshape(L, H, DH).astype(jnp.float32)
        kpart = act[3].reshape(L, H, DH).astype(jnp.float32)
        scores = jnp.einsum('ihe,jhe->hij', qpart, kpart) / math.sqrt(DH)
        diff = jnp.abs(events[:, None] - events[None, :])
        scores = scores + pos_term + time_bias[:, diff]
        mask = causal & (pos[None, :] < length)
        weights = jnp.where(mask[None], jax.nn.silu(scores), 0.0) / length.astype(jnp.float32)
        weights = weights.astype(jnp.bfloat16).astype(jnp.float32)
        y = jnp.einsum('hij,jhe->ihe', weights, vpart).reshape(L, width)
        total = lax.optimization_barrier(jnp.sum(y, axis=1, keepdims=True)) / width
        square = lax.optimization_barrier(jnp.sum(y * y, axis=1, keepdims=True)) / width
        normed = (y - total) * lax.rsqrt(square - total * total + epsilon) * out_gain
        mixed = (normed * upart.astype(jnp.float32)).astype(jnp.bfloat16)
        out = jnp.dot(mixed, out_proj, preferred_element_type=jnp.float32) + xf
        return out.astype(jnp.bfloat16)
    return lax.map(one_user, (hist_ids[source], lengths[source], time_bucket[source]))
```

```python
import functools
import math

import jax
import jax.numpy as jnp
from jax import lax
from jax.experimental import pallas as pl
from jax.experimental.pallas import tpu as pltpu
from jax.sharding import PartitionSpec as P

epsilon = 1e-05
BF = jnp.bfloat16
F32 = jnp.float32
VMEM_BYTES = 56 * 1024 * 1024
FAR = -1e30


def buckets_of(length, buckets):
    found = []
    for d in range(length):
        b = d if d < 16 else 15 + sum(1 for power in range(4, 20) if d >= 2**power)
        found.append(min(b, buckets - 1))
    return found


def vspec():
    return pl.BlockSpec(memory_space=pltpu.VMEM)


def sspec():
    return pl.BlockSpec(memory_space=pltpu.SMEM)


def params():
    return pltpu.CompilerParams(vmem_limit_bytes=VMEM_BYTES)


def iota(shape, axis):
    return lax.broadcasted_iota(jnp.int32, shape, axis)


def dot(a, b):
    return jnp.dot(a, b, preferred_element_type=F32)


def dot_nt(a, b):
    return lax.dot_general(a, b, (((1,), (1,)), ((), ())), preferred_element_type=F32)


class Sizes:
    def __init__(self, mesh_sizes, table_rows, hist_ids, lengths, pos_bias):
        self.n, self.bal, self.mp = mesh_sizes
        self.rows, self.width = table_rows.shape
        self.users, self.length = hist_ids.shape
        self.group = lengths.shape[0]
        self.pair = self.group // self.bal
        self.mine = self.pair // self.mp
        self.half = self.length // self.mp
        self.tokens = self.pair * self.half
        self.cap = self.pair * self.length // self.n
        self.heads = pos_bias.shape[0] * self.mp
        self.shift = self.rows.bit_length() - 1


def member(z, plan_ref, dest, slot):
    found = jnp.int32(0)
    for j in range(z.group):
        found = found + jnp.where(plan_ref[dest * z.group + j] == slot, j, 0)
    return found


def slot_of(z, mp_pos, s):
    if s < z.mine:
        return mp_pos * z.mine + s
    return (1 - mp_pos) * z.mine + (s - z.mine)


def token_ids(z, plan_ref, hist_ref, dest, bal_pos, mp_pos):
    parts = []
    for s in range(z.pair):
        slot = bal_pos * z.pair + slot_of(z, mp_pos, s)
        user = dest * z.group + member(z, plan_ref, dest, slot)
        row = hist_ref[pl.ds(user, 1), :]
        parts.append(jnp.where(mp_pos == 0, row[:, : z.half], row[:, z.half :]))
    return jnp.concatenate(parts, axis=1)


def scaled_rows(z, table_ref, scale_ref, rows_ref):
    chunk = 128

    def step(i, carry):
        start = pl.multiple_of(i * chunk, chunk)
        row = scale_ref[pl.ds(i, 1), :]
        column = jnp.broadcast_to(row, (chunk, chunk)).T
        for c in range(z.width // chunk):
            cols = slice(c * chunk, (c + 1) * chunk)
            rows_ref[pl.ds(start, chunk), cols] = (
                table_ref[pl.ds(start, chunk), cols].astype(F32) * column
            ).astype(BF)
        return carry

    lax.fori_loop(0, z.rows // chunk, step, 0)


def two_digits(values):
    row = iota((8, values.shape[1]), 0)
    high = lax.shift_right_logical(values, 7)
    low = values & 127
    return jnp.where(row == 0, high, jnp.where(row == 1, low, 0)).astype(F32).astype(BF)


def column_of(pairs):
    return (pairs[:, 0:1] * 128.0 + pairs[:, 1:2]).astype(jnp.int32)


def triangle(tokens):
    return (iota((tokens, tokens), 0) <= iota((tokens, tokens), 1)).astype(F32).astype(BF)


def send_kernel(z, plan_ref, hist_ref, table_ref, scale_ref, *refs):
    outs, rows_ref = refs[:-1], refs[-1]
    table_pos = lax.axis_index("table")
    bal_pos = lax.axis_index("bal")
    mp_pos = lax.axis_index("mp")
    scaled_rows(z, table_ref, scale_ref, rows_ref)
    tri = triangle(z.tokens)
    for k in range(1, z.n):
        dest = lax.rem(table_pos + k, z.n)
        ids = token_ids(z, plan_ref, hist_ref, dest, bal_pos, mp_pos)
        mine = lax.shift_right_logical(ids, z.shift) == table_pos
        flags = jnp.broadcast_to(mine.astype(F32), (8, z.tokens)).astype(BF)
        rank = dot(flags, tri)[0:1, :].astype(jnp.int32) - 1
        place = jnp.where(mine, rank, -1)
        compact = (iota((z.cap, z.tokens), 0) == place).astype(F32).astype(BF)
        local = column_of(dot_nt(compact, two_digits(ids & (z.rows - 1))))
        pick = (iota((z.cap, z.rows), 1) == local).astype(F32).astype(BF)
        outs[k - 1][...] = dot(pick, rows_ref[...]).astype(BF)


def keep_kernel(z, plan_ref, hist_ref, table_ref, scale_ref, own_ref, route_ref, rows_ref):
    table_pos = lax.axis_index("table")
    bal_pos = lax.axis_index("bal")
    mp_pos = lax.axis_index("mp")
    scaled_rows(z, table_ref, scale_ref, rows_ref)
    tri = triangle(z.tokens)
    ids = token_ids(z, plan_ref, hist_ref, table_pos, bal_pos, mp_pos)
    owner = lax.shift_right_logical(ids, z.shift)
    local = ids & (z.rows - 1)
    eye = (iota((z.tokens, z.tokens), 0) == iota((z.tokens, z.tokens), 1)).astype(F32).astype(BF)
    local_col = column_of(dot_nt(eye, two_digits(jnp.where(owner == table_pos, local, z.rows))))
    pick = (iota((z.tokens, z.rows), 1) == local_col).astype(F32).astype(BF)
    own_ref[...] = dot(pick, rows_ref[...]).astype(BF)
    lanes = max(8, z.n)
    offset = iota((lanes, z.tokens), 0)
    source = table_pos - offset
    source = jnp.where(source < 0, source + z.n, source)
    flags = (owner == source) & (offset >= 1) & (offset < z.n)
    rank = dot(flags.astype(F32).astype(BF), tri).astype(jnp.int32) - 1
    slots = z.n * z.cap
    slot = jnp.sum(
        jnp.where(flags, (offset - 1) * z.cap + rank + 1, 0), axis=0, keepdims=True
    )
    slot = jnp.where(slot == 0, slots, slot - 1)
    slot_col = column_of(dot_nt(eye, two_digits(slot)))
    route_ref[...] = (
        (iota((z.tokens, (z.n - 1) * z.cap), 1) == slot_col).astype(F32).astype(BF)
    )


def place_kernel(z, own_ref, route_ref, *refs):
    got, keep_ref, give_ref = refs[: z.n - 1], refs[-2], refs[-1]
    total = own_ref[...].astype(F32)
    block = max(1, 256 // z.cap)
    for k in range(0, z.n - 1, block):
        group = range(k, min(k + block, z.n - 1))
        rows = [got[g][...] for g in group]
        rows = rows[0] if len(rows) == 1 else jnp.concatenate(rows, axis=0)
        total = total + dot(route_ref[:, k * z.cap : k * z.cap + rows.shape[0]], rows)
    total = total.astype(BF)
    cut = z.tokens // z.mp
    keep_ref[...] = total[:cut]
    give_ref[...] = total[cut:]


def bias_kernel(z, small_ref, plan_ref, lens_ref, time_ref, bias_ref, *, buckets, tbuckets):
    table_pos = lax.axis_index("table")
    bal_pos = lax.axis_index("bal")
    mp_pos = lax.axis_index("mp")
    size = z.length
    number = buckets_of(size, buckets)
    lane = iota((8, size), 1)
    dist = jnp.where(lane == 0, 0, size - lane)
    position = []
    for h in range(z.heads):
        row = jnp.zeros((8, size), F32)
        for b in sorted(set(number)):
            low, high = number.index(b), size - 1 - number[::-1].index(b)
            row = jnp.where((dist >= low) & (dist <= high), small_ref[h, b], row)
        full = jnp.broadcast_to(row[0:1], (size, size))
        position.append(pltpu.roll(full, 0, 1, stride=1, stride_axis=0))
    for h in range(z.heads):
        for u in range(z.mine):
            bias_ref[u, h] = position[h]
    block = 32
    for u in range(z.mine):
        user = member(z, plan_ref, table_pos, bal_pos * z.pair + mp_pos * z.mine + u)
        size_u = lens_ref[user]
        events = time_ref[pl.ds(user, 1), :]
        columns = jnp.broadcast_to(events, (size, size)).T

        for r in range(0, size, block):
            rows = slice(r, r + block)
            diff = jnp.abs(columns[rows] - events)
            column = iota((block, size), 1)
            valid = (column <= iota((block, size), 0) + r) & (column < size_u)
            for h in range(z.heads):
                term = jnp.zeros((block, size), F32)
                for b in range(tbuckets):
                    term = jnp.where(diff == b, small_ref[h, buckets + b], term)
                bias_ref[u, h, rows, :] = jnp.where(valid, bias_ref[u, h, rows, :] + term, FAR)


def silu(s):
    half = 0.5 * s
    return half + half * jnp.tanh(half)


def layer_kernel(
    z, load, n_weights, plan_ref, lens_ref, keep_ref, got_ref, gain_ref, out_gain_ref, bias_ref, *refs
):
    weights = refs[:n_weights]
    own_out, give_out = refs[n_weights : n_weights + 2]
    (e_ref, w_ref, o_ref, emb_ref, x_ref, xn_ref, act_ref, y_ref, z_ref, sems) = refs[n_weights + 2 :]
    table_pos = lax.axis_index("table")
    bal_pos = lax.axis_index("bal")
    mp_pos = lax.axis_index("mp")
    width = x_ref.shape[1]
    copies = load(weights, e_ref, w_ref, o_ref, sems)
    for group in copies:
        for c in group:
            c.start()
    for u in range(z.mine):
        near = pl.multiple_of(u * z.length + mp_pos * z.half, z.half)
        far = pl.multiple_of(u * z.length + (1 - mp_pos) * z.half, z.half)
        rows = slice(u * z.half, (u + 1) * z.half)
        emb_ref[pl.ds(near, z.half), :] = keep_ref[rows, :]
        emb_ref[pl.ds(far, z.half), :] = got_ref[rows, :]
    for c in copies[0]:
        c.wait()
    tokens = z.mine * z.length
    block = 256
    for r in range(0, tokens, block):
        rows = slice(r, r + block)
        x = dot(emb_ref[rows, :], e_ref[...]).astype(BF)
        x_ref[rows, :] = x
        x = x.astype(F32)
        mean = jnp.mean(x, axis=1, keepdims=True)
        centred = x - mean
        var = jnp.mean(centred * centred, axis=1, keepdims=True)
        xn_ref[rows, :] = (centred * lax.rsqrt(var + epsilon) * gain_ref[...]).astype(BF)
    for c in copies[1]:
        c.wait()
    step = 256

    def project(i, carry):
        c, nb = i // (width // step), i % (width // step)
        cols = pl.ds(pl.multiple_of(nb * step, step), step)
        s = dot(xn_ref[...], w_ref[c, :, cols])
        act_ref[c, :, cols] = silu(s).astype(BF)
        return carry

    lax.fori_loop(0, 4 * (width // step), project, 0, unroll=2)
    scale = 1.0 / math.sqrt(width // z.heads)
    size = width // z.heads
    for u in range(z.mine):
        user = member(z, plan_ref, table_pos, bal_pos * z.pair + mp_pos * z.mine + u)
        inverse = 1.0 / jnp.full((1, z.length), lens_ref[user], jnp.int32).astype(F32)
        rows = slice(u * z.length, (u + 1) * z.length)

        def attend(h, carry):
            total, square = carry
            cols = pl.ds(pl.multiple_of(h * size, size), size)
            s = dot_nt(act_ref[2, rows, cols], act_ref[3, rows, cols]) * scale + bias_ref[u, h]
            a = (silu(s) * inverse).astype(BF)
            y = dot(a, act_ref[1, rows, cols])
            y_ref[rows, cols] = y
            return (
                total + jnp.sum(y, axis=1, keepdims=True),
                square + jnp.sum(y * y, axis=1, keepdims=True),
            )

        zero = jnp.zeros((z.length, 1), F32)
        total, square = lax.fori_loop(0, z.heads, attend, (zero, zero), unroll=4)
        mean = total / width
        var = square / width - mean * mean
        factor = lax.rsqrt(var + epsilon)
        for h in range(z.heads):
            cols = slice(h * size, (h + 1) * size)
            normed = (y_ref[rows, cols] - mean) * factor * out_gain_ref[h : h + 1, :]
            z_ref[rows, cols] = (normed * act_ref[0, rows, cols].astype(F32)).astype(BF)
    for c in copies[2]:
        c.wait()
    out_cols = width // z.mp
    for which, ref in ((1 - mp_pos, give_out), (mp_pos, own_out)):
        for nb in range(out_cols // step):
            cols = pl.ds(pl.multiple_of(which * out_cols + nb * step, step), step)
            term = dot(z_ref[...], o_ref[:, cols])
            ref[:, nb * step : (nb + 1) * step] = (
                term + x_ref[:, cols].astype(F32)
            ).astype(BF)


def swap(x, axis, size, k=1):
    return lax.ppermute(x, axis, [(i, (i + k) % size) for i in range(size)])


Q_ROWS, CUT = 256, 192


def quarter_pack(z, embed_proj, qkvu_proj, out_proj):
    width = embed_proj.shape[0]
    q = lax.axis_index("parts") * z.bal + lax.axis_index("bal")
    m = lax.axis_index("mp")
    four, deep, cols = qkvu_proj.shape
    share = deep // 4
    qk = lax.dynamic_slice_in_dim(qkvu_proj, q * share, share, 1).reshape(four * share, cols)
    e_rows = width // 8
    e = lax.dynamic_slice_in_dim(embed_proj, (q * 2 + m) * e_rows, e_rows, 0)
    e = jnp.concatenate([e[: e_rows // 2], e[e_rows // 2 :]], axis=1)
    o_rows = out_proj.shape[0] // 4
    o = lax.dynamic_slice_in_dim(out_proj, q * o_rows, o_rows, 0)
    o = jnp.concatenate([o[: o_rows // 2], o[o_rows // 2 :]], axis=1)
    return jnp.concatenate([qk, e, o], axis=0)


def gather_weights(z, embed_proj, qkvu_proj, out_proj):
    pack = quarter_pack(z, embed_proj, qkvu_proj, out_proj)
    remote = [pack]
    for _ in range(z.n - 1):
        remote.append(swap(remote[-1], "table", z.n))
    pieces = [embed_proj, qkvu_proj, out_proj]
    pieces += [swap(qkvu_proj, "mp", 2), swap(out_proj, "mp", 2)]
    for r in remote[1:]:
        x = swap(r, "bal", 2)
        y = swap(r, "parts", 2)
        dx = swap(y[:CUT], "bal", 2)
        dy = swap(x[CUT:], "parts", 2)
        for piece in (r, x, y, dx, dy):
            pieces += [piece, swap(piece, "mp", 2)]
    return pieces


def load_pieces(z):
    def load(refs, e_ref, w_ref, o_ref, sems):
        t, m = lax.axis_index("table"), lax.axis_index("mp")
        parts_pos, bal_pos = lax.axis_index("parts"), lax.axis_index("bal")
        e_own, w_own, o_own, w_near, o_near = refs[:5]
        deep, cols = w_own.shape[1], w_own.shape[2]
        e_cols = e_own.shape[1]
        o_rows = o_own.shape[0]
        groups = [[], [], []]

        def add(g, src, dst):
            groups[g].append(pltpu.make_async_copy(src, dst, sems.at[g]))

        def at(x, size):
            return pl.ds(pl.multiple_of(x, size), size)

        add(0, e_own, e_ref.at[:, at(t * e_cols, e_cols)])
        for core, w, o in ((m, w_own, o_own), (1 - m, w_near, o_near)):
            add(1, w, w_ref.at[:, at(t * deep, deep), at(core * cols, cols)])
            add(2, o, o_ref.at[at(core * o_rows, o_rows), at(t * e_cols, e_cols)])
        share = deep // 4
        e_part = e_ref.shape[0] // 16
        o_part = o_rows // 8
        rest = refs[5:]
        for k in range(1, z.n):
            source = lax.rem(t + z.n - k, z.n)
            block = rest[(k - 1) * 10 : k * 10]
            for i, (dp, db) in enumerate(((0, 0), (0, 1), (1, 0), (1, 1), (1, 1))):
                pp = parts_pos if dp == 0 else 1 - parts_pos
                bb = bal_pos if db == 0 else 1 - bal_pos
                q = pp * 2 + bb
                low = CUT if i == 4 else 0
                high = CUT if i == 3 else 4 * share + e_part + o_part
                for core, ref in ((m, block[2 * i]), (1 - m, block[2 * i + 1])):
                    for c in range(4):
                        if low <= c * share < high:
                            add(
                                1,
                                ref.at[c * share - low : (c + 1) * share - low, :],
                                w_ref.at[c, at(source * deep + q * share, share), at(core * cols, cols)],
                            )
                    if high <= 4 * share:
                        continue
                    first = 4 * share - low
                    for j in range(2):
                        lanes = slice(j * e_cols, (j + 1) * e_cols)
                        add(
                            0,
                            ref.at[first : first + e_part, lanes],
                            e_ref.at[at(((q * 2 + core) * 2 + j) * e_part, e_part), at(source * e_cols, e_cols)],
                        )
                        add(
                            2,
                            ref.at[first + e_part : first + e_part + o_part, lanes],
                            o_ref.at[
                                at(core * o_rows + (q * 2 + j) * o_part, o_part), at(source * e_cols, e_cols)
                            ],
                        )
        return groups

    return load


def load_whole(refs, e_ref, w_ref, o_ref, sems):
    return [
        [pltpu.make_async_copy(src, dst, sems.at[i])]
        for i, (src, dst) in enumerate(zip(refs, (e_ref, w_ref, o_ref)))
    ]


def body(
    table_rows,
    row_scale,
    hist_ids,
    lengths,
    plan,
    time_bucket,
    embed_proj,
    in_gain,
    qkvu_proj,
    out_gain,
    out_proj,
    pos_bias,
    time_bias,
):
    axes = tuple(lax.axis_size(a) for a in ("table", "bal", "mp"))
    z = Sizes(axes, table_rows, hist_ids, lengths, pos_bias)
    width = in_gain.shape[0]
    mp_pos = lax.axis_index("mp")
    scale = row_scale.reshape(z.rows // 128, 128)
    sent = pl.pallas_call(
        functools.partial(send_kernel, z),
        out_shape=[jax.ShapeDtypeStruct((z.cap, z.width), BF)] * (z.n - 1),
        in_specs=[sspec(), vspec(), vspec(), vspec()],
        out_specs=[vspec()] * (z.n - 1),
        scratch_shapes=[pltpu.VMEM((z.rows, z.width), BF)],
        compiler_params=params(),
        name="send_rows",
    )(plan, hist_ids, table_rows, scale)
    got = [swap(s, "table", z.n, k + 1) for k, s in enumerate(sent)]
    own, route = pl.pallas_call(
        functools.partial(keep_kernel, z),
        out_shape=[
            jax.ShapeDtypeStruct((z.tokens, z.width), BF),
            jax.ShapeDtypeStruct((z.tokens, (z.n - 1) * z.cap), BF),
        ],
        in_specs=[sspec(), vspec(), vspec(), vspec()],
        out_specs=[vspec()] * 2,
        scratch_shapes=[pltpu.VMEM((z.rows, z.width), BF)],
        compiler_params=params(),
        name="keep_rows",
    )(plan, hist_ids, table_rows, scale)

    small = jnp.concatenate([pos_bias, time_bias, out_gain.reshape(pos_bias.shape[0], -1)], axis=1)
    other = swap(small, "mp", z.mp)
    small = jnp.where(
        mp_pos == 0, jnp.concatenate([small, other], 0), jnp.concatenate([other, small], 0)
    )
    buckets, tbuckets = pos_bias.shape[1], time_bias.shape[1]
    bias = pl.pallas_call(
        functools.partial(bias_kernel, z, buckets=buckets, tbuckets=tbuckets),
        out_shape=jax.ShapeDtypeStruct((z.mine, z.heads, z.length, z.length), F32),
        in_specs=[sspec(), sspec(), sspec(), vspec()],
        out_specs=vspec(),
        compiler_params=params(),
        name="bias",
    )(small[:, : buckets + tbuckets], plan, lengths, time_bucket)
    gains = small[:, buckets + tbuckets :]

    if z.n == 4 and z.bal == 2 and lax.axis_size("parts") == 2:
        weights = gather_weights(z, embed_proj, qkvu_proj, out_proj)
        load = load_pieces(z)
    else:
        q_full = lax.all_gather(qkvu_proj, "table", axis=1, tiled=True)
        o_full = lax.all_gather(out_proj, "table", axis=1, tiled=True)
        weights = [
            lax.all_gather(embed_proj, "table", axis=1, tiled=True),
            lax.all_gather(q_full, "mp", axis=2, tiled=True),
            lax.all_gather(o_full, "mp", axis=0, tiled=True),
        ]
        load = load_whole

    keep, give = pl.pallas_call(
        functools.partial(place_kernel, z),
        out_shape=[jax.ShapeDtypeStruct((z.tokens // z.mp, z.width), BF)] * 2,
        in_specs=[vspec()] * (z.n + 1),
        out_specs=[vspec()] * 2,
        compiler_params=params(),
        name="place_rows",
    )(own, route, *got)
    back = swap(give, "mp", z.mp)

    tokens = z.mine * z.length
    out_cols = width // z.mp
    out_own, out_give = pl.pallas_call(
        functools.partial(layer_kernel, z, load, len(weights)),
        out_shape=[jax.ShapeDtypeStruct((tokens, out_cols), BF)] * 2,
        in_specs=[sspec(), sspec()] + [vspec()] * 5 + [pl.BlockSpec(memory_space=pl.ANY)] * len(weights),
        out_specs=[vspec()] * 2,
        scratch_shapes=[
            pltpu.VMEM((z.width, width), BF),
            pltpu.VMEM((4, width, width), BF),
            pltpu.VMEM((width, width), BF),
            pltpu.VMEM((tokens, z.width), BF),
            pltpu.VMEM((tokens, width), BF),
            pltpu.VMEM((tokens, width), BF),
            pltpu.VMEM((4, tokens, width), BF),
            pltpu.VMEM((tokens, width), F32),
            pltpu.VMEM((tokens, width), BF),
            pltpu.SemaphoreType.DMA((3,)),
        ],
        compiler_params=params(),
        name="layer",
    )(plan, lengths, keep, back, in_gain.reshape(1, width), gains, bias, *weights)
    out_got = swap(out_give, "mp", z.mp)
    out = jnp.where(
        mp_pos == 0,
        jnp.concatenate([out_own, out_got], 0),
        jnp.concatenate([out_got, out_own], 0),
    )
    return out.reshape(z.pair, z.length, out_cols)


def solution(mesh):
    return jax.shard_map(
        body,
        mesh=mesh,
        in_specs=(
            P("table", None),
            P("table"),
            P("parts", None),
            P(("parts", "table")),
            P("parts"),
            P(("parts", "table"), None),
            P(None, "table"),
            P(),
            P(None, "table", "mp"),
            P("mp"),
            P("mp", "table"),
            P("mp", None),
            P("mp", None),
        ),
        out_specs=P(("parts", "table", "bal"), None, "mp"),
        check_vma=False,
    )
```

```python
import functools
import math

import jax
import jax.numpy as jnp
from jax import lax
from jax.experimental import pallas as pl
from jax.experimental.pallas import tpu as pltpu
from jax.sharding import PartitionSpec as P

epsilon = 1e-05
BF = jnp.bfloat16
F32 = jnp.float32
VMEM_BYTES = 56 * 1024 * 1024
FAR = -1e30


def buckets_of(length, buckets):
    found = []
    for d in range(length):
        b = d if d < 16 else 15 + sum(1 for power in range(4, 20) if d >= 2**power)
        found.append(min(b, buckets - 1))
    return found


def vspec():
    return pl.BlockSpec(memory_space=pltpu.VMEM)


def sspec():
    return pl.BlockSpec(memory_space=pltpu.SMEM)


def params():
    return pltpu.CompilerParams(vmem_limit_bytes=VMEM_BYTES)


def iota(shape, axis):
    return lax.broadcasted_iota(jnp.int32, shape, axis)


def dot(a, b):
    return jnp.dot(a, b, preferred_element_type=F32)


def dot_nt(a, b):
    return lax.dot_general(a, b, (((1,), (1,)), ((), ())), preferred_element_type=F32)


def cost(us):
    return pl.CostEstimate(flops=int(us * 9e8), bytes_accessed=int(us * 2e6), transcendentals=0)


def fence(*values):
    return lax.optimization_barrier(values)


class Sizes:
    def __init__(self, mesh_sizes, table_rows, hist_ids, lengths, pos_bias):
        self.n, self.bal, self.mp = mesh_sizes
        self.rows, self.width = table_rows.shape
        self.users, self.length = hist_ids.shape
        self.group = lengths.shape[0]
        self.pair = self.group // self.bal
        self.mine = self.pair // self.mp
        self.half = self.length // self.mp
        self.tokens = self.pair * self.half
        self.cap = self.pair * self.length // self.n
        self.heads = pos_bias.shape[0] * self.mp
        self.shift = self.rows.bit_length() - 1


def member(z, plan_ref, dest, slot):
    found = jnp.int32(0)
    for j in range(z.group):
        found = found + jnp.where(plan_ref[dest * z.group + j] == slot, j, 0)
    return found


def slot_of(z, mp_pos, s):
    if s < z.mine:
        return mp_pos * z.mine + s
    return (1 - mp_pos) * z.mine + (s - z.mine)


def token_ids(z, plan_ref, hist_ref, dest, bal_pos, mp_pos):
    parts = []
    for s in range(z.pair):
        slot = bal_pos * z.pair + slot_of(z, mp_pos, s)
        user = dest * z.group + member(z, plan_ref, dest, slot)
        row = hist_ref[pl.ds(user, 1), :]
        parts.append(jnp.where(mp_pos == 0, row[:, : z.half], row[:, z.half :]))
    return jnp.concatenate(parts, axis=1)


def scaled_rows(z, table_ref, scale_ref, rows_ref):
    chunk = 128

    def step(i, carry):
        start = pl.multiple_of(i * chunk, chunk)
        row = scale_ref[pl.ds(i, 1), :]
        column = jnp.broadcast_to(row, (chunk, chunk)).T
        for c in range(z.width // chunk):
            cols = slice(c * chunk, (c + 1) * chunk)
            rows_ref[pl.ds(start, chunk), cols] = (
                table_ref[pl.ds(start, chunk), cols].astype(F32) * column
            ).astype(BF)
        return carry

    lax.fori_loop(0, z.rows // chunk, step, 0)


def two_digits(values):
    row = iota((8, values.shape[1]), 0)
    high = lax.shift_right_logical(values, 7)
    low = values & 127
    return jnp.where(row == 0, high, jnp.where(row == 1, low, 0)).astype(F32).astype(BF)


def column_of(pairs):
    return (pairs[:, 0:1] * 128.0 + pairs[:, 1:2]).astype(jnp.int32)


def triangle(tokens):
    return (iota((tokens, tokens), 0) <= iota((tokens, tokens), 1)).astype(F32).astype(BF)


def send_kernel(z, plan_ref, hist_ref, table_ref, scale_ref, *refs):
    outs, rows_ref = refs[:-1], refs[-1]
    table_pos = lax.axis_index("table")
    bal_pos = lax.axis_index("bal")
    mp_pos = lax.axis_index("mp")
    scaled_rows(z, table_ref, scale_ref, rows_ref)
    tri = triangle(z.tokens)
    for k in range(1, z.n):
        dest = lax.rem(table_pos + k, z.n)
        ids = token_ids(z, plan_ref, hist_ref, dest, bal_pos, mp_pos)
        mine = lax.shift_right_logical(ids, z.shift) == table_pos
        flags = jnp.broadcast_to(mine.astype(F32), (8, z.tokens)).astype(BF)
        rank = dot(flags, tri)[0:1, :].astype(jnp.int32) - 1
        place = jnp.where(mine, rank, -1)
        compact = (iota((z.cap, z.tokens), 0) == place).astype(F32).astype(BF)
        local = column_of(dot_nt(compact, two_digits(ids & (z.rows - 1))))
        pick = (iota((z.cap, z.rows), 1) == local).astype(F32).astype(BF)
        outs[k - 1][...] = dot(pick, rows_ref[...]).astype(BF)


def keep_kernel(z, plan_ref, hist_ref, table_ref, scale_ref, own_ref, route_ref, rows_ref):
    table_pos = lax.axis_index("table")
    bal_pos = lax.axis_index("bal")
    mp_pos = lax.axis_index("mp")
    scaled_rows(z, table_ref, scale_ref, rows_ref)
    tri = triangle(z.tokens)
    ids = token_ids(z, plan_ref, hist_ref, table_pos, bal_pos, mp_pos)
    owner = lax.shift_right_logical(ids, z.shift)
    local = ids & (z.rows - 1)
    eye = (iota((z.tokens, z.tokens), 0) == iota((z.tokens, z.tokens), 1)).astype(F32).astype(BF)
    local_col = column_of(dot_nt(eye, two_digits(jnp.where(owner == table_pos, local, z.rows))))
    pick = (iota((z.tokens, z.rows), 1) == local_col).astype(F32).astype(BF)
    own_ref[...] = dot(pick, rows_ref[...]).astype(BF)
    lanes = max(8, z.n)
    offset = iota((lanes, z.tokens), 0)
    source = table_pos - offset
    source = jnp.where(source < 0, source + z.n, source)
    flags = (owner == source) & (offset >= 1) & (offset < z.n)
    rank = dot(flags.astype(F32).astype(BF), tri).astype(jnp.int32) - 1
    slots = z.n * z.cap
    slot = jnp.sum(
        jnp.where(flags, (offset - 1) * z.cap + rank + 1, 0), axis=0, keepdims=True
    )
    slot = jnp.where(slot == 0, slots, slot - 1)
    slot_col = column_of(dot_nt(eye, two_digits(slot)))
    route_ref[...] = (
        (iota((z.tokens, (z.n - 1) * z.cap), 1) == slot_col).astype(F32).astype(BF)
    )


def place_kernel(z, own_ref, route_ref, *refs):
    got, keep_ref, give_ref = refs[: z.n - 1], refs[-2], refs[-1]
    total = own_ref[...].astype(F32)
    block = max(1, 256 // z.cap)
    for k in range(0, z.n - 1, block):
        group = range(k, min(k + block, z.n - 1))
        rows = [got[g][...] for g in group]
        rows = rows[0] if len(rows) == 1 else jnp.concatenate(rows, axis=0)
        total = total + dot(route_ref[:, k * z.cap : k * z.cap + rows.shape[0]], rows)
    total = total.astype(BF)
    cut = z.tokens // z.mp
    keep_ref[...] = total[:cut]
    give_ref[...] = total[cut:]


def bias_kernel(z, small_ref, plan_ref, lens_ref, time_ref, bias_ref, *, buckets, tbuckets):
    table_pos = lax.axis_index("table")
    bal_pos = lax.axis_index("bal")
    mp_pos = lax.axis_index("mp")
    size = z.length
    number = buckets_of(size, buckets)
    lane = iota((8, size), 1)
    dist = jnp.where(lane == 0, 0, size - lane)
    position = []
    for h in range(z.heads):
        row = jnp.zeros((8, size), F32)
        for b in sorted(set(number)):
            low, high = number.index(b), size - 1 - number[::-1].index(b)
            row = jnp.where((dist >= low) & (dist <= high), small_ref[h, b], row)
        full = jnp.broadcast_to(row[0:1], (size, size))
        position.append(pltpu.roll(full, 0, 1, stride=1, stride_axis=0))
    for h in range(z.heads):
        for u in range(z.mine):
            bias_ref[u, h] = position[h]
    block = 32
    for u in range(z.mine):
        user = member(z, plan_ref, table_pos, bal_pos * z.pair + mp_pos * z.mine + u)
        size_u = lens_ref[user]
        events = time_ref[pl.ds(user, 1), :]
        columns = jnp.broadcast_to(events, (size, size)).T

        for r in range(0, size, block):
            rows = slice(r, r + block)
            diff = jnp.abs(columns[rows] - events)
            column = iota((block, size), 1)
            valid = (column <= iota((block, size), 0) + r) & (column < size_u)
            for h in range(z.heads):
                term = jnp.zeros((block, size), F32)
                for b in range(tbuckets):
                    term = jnp.where(diff == b, small_ref[h, buckets + b], term)
                bias_ref[u, h, rows, :] = jnp.where(valid, bias_ref[u, h, rows, :] + term, FAR)


def silu(s):
    half = 0.5 * s
    return half + half * jnp.tanh(half)


def layer_kernel(
    z, load, n_weights, plan_ref, lens_ref, keep_ref, got_ref, gain_ref, out_gain_ref, bias_ref, *refs
):
    weights = refs[:n_weights]
    own_out, give_out = refs[n_weights : n_weights + 2]
    (e_ref, w_ref, o_ref, emb_ref, x_ref, xn_ref, act_ref, y_ref, z_ref, sems) = refs[n_weights + 2 :]
    table_pos = lax.axis_index("table")
    bal_pos = lax.axis_index("bal")
    mp_pos = lax.axis_index("mp")
    width = x_ref.shape[1]
    copies = load(weights, e_ref, w_ref, o_ref, sems)
    for group in copies:
        for c in group:
            c.start()
    for u in range(z.mine):
        near = pl.multiple_of(u * z.length + mp_pos * z.half, z.half)
        far = pl.multiple_of(u * z.length + (1 - mp_pos) * z.half, z.half)
        rows = slice(u * z.half, (u + 1) * z.half)
        emb_ref[pl.ds(near, z.half), :] = keep_ref[rows, :]
        emb_ref[pl.ds(far, z.half), :] = got_ref[rows, :]
    for c in copies[0]:
        c.wait()
    tokens = z.mine * z.length
    block = 256
    for r in range(0, tokens, block):
        rows = slice(r, r + block)
        x = dot(emb_ref[rows, :], e_ref[...]).astype(BF)
        x_ref[rows, :] = x
        x = x.astype(F32)
        mean = jnp.mean(x, axis=1, keepdims=True)
        centred = x - mean
        var = jnp.mean(centred * centred, axis=1, keepdims=True)
        xn_ref[rows, :] = (centred * lax.rsqrt(var + epsilon) * gain_ref[...]).astype(BF)
    for c in copies[1]:
        c.wait()
    step = 256

    def project(i, carry):
        c, nb = i // (width // step), i % (width // step)
        cols = pl.ds(pl.multiple_of(nb * step, step), step)
        s = dot(xn_ref[...], w_ref[c, :, cols])
        act_ref[c, :, cols] = silu(s).astype(BF)
        return carry

    lax.fori_loop(0, 4 * (width // step), project, 0, unroll=2)
    scale = 1.0 / math.sqrt(width // z.heads)
    size = width // z.heads
    for u in range(z.mine):
        user = member(z, plan_ref, table_pos, bal_pos * z.pair + mp_pos * z.mine + u)
        inverse = 1.0 / jnp.full((1, z.length), lens_ref[user], jnp.int32).astype(F32)
        rows = slice(u * z.length, (u + 1) * z.length)

        def attend(h, carry):
            total, square = carry
            cols = pl.ds(pl.multiple_of(h * size, size), size)
            s = dot_nt(act_ref[2, rows, cols], act_ref[3, rows, cols]) * scale + bias_ref[u, h]
            a = (silu(s) * inverse).astype(BF)
            y = dot(a, act_ref[1, rows, cols])
            y_ref[rows, cols] = y
            return (
                total + jnp.sum(y, axis=1, keepdims=True),
                square + jnp.sum(y * y, axis=1, keepdims=True),
            )

        zero = jnp.zeros((z.length, 1), F32)
        total, square = lax.fori_loop(0, z.heads, attend, (zero, zero), unroll=4)
        mean = total / width
        var = square / width - mean * mean
        factor = lax.rsqrt(var + epsilon)
        for h in range(z.heads):
            cols = slice(h * size, (h + 1) * size)
            normed = (y_ref[rows, cols] - mean) * factor * out_gain_ref[h : h + 1, :]
            z_ref[rows, cols] = (normed * act_ref[0, rows, cols].astype(F32)).astype(BF)
    for c in copies[2]:
        c.wait()
    out_cols = width // z.mp
    for which, ref in ((1 - mp_pos, give_out), (mp_pos, own_out)):
        for nb in range(out_cols // step):
            cols = pl.ds(pl.multiple_of(which * out_cols + nb * step, step), step)
            term = dot(z_ref[...], o_ref[:, cols])
            ref[:, nb * step : (nb + 1) * step] = (
                term + x_ref[:, cols].astype(F32)
            ).astype(BF)


def swap(x, axis, size, k=1):
    return lax.ppermute(x, axis, [(i, (i + k) % size) for i in range(size)])


Q_ROWS, CUT = 256, 192


def quarter_pack(z, embed_proj, qkvu_proj, out_proj):
    width = embed_proj.shape[0]
    q = lax.axis_index("parts") * z.bal + lax.axis_index("bal")
    m = lax.axis_index("mp")
    four, deep, cols = qkvu_proj.shape
    share = deep // 4
    qk = lax.dynamic_slice_in_dim(qkvu_proj, q * share, share, 1).reshape(four * share, cols)
    e_rows = width // 8
    e = lax.dynamic_slice_in_dim(embed_proj, (q * 2 + m) * e_rows, e_rows, 0)
    e = jnp.concatenate([e[: e_rows // 2], e[e_rows // 2 :]], axis=1)
    o_rows = out_proj.shape[0] // 4
    o = lax.dynamic_slice_in_dim(out_proj, q * o_rows, o_rows, 0)
    o = jnp.concatenate([o[: o_rows // 2], o[o_rows // 2 :]], axis=1)
    return jnp.concatenate([qk, e, o], axis=0)


def load_pieces(z):
    def load(refs, e_ref, w_ref, o_ref, sems):
        t, m = lax.axis_index("table"), lax.axis_index("mp")
        parts_pos, bal_pos = lax.axis_index("parts"), lax.axis_index("bal")
        e_own, w_own, o_own, w_near, o_near = refs[:5]
        deep, cols = w_own.shape[1], w_own.shape[2]
        e_cols = e_own.shape[1]
        o_rows = o_own.shape[0]
        groups = [[], [], []]

        def add(g, src, dst):
            groups[g].append(pltpu.make_async_copy(src, dst, sems.at[g]))

        def at(x, size):
            return pl.ds(pl.multiple_of(x, size), size)

        add(0, e_own, e_ref.at[:, at(t * e_cols, e_cols)])
        for core, w, o in ((m, w_own, o_own), (1 - m, w_near, o_near)):
            add(1, w, w_ref.at[:, at(t * deep, deep), at(core * cols, cols)])
            add(2, o, o_ref.at[at(core * o_rows, o_rows), at(t * e_cols, e_cols)])
        share = deep // 4
        e_part = e_ref.shape[0] // 16
        o_part = o_rows // 8
        rest = refs[5:]
        for k in range(1, z.n):
            source = lax.rem(t + z.n - k, z.n)
            block = rest[(k - 1) * 10 : k * 10]
            for i, (dp, db) in enumerate(((0, 0), (0, 1), (1, 0), (1, 1), (1, 1))):
                pp = parts_pos if dp == 0 else 1 - parts_pos
                bb = bal_pos if db == 0 else 1 - bal_pos
                q = pp * 2 + bb
                low = CUT if i == 4 else 0
                high = CUT if i == 3 else 4 * share + e_part + o_part
                for core, ref in ((m, block[2 * i]), (1 - m, block[2 * i + 1])):
                    for c in range(4):
                        if low <= c * share < high:
                            add(
                                1,
                                ref.at[c * share - low : (c + 1) * share - low, :],
                                w_ref.at[c, at(source * deep + q * share, share), at(core * cols, cols)],
                            )
                    if high <= 4 * share:
                        continue
                    first = 4 * share - low
                    for j in range(2):
                        lanes = slice(j * e_cols, (j + 1) * e_cols)
                        add(
                            0,
                            ref.at[first : first + e_part, lanes],
                            e_ref.at[at(((q * 2 + core) * 2 + j) * e_part, e_part), at(source * e_cols, e_cols)],
                        )
                        add(
                            2,
                            ref.at[first + e_part : first + e_part + o_part, lanes],
                            o_ref.at[
                                at(core * o_rows + (q * 2 + j) * o_part, o_part), at(source * e_cols, e_cols)
                            ],
                        )
        return groups

    return load


def load_whole(refs, e_ref, w_ref, o_ref, sems):
    return [
        [pltpu.make_async_copy(src, dst, sems.at[i])]
        for i, (src, dst) in enumerate(zip(refs, (e_ref, w_ref, o_ref)))
    ]


def body(
    table_rows,
    row_scale,
    hist_ids,
    lengths,
    plan,
    time_bucket,
    embed_proj,
    in_gain,
    qkvu_proj,
    out_gain,
    out_proj,
    pos_bias,
    time_bias,
):
    axes = tuple(lax.axis_size(a) for a in ("table", "bal", "mp"))
    z = Sizes(axes, table_rows, hist_ids, lengths, pos_bias)
    width = in_gain.shape[0]
    mp_pos = lax.axis_index("mp")
    scale = row_scale.reshape(z.rows // 128, 128)
    send_rows = pl.pallas_call(
        functools.partial(send_kernel, z),
        out_shape=[jax.ShapeDtypeStruct((z.cap, z.width), BF)] * (z.n - 1),
        in_specs=[sspec(), vspec(), vspec(), vspec()],
        out_specs=[vspec()] * (z.n - 1),
        scratch_shapes=[pltpu.VMEM((z.rows, z.width), BF)],
        compiler_params=params(),
        cost_estimate=cost(7),
        name="send_rows",
    )
    keep_rows = pl.pallas_call(
        functools.partial(keep_kernel, z),
        out_shape=[
            jax.ShapeDtypeStruct((z.tokens, z.width), BF),
            jax.ShapeDtypeStruct((z.tokens, (z.n - 1) * z.cap), BF),
        ],
        in_specs=[sspec(), vspec(), vspec(), vspec()],
        out_specs=[vspec()] * 2,
        scratch_shapes=[pltpu.VMEM((z.rows, z.width), BF)],
        compiler_params=params(),
        cost_estimate=cost(7),
        name="keep_rows",
    )
    buckets, tbuckets = pos_bias.shape[1], time_bias.shape[1]
    make_bias = pl.pallas_call(
        functools.partial(bias_kernel, z, buckets=buckets, tbuckets=tbuckets),
        out_shape=jax.ShapeDtypeStruct((z.mine, z.heads, z.length, z.length), F32),
        in_specs=[sspec(), sspec(), sspec(), vspec()],
        out_specs=vspec(),
        compiler_params=params(),
        cost_estimate=cost(7),
        name="bias",
    )
    place_rows = pl.pallas_call(
        functools.partial(place_kernel, z),
        out_shape=[jax.ShapeDtypeStruct((z.tokens // z.mp, z.width), BF)] * 2,
        in_specs=[vspec()] * (z.n + 1),
        out_specs=[vspec()] * 2,
        compiler_params=params(),
        cost_estimate=cost(3),
        name="place_rows",
    )

    def both(x):
        other = swap(x, "mp", z.mp)
        return jnp.where(
            mp_pos == 0, jnp.concatenate([x, other], 0), jnp.concatenate([other, x], 0)
        )

    def biases():
        small = jnp.concatenate(
            [pos_bias, time_bias, out_gain.reshape(pos_bias.shape[0], -1)], axis=1
        )
        small = both(small)
        return small[:, : buckets + tbuckets], small[:, buckets + tbuckets :]

    if z.n == 4 and z.bal == 2 and lax.axis_size("parts") == 2:
        pack = quarter_pack(z, embed_proj, qkvu_proj, out_proj)
        near = functools.partial(swap, axis="mp", size=2)
        hop = functools.partial(swap, axis="table", size=z.n)

        def first(r):
            return swap(r, "bal", 2), swap(r, "parts", 2)

        def second(x, y):
            return swap(y[:CUT], "bal", 2), swap(x[CUT:], "parts", 2)

        table, gains = biases()
        r1 = hop(pack)
        sent = send_rows(plan, hist_ids, table_rows, scale)
        w_near, o_near = near(qkvu_proj), near(out_proj)
        r1, sent, w_near, o_near, table, gains, plan1 = fence(
            r1, sent, w_near, o_near, table, gains, plan
        )
        r2 = hop(r1)
        x1, y1 = first(r1)
        r1n = near(r1)
        bias = make_bias(table, plan1, lengths, time_bucket)
        r1, r2, x1, y1, r1n, bias, sent, plan2 = fence(r1, r2, x1, y1, r1n, bias, sent, plan1)
        r3 = hop(r2)
        got2 = swap(sent[1], "table", z.n, 2)
        x2, y2 = first(r2)
        dx1, dy1 = second(x1, y1)
        r2n, x1n, y1n = near(r2), near(x1), near(y1)
        own, route = keep_rows(plan2, hist_ids, table_rows, scale)
        r2, r3, got2, x2, y2, dx1, dy1, r2n, x1n, y1n, own, route, sent = fence(
            r2, r3, got2, x2, y2, dx1, dy1, r2n, x1n, y1n, own, route, sent
        )
        got1 = swap(sent[0], "table", z.n, 1)
        got3 = swap(sent[2], "table", z.n, 3)
        x3, y3 = first(r3)
        dx2, dy2 = second(x2, y2)
        r3n, x2n, y2n, dx1n, dy1n = [near(v) for v in (r3, x2, y2, dx1, dy1)]
        r3, got1, got3, x3, y3, dx2, dy2, r3n, x2n, y2n, dx1n, dy1n = fence(
            r3, got1, got3, x3, y3, dx2, dy2, r3n, x2n, y2n, dx1n, dy1n
        )
        dx3, dy3 = second(x3, y3)
        keep, give = place_rows(own, route, got1, got2, got3)
        back = near(give)
        x3n, y3n, dx2n, dy2n = [near(v) for v in (x3, y3, dx2, dy2)]
        weights = [embed_proj, qkvu_proj, out_proj, w_near, o_near]
        weights += [r1, r1n, x1, x1n, y1, y1n, dx1, dx1n, dy1, dy1n]
        weights += [r2, r2n, x2, x2n, y2, y2n, dx2, dx2n, dy2, dy2n]
        weights += [r3, r3n, x3, x3n, y3, y3n, dx3, near(dx3), dy3, near(dy3)]
        load = load_pieces(z)
    else:
        table, gains = biases()
        bias = make_bias(table, plan, lengths, time_bucket)
        sent = send_rows(plan, hist_ids, table_rows, scale)
        got = [swap(s, "table", z.n, k + 1) for k, s in enumerate(sent)]
        own, route = keep_rows(plan, hist_ids, table_rows, scale)
        q_full = lax.all_gather(qkvu_proj, "table", axis=1, tiled=True)
        o_full = lax.all_gather(out_proj, "table", axis=1, tiled=True)
        weights = [
            lax.all_gather(embed_proj, "table", axis=1, tiled=True),
            lax.all_gather(q_full, "mp", axis=2, tiled=True),
            lax.all_gather(o_full, "mp", axis=0, tiled=True),
        ]
        load = load_whole
        keep, give = place_rows(own, route, *got)
        back = swap(give, "mp", z.mp)

    tokens = z.mine * z.length
    out_cols = width // z.mp
    out_own, out_give = pl.pallas_call(
        functools.partial(layer_kernel, z, load, len(weights)),
        out_shape=[jax.ShapeDtypeStruct((tokens, out_cols), BF)] * 2,
        in_specs=[sspec(), sspec()] + [vspec()] * 5 + [pl.BlockSpec(memory_space=pl.ANY)] * len(weights),
        out_specs=[vspec()] * 2,
        scratch_shapes=[
            pltpu.VMEM((z.width, width), BF),
            pltpu.VMEM((4, width, width), BF),
            pltpu.VMEM((width, width), BF),
            pltpu.VMEM((tokens, z.width), BF),
            pltpu.VMEM((tokens, width), BF),
            pltpu.VMEM((tokens, width), BF),
            pltpu.VMEM((4, tokens, width), BF),
            pltpu.VMEM((tokens, width), F32),
            pltpu.VMEM((tokens, width), BF),
            pltpu.SemaphoreType.DMA((3,)),
        ],
        compiler_params=params(),
        name="layer",
    )(plan, lengths, keep, back, in_gain.reshape(1, width), gains, bias, *weights)
    out_got = swap(out_give, "mp", z.mp)
    out = jnp.where(
        mp_pos == 0,
        jnp.concatenate([out_own, out_got], 0),
        jnp.concatenate([out_got, out_own], 0),
    )
    return out.reshape(z.pair, z.length, out_cols)


def solution(mesh):
    return jax.shard_map(
        body,
        mesh=mesh,
        in_specs=(
            P("table", None),
            P("table"),
            P("parts", None),
            P(("parts", "table")),
            P("parts"),
            P(("parts", "table"), None),
            P(None, "table"),
            P(),
            P(None, "table", "mp"),
            P("mp"),
            P("mp", "table"),
            P("mp", None),
            P("mp", None),
        ),
        out_specs=P(("parts", "table", "bal"), None, "mp"),
        check_vma=False,
    )
```

```python
import functools
import math

import jax
import jax.numpy as jnp
from jax import lax
from jax.experimental import pallas as pl
from jax.experimental.pallas import tpu as pltpu
from jax.sharding import PartitionSpec as P

epsilon = 1e-05
BF = jnp.bfloat16
F32 = jnp.float32
VMEM_BYTES = 56 * 1024 * 1024
FAR = -1e30


def buckets_of(length, buckets):
    found = []
    for d in range(length):
        b = d if d < 16 else 15 + sum(1 for power in range(4, 20) if d >= 2**power)
        found.append(min(b, buckets - 1))
    return found


def vspec():
    return pl.BlockSpec(memory_space=pltpu.VMEM)


def sspec():
    return pl.BlockSpec(memory_space=pltpu.SMEM)


def params():
    return pltpu.CompilerParams(vmem_limit_bytes=VMEM_BYTES)


def iota(shape, axis):
    return lax.broadcasted_iota(jnp.int32, shape, axis)


def dot(a, b):
    return jnp.dot(a, b, preferred_element_type=F32)


def dot_nt(a, b):
    return lax.dot_general(a, b, (((1,), (1,)), ((), ())), preferred_element_type=F32)


def cost(us):
    return pl.CostEstimate(flops=int(us * 9e8), bytes_accessed=int(us * 2e6), transcendentals=0)


def fence(*values):
    return lax.optimization_barrier(values)


class Sizes:
    def __init__(self, mesh_sizes, table_rows, hist_ids, lengths, pos_bias):
        self.n, self.bal, self.mp = mesh_sizes
        self.rows, self.width = table_rows.shape
        self.users, self.length = hist_ids.shape
        self.group = lengths.shape[0]
        self.pair = self.group // self.bal
        self.mine = self.pair // self.mp
        self.half = self.length // self.mp
        self.tokens = self.pair * self.half
        self.cap = self.pair * self.length // self.n
        self.heads = pos_bias.shape[0] * self.mp
        self.shift = self.rows.bit_length() - 1


def member(z, plan_ref, dest, slot):
    found = jnp.int32(0)
    for j in range(z.group):
        found = found + jnp.where(plan_ref[dest * z.group + j] == slot, j, 0)
    return found


def slot_of(z, mp_pos, s):
    if s < z.mine:
        return mp_pos * z.mine + s
    return (1 - mp_pos) * z.mine + (s - z.mine)


def token_ids(z, plan_ref, hist_ref, dest, bal_pos, mp_pos):
    parts = []
    for s in range(z.pair):
        slot = bal_pos * z.pair + slot_of(z, mp_pos, s)
        user = dest * z.group + member(z, plan_ref, dest, slot)
        row = hist_ref[pl.ds(user, 1), :]
        parts.append(jnp.where(mp_pos == 0, row[:, : z.half], row[:, z.half :]))
    return jnp.concatenate(parts, axis=1)


def scaled_rows(z, table_ref, scale_ref, rows_ref):
    chunk = 128

    def step(i, carry):
        start = pl.multiple_of(i * chunk, chunk)
        row = scale_ref[pl.ds(i, 1), :]
        column = jnp.broadcast_to(row, (chunk, chunk)).T
        for c in range(z.width // chunk):
            cols = slice(c * chunk, (c + 1) * chunk)
            rows_ref[pl.ds(start, chunk), cols] = (
                table_ref[pl.ds(start, chunk), cols].astype(F32) * column
            ).astype(BF)
        return carry

    lax.fori_loop(0, z.rows // chunk, step, 0)


def two_digits(values):
    row = iota((8, values.shape[1]), 0)
    high = lax.shift_right_logical(values, 7)
    low = values & 127
    return jnp.where(row == 0, high, jnp.where(row == 1, low, 0)).astype(F32).astype(BF)


def column_of(pairs):
    return (pairs[:, 0:1] * 128.0 + pairs[:, 1:2]).astype(jnp.int32)


def triangle(tokens):
    return (iota((tokens, tokens), 0) <= iota((tokens, tokens), 1)).astype(F32).astype(BF)


def send_kernel(z, plan_ref, hist_ref, table_ref, scale_ref, *refs):
    outs, rows_ref = refs[:-1], refs[-1]
    table_pos = lax.axis_index("table")
    bal_pos = lax.axis_index("bal")
    mp_pos = lax.axis_index("mp")
    scaled_rows(z, table_ref, scale_ref, rows_ref)
    tri = triangle(z.tokens)
    for k in range(1, z.n):
        dest = lax.rem(table_pos + k, z.n)
        ids = token_ids(z, plan_ref, hist_ref, dest, bal_pos, mp_pos)
        mine = lax.shift_right_logical(ids, z.shift) == table_pos
        flags = jnp.broadcast_to(mine.astype(F32), (8, z.tokens)).astype(BF)
        rank = dot(flags, tri)[0:1, :].astype(jnp.int32) - 1
        place = jnp.where(mine, rank, -1)
        compact = (iota((z.cap, z.tokens), 0) == place).astype(F32).astype(BF)
        local = column_of(dot_nt(compact, two_digits(ids & (z.rows - 1))))
        pick = (iota((z.cap, z.rows), 1) == local).astype(F32).astype(BF)
        outs[k - 1][...] = dot(pick, rows_ref[...]).astype(BF)


def keep_kernel(z, plan_ref, hist_ref, table_ref, scale_ref, own_ref, route_ref, rows_ref):
    table_pos = lax.axis_index("table")
    bal_pos = lax.axis_index("bal")
    mp_pos = lax.axis_index("mp")
    scaled_rows(z, table_ref, scale_ref, rows_ref)
    tri = triangle(z.tokens)
    ids = token_ids(z, plan_ref, hist_ref, table_pos, bal_pos, mp_pos)
    owner = lax.shift_right_logical(ids, z.shift)
    local = ids & (z.rows - 1)
    eye = (iota((z.tokens, z.tokens), 0) == iota((z.tokens, z.tokens), 1)).astype(F32).astype(BF)
    local_col = column_of(dot_nt(eye, two_digits(jnp.where(owner == table_pos, local, z.rows))))
    pick = (iota((z.tokens, z.rows), 1) == local_col).astype(F32).astype(BF)
    own_ref[...] = dot(pick, rows_ref[...]).astype(BF)
    lanes = max(8, z.n)
    offset = iota((lanes, z.tokens), 0)
    source = table_pos - offset
    source = jnp.where(source < 0, source + z.n, source)
    flags = (owner == source) & (offset >= 1) & (offset < z.n)
    rank = dot(flags.astype(F32).astype(BF), tri).astype(jnp.int32) - 1
    slots = z.n * z.cap
    slot = jnp.sum(
        jnp.where(flags, (offset - 1) * z.cap + rank + 1, 0), axis=0, keepdims=True
    )
    slot = jnp.where(slot == 0, slots, slot - 1)
    slot_col = column_of(dot_nt(eye, two_digits(slot)))
    route_ref[...] = (
        (iota((z.tokens, (z.n - 1) * z.cap), 1) == slot_col).astype(F32).astype(BF)
    )


def place_kernel(z, own_ref, route_ref, *refs):
    got, keep_ref, give_ref = refs[: z.n - 1], refs[-2], refs[-1]
    total = own_ref[...].astype(F32)
    block = max(1, 256 // z.cap)
    for k in range(0, z.n - 1, block):
        group = range(k, min(k + block, z.n - 1))
        rows = [got[g][...] for g in group]
        rows = rows[0] if len(rows) == 1 else jnp.concatenate(rows, axis=0)
        total = total + dot(route_ref[:, k * z.cap : k * z.cap + rows.shape[0]], rows)
    total = total.astype(BF)
    cut = z.tokens // z.mp
    keep_ref[...] = total[:cut]
    give_ref[...] = total[cut:]


def bias_kernel(z, small_ref, plan_ref, lens_ref, time_ref, bias_ref, *, buckets, tbuckets):
    table_pos = lax.axis_index("table")
    bal_pos = lax.axis_index("bal")
    mp_pos = lax.axis_index("mp")
    size = z.length
    number = buckets_of(size, buckets)
    lane = iota((8, size), 1)
    dist = jnp.where(lane == 0, 0, size - lane)
    position = []
    for h in range(z.heads):
        row = jnp.zeros((8, size), F32)
        for b in sorted(set(number)):
            low, high = number.index(b), size - 1 - number[::-1].index(b)
            row = jnp.where((dist >= low) & (dist <= high), small_ref[h, b], row)
        full = jnp.broadcast_to(row[0:1], (size, size))
        position.append(pltpu.roll(full, 0, 1, stride=1, stride_axis=0))
    for h in range(z.heads):
        for u in range(z.mine):
            bias_ref[u, h] = position[h]
    block = 32
    for u in range(z.mine):
        user = member(z, plan_ref, table_pos, bal_pos * z.pair + mp_pos * z.mine + u)
        size_u = lens_ref[user]
        events = time_ref[pl.ds(user, 1), :]
        columns = jnp.broadcast_to(events, (size, size)).T

        for r in range(0, size, block):
            rows = slice(r, r + block)
            diff = jnp.abs(columns[rows] - events)
            column = iota((block, size), 1)
            valid = (column <= iota((block, size), 0) + r) & (column < size_u)
            for h in range(z.heads):
                term = jnp.zeros((block, size), F32)
                for b in range(tbuckets):
                    term = jnp.where(diff == b, small_ref[h, buckets + b], term)
                bias_ref[u, h, rows, :] = jnp.where(valid, bias_ref[u, h, rows, :] + term, FAR)


def silu(s):
    half = 0.5 * s
    return half + half * jnp.tanh(half)


def layer_kernel(
    z, load, n_weights, plan_ref, lens_ref, keep_ref, got_ref, gain_ref, out_gain_ref, bias_ref, *refs
):
    weights = refs[:n_weights]
    own_out, give_out = refs[n_weights : n_weights + 2]
    (e_ref, w_ref, o_ref, emb_ref, x_ref, xn_ref, act_ref, y_ref, z_ref, sems) = refs[n_weights + 2 :]
    table_pos = lax.axis_index("table")
    bal_pos = lax.axis_index("bal")
    mp_pos = lax.axis_index("mp")
    width = x_ref.shape[1]
    copies = load(weights, e_ref, w_ref, o_ref, sems)
    for group in copies:
        for c in group:
            c.start()
    for u in range(z.mine):
        near = pl.multiple_of(u * z.length + mp_pos * z.half, z.half)
        far = pl.multiple_of(u * z.length + (1 - mp_pos) * z.half, z.half)
        rows = slice(u * z.half, (u + 1) * z.half)
        emb_ref[pl.ds(near, z.half), :] = keep_ref[rows, :]
        emb_ref[pl.ds(far, z.half), :] = got_ref[rows, :]
    for c in copies[0]:
        c.wait()
    tokens = z.mine * z.length
    block = 256
    for r in range(0, tokens, block):
        rows = slice(r, r + block)
        x = dot(emb_ref[rows, :], e_ref[...]).astype(BF)
        x_ref[rows, :] = x
        x = x.astype(F32)
        mean = jnp.mean(x, axis=1, keepdims=True)
        centred = x - mean
        var = jnp.mean(centred * centred, axis=1, keepdims=True)
        xn_ref[rows, :] = (centred * lax.rsqrt(var + epsilon) * gain_ref[...]).astype(BF)
    for c in copies[1]:
        c.wait()
    step = 256

    def project(i, carry):
        c, nb = i // (width // step), i % (width // step)
        cols = pl.ds(pl.multiple_of(nb * step, step), step)
        s = dot(xn_ref[...], w_ref[c, :, cols])
        act_ref[c, :, cols] = silu(s).astype(BF)
        return carry

    lax.fori_loop(0, 4 * (width // step), project, 0, unroll=2)
    scale = 1.0 / math.sqrt(width // z.heads)
    size = width // z.heads
    for u in range(z.mine):
        user = member(z, plan_ref, table_pos, bal_pos * z.pair + mp_pos * z.mine + u)
        inverse = 1.0 / jnp.full((1, z.length), lens_ref[user], jnp.int32).astype(F32)
        rows = slice(u * z.length, (u + 1) * z.length)

        def attend(h, carry):
            total, square = carry
            cols = pl.ds(pl.multiple_of(h * size, size), size)
            s = dot_nt(act_ref[2, rows, cols], act_ref[3, rows, cols]) * scale + bias_ref[u, h]
            a = (silu(s) * inverse).astype(BF)
            y = dot(a, act_ref[1, rows, cols])
            y_ref[rows, cols] = y
            return (
                total + jnp.sum(y, axis=1, keepdims=True),
                square + jnp.sum(y * y, axis=1, keepdims=True),
            )

        zero = jnp.zeros((z.length, 1), F32)
        total, square = lax.fori_loop(0, z.heads, attend, (zero, zero), unroll=4)
        mean = total / width
        var = square / width - mean * mean
        factor = lax.rsqrt(var + epsilon)
        for h in range(z.heads):
            cols = slice(h * size, (h + 1) * size)
            normed = (y_ref[rows, cols] - mean) * factor * out_gain_ref[h : h + 1, :]
            z_ref[rows, cols] = (normed * act_ref[0, rows, cols].astype(F32)).astype(BF)
    for c in copies[2]:
        c.wait()
    out_cols = width // z.mp
    for which, ref in ((1 - mp_pos, give_out), (mp_pos, own_out)):
        for nb in range(out_cols // step):
            cols = pl.ds(pl.multiple_of(which * out_cols + nb * step, step), step)
            term = dot(z_ref[...], o_ref[:, cols])
            ref[:, nb * step : (nb + 1) * step] = (
                term + x_ref[:, cols].astype(F32)
            ).astype(BF)


def swap(x, axis, size, k=1):
    return lax.ppermute(x, axis, [(i, (i + k) % size) for i in range(size)])


def cross(x, near_first):
    pairs = []
    for i in range(8):
        p, b, m = i // 4, i // 2 % 2, i % 2
        p, b = (p, 1 - b) if (m == 0) == near_first else (1 - p, b)
        pairs.append((i, (p * 2 + b) * 2 + m))
    return lax.ppermute(x, ("parts", "bal", "mp"), pairs)


def pack_kernel(e_ref, w_ref, o_ref, out_ref, sems):
    q = lax.axis_index("parts") * 2 + lax.axis_index("bal")
    m = lax.axis_index("mp")
    share = w_ref.shape[1] // 4
    cols = e_ref.shape[1]
    e_part = e_ref.shape[0] // 16
    o_part = o_ref.shape[0] // 8
    copies = []

    def add(src, dst):
        copies.append(pltpu.make_async_copy(src, dst, sems))

    def at(x, size):
        return pl.ds(pl.multiple_of(x * size, size), size)

    for c in range(4):
        add(w_ref.at[c, at(q, share), :], out_ref.at[c * share : (c + 1) * share, :])
    first = 4 * share
    for j in range(2):
        lanes = slice(j * cols, (j + 1) * cols)
        add(e_ref.at[at((q * 2 + m) * 2 + j, e_part), :], out_ref.at[first : first + e_part, lanes])
        add(
            o_ref.at[at(q * 2 + j, o_part), :],
            out_ref.at[first + e_part : first + e_part + o_part, lanes],
        )
    for c in copies:
        c.start()
    for c in copies:
        c.wait()


def merge_kernel(*refs):
    out_ref, sem = refs[4:]
    copies = [pltpu.make_async_copy(refs[i], out_ref.at[i], sem) for i in range(4)]
    for c in copies:
        c.start()
    for c in copies:
        c.wait()


def load_pieces(z):
    def load(refs, e_ref, w_ref, o_ref, sems):
        t, m = lax.axis_index("table"), lax.axis_index("mp")
        p, b = lax.axis_index("parts"), lax.axis_index("bal")
        e_own, w_own, o_own, w_near, o_near = refs[:5]
        deep, cols = w_own.shape[1], w_own.shape[2]
        e_cols = e_own.shape[1]
        o_rows = o_own.shape[0]
        groups = [[], [], []]

        def add(g, src, dst):
            groups[g].append(pltpu.make_async_copy(src, dst, sems.at[g]))

        def at(x, size):
            return pl.ds(pl.multiple_of(x * size, size), size)

        add(0, e_own, e_ref.at[:, at(t, e_cols)])
        for core, w, o in ((m, w_own, o_own), (1 - m, w_near, o_near)):
            add(1, w, w_ref.at[:, at(t, deep), at(core, cols)])
            add(2, o, o_ref.at[at(core, o_rows), at(t, e_cols)])
        share = deep // 4
        e_part = e_ref.shape[0] // 16
        o_part = o_rows // 8
        first = 4 * share
        along_b, along_p = p * 2 + 1 - b, (1 - p) * 2 + b
        for k in range(1, z.n):
            source = lax.rem(t + z.n - k, z.n)
            block = refs[9:]
            if k < 3:
                both = refs[5 + (k - 1) * 2 : 5 + k * 2]
                block = [ref.at[i] for i in range(4) for ref in both]
            for i in range(4):
                for core, ref in ((m, block[2 * i]), (1 - m, block[2 * i + 1])):
                    q = (
                        p * 2 + b,
                        jnp.where(core == 0, along_b, along_p),
                        jnp.where(core == 0, along_p, along_b),
                        (1 - p) * 2 + 1 - b,
                    )[i]
                    for c in range(4):
                        add(
                            1,
                            ref.at[c * share : (c + 1) * share, :],
                            w_ref.at[c, at(source * 4 + q, share), at(core, cols)],
                        )
                    for j in range(2):
                        lanes = slice(j * e_cols, (j + 1) * e_cols)
                        add(
                            0,
                            ref.at[first : first + e_part, lanes],
                            e_ref.at[at((q * 2 + core) * 2 + j, e_part), at(source, e_cols)],
                        )
                        add(
                            2,
                            ref.at[first + e_part : first + e_part + o_part, lanes],
                            o_ref.at[at(core * 8 + q * 2 + j, o_part), at(source, e_cols)],
                        )
        return groups

    return load


def load_whole(refs, e_ref, w_ref, o_ref, sems):
    return [
        [pltpu.make_async_copy(src, dst, sems.at[i])]
        for i, (src, dst) in enumerate(zip(refs, (e_ref, w_ref, o_ref)))
    ]


def body(
    table_rows,
    row_scale,
    hist_ids,
    lengths,
    plan,
    time_bucket,
    embed_proj,
    in_gain,
    qkvu_proj,
    out_gain,
    out_proj,
    pos_bias,
    time_bias,
):
    axes = tuple(lax.axis_size(a) for a in ("table", "bal", "mp"))
    z = Sizes(axes, table_rows, hist_ids, lengths, pos_bias)
    width = in_gain.shape[0]
    mp_pos = lax.axis_index("mp")
    scale = row_scale.reshape(z.rows // 128, 128)
    send_rows = pl.pallas_call(
        functools.partial(send_kernel, z),
        out_shape=[jax.ShapeDtypeStruct((z.cap, z.width), BF)] * (z.n - 1),
        in_specs=[sspec(), vspec(), vspec(), vspec()],
        out_specs=[vspec()] * (z.n - 1),
        scratch_shapes=[pltpu.VMEM((z.rows, z.width), BF)],
        compiler_params=params(),
        cost_estimate=cost(7),
        name="send_rows",
    )
    keep_rows = pl.pallas_call(
        functools.partial(keep_kernel, z),
        out_shape=[
            jax.ShapeDtypeStruct((z.tokens, z.width), BF),
            jax.ShapeDtypeStruct((z.tokens, (z.n - 1) * z.cap), BF),
        ],
        in_specs=[sspec(), vspec(), vspec(), vspec()],
        out_specs=[vspec()] * 2,
        scratch_shapes=[pltpu.VMEM((z.rows, z.width), BF)],
        compiler_params=params(),
        cost_estimate=cost(7),
        name="keep_rows",
    )
    buckets, tbuckets = pos_bias.shape[1], time_bias.shape[1]
    make_bias = pl.pallas_call(
        functools.partial(bias_kernel, z, buckets=buckets, tbuckets=tbuckets),
        out_shape=jax.ShapeDtypeStruct((z.mine, z.heads, z.length, z.length), F32),
        in_specs=[sspec(), sspec(), sspec(), vspec()],
        out_specs=vspec(),
        compiler_params=params(),
        cost_estimate=cost(7),
        name="bias",
    )
    place_rows = pl.pallas_call(
        functools.partial(place_kernel, z),
        out_shape=[jax.ShapeDtypeStruct((z.tokens // z.mp, z.width), BF)] * 2,
        in_specs=[vspec()] * (z.n + 1),
        out_specs=[vspec()] * 2,
        compiler_params=params(),
        cost_estimate=cost(3),
        name="place_rows",
    )

    def both(x):
        other = swap(x, "mp", z.mp)
        return jnp.where(
            mp_pos == 0, jnp.concatenate([x, other], 0), jnp.concatenate([other, x], 0)
        )

    def biases(pos_bias, time_bias, out_gain):
        small = jnp.concatenate(
            [pos_bias, time_bias, out_gain.reshape(pos_bias.shape[0], -1)], axis=1
        )
        small = both(small)
        return small[:, : buckets + tbuckets], small[:, buckets + tbuckets :]

    if z.n == 4 and z.bal == 2 and lax.axis_size("parts") == 2:
        near = functools.partial(swap, axis="mp", size=2)
        hop = functools.partial(swap, axis="table", size=z.n)
        rows = qkvu_proj.shape[1] + z.width // 16 + out_proj.shape[0] // 8
        pack = pl.pallas_call(
            pack_kernel,
            out_shape=jax.ShapeDtypeStruct((rows, qkvu_proj.shape[2]), BF),
            in_specs=[pl.BlockSpec(memory_space=pl.ANY)] * 3,
            out_specs=vspec(),
            scratch_shapes=[pltpu.SemaphoreType.DMA],
            compiler_params=params(),
            name="pack",
        )(embed_proj, qkvu_proj, out_proj)
        merge = pl.pallas_call(
            merge_kernel,
            out_shape=jax.ShapeDtypeStruct((4, rows, qkvu_proj.shape[2]), BF),
            in_specs=[pl.BlockSpec(memory_space=pl.ANY)] * 4,
            out_specs=vspec(),
            scratch_shapes=[pltpu.SemaphoreType.DMA],
            compiler_params=params(),
            cost_estimate=cost(2),
            name="merge",
        )
        r1 = hop(pack)
        sent = send_rows(plan, hist_ids, table_rows, scale)
        w_near, o_near = near(qkvu_proj), near(out_proj)
        sent, small_in = fence(sent, (pos_bias, time_bias, out_gain))
        table, gains = biases(*small_in)
        r1, sent, table, w_near, o_near = fence(r1, sent, table, w_near, o_near)
        r2 = hop(r1)
        got1 = swap(sent[0], "table", z.n, 1)
        a1, b1 = cross(r1, True), cross(r1, False)
        bias = make_bias(table, plan, lengths, time_bucket)
        r1, r2, got1, a1, b1, bias, sent, plan1 = fence(r1, r2, got1, a1, b1, bias, sent, plan)
        r3 = hop(r2)
        got3 = swap(sent[2], "table", z.n, 3)
        a2, b2, d1 = cross(r2, True), cross(r2, False), cross(b1, True)
        own, route = keep_rows(plan1, hist_ids, table_rows, scale)
        r1, a1, b1, d1, r2, r3, a2, b2, got3, own, route, sent = fence(
            r1, a1, b1, d1, r2, r3, a2, b2, got3, own, route, sent
        )
        got2 = swap(sent[1], "table", z.n, 2)
        a3, b3, d2 = cross(r3, True), cross(r3, False), cross(b2, True)
        chunk1 = merge(r1, a1, b1, d1)
        near1 = near(chunk1)
        a3, b3, d2, chunk1, near1, got2, r2, a2, b2, r3 = fence(
            a3, b3, d2, chunk1, near1, got2, r2, a2, b2, r3
        )
        d3 = cross(b3, True)
        keep, give = place_rows(own, route, got1, got2, got3)
        back = near(give)
        chunk2 = merge(r2, a2, b2, d2)
        near2 = near(chunk2)
        weights = [embed_proj, qkvu_proj, out_proj, w_near, o_near, chunk1, near1, chunk2, near2]
        for v in (r3, a3, b3, d3):
            weights += [v, near(v)]
        load = load_pieces(z)
    else:
        table, gains = biases(pos_bias, time_bias, out_gain)
        bias = make_bias(table, plan, lengths, time_bucket)
        sent = send_rows(plan, hist_ids, table_rows, scale)
        got = [swap(s, "table", z.n, k + 1) for k, s in enumerate(sent)]
        own, route = keep_rows(plan, hist_ids, table_rows, scale)
        q_full = lax.all_gather(qkvu_proj, "table", axis=1, tiled=True)
        o_full = lax.all_gather(out_proj, "table", axis=1, tiled=True)
        weights = [
            lax.all_gather(embed_proj, "table", axis=1, tiled=True),
            lax.all_gather(q_full, "mp", axis=2, tiled=True),
            lax.all_gather(o_full, "mp", axis=0, tiled=True),
        ]
        load = load_whole
        keep, give = place_rows(own, route, *got)
        back = swap(give, "mp", z.mp)

    tokens = z.mine * z.length
    out_cols = width // z.mp
    out_own, out_give = pl.pallas_call(
        functools.partial(layer_kernel, z, load, len(weights)),
        out_shape=[jax.ShapeDtypeStruct((tokens, out_cols), BF)] * 2,
        in_specs=[sspec(), sspec()] + [vspec()] * 5 + [pl.BlockSpec(memory_space=pl.ANY)] * len(weights),
        out_specs=[vspec()] * 2,
        scratch_shapes=[
            pltpu.VMEM((z.width, width), BF),
            pltpu.VMEM((4, width, width), BF),
            pltpu.VMEM((width, width), BF),
            pltpu.VMEM((tokens, z.width), BF),
            pltpu.VMEM((tokens, width), BF),
            pltpu.VMEM((tokens, width), BF),
            pltpu.VMEM((4, tokens, width), BF),
            pltpu.VMEM((tokens, width), F32),
            pltpu.VMEM((tokens, width), BF),
            pltpu.SemaphoreType.DMA((3,)),
        ],
        compiler_params=params(),
        name="layer",
    )(plan, lengths, keep, back, in_gain.reshape(1, width), gains, bias, *weights)
    out_got = swap(out_give, "mp", z.mp)
    out = jnp.where(
        mp_pos == 0,
        jnp.concatenate([out_own, out_got], 0),
        jnp.concatenate([out_got, out_own], 0),
    )
    return out.reshape(z.pair, z.length, out_cols)


def solution(mesh):
    return jax.shard_map(
        body,
        mesh=mesh,
        in_specs=(
            P("table", None),
            P("table"),
            P("parts", None),
            P(("parts", "table")),
            P("parts"),
            P(("parts", "table"), None),
            P(None, "table"),
            P(),
            P(None, "table", "mp"),
            P("mp"),
            P("mp", "table"),
            P("mp", None),
            P("mp", None),
        ),
        out_specs=P(("parts", "table", "bal"), None, "mp"),
        check_vma=False,
    )
```

```python
import functools
import math

import jax
import jax.numpy as jnp
from jax import lax
from jax.experimental import pallas as pl
from jax.experimental.pallas import tpu as pltpu
from jax.sharding import PartitionSpec as P

epsilon = 1e-05
BF = jnp.bfloat16
F32 = jnp.float32
MIB = 1024 * 1024
FAR = -1e30


def buckets_of(length, buckets):
    found = []
    for d in range(length):
        b = d if d < 16 else 15 + sum(1 for power in range(4, 20) if d >= 2**power)
        found.append(min(b, buckets - 1))
    return found


def vspec():
    return pl.BlockSpec(memory_space=pltpu.VMEM)


def sspec():
    return pl.BlockSpec(memory_space=pltpu.SMEM)


def params(mib):
    return pltpu.CompilerParams(vmem_limit_bytes=mib * MIB)


def iota(shape, axis):
    return lax.broadcasted_iota(jnp.int32, shape, axis)


def dot(a, b):
    return jnp.dot(a, b, preferred_element_type=F32)


def dot_nt(a, b):
    return lax.dot_general(a, b, (((1,), (1,)), ((), ())), preferred_element_type=F32)


def cost(us):
    return pl.CostEstimate(flops=int(us * 9e8), bytes_accessed=int(us * 2e6), transcendentals=0)


def fence(*values):
    return lax.optimization_barrier(values)


class Sizes:
    def __init__(self, mesh_sizes, table_rows, hist_ids, lengths, pos_bias):
        self.n, self.bal, self.mp = mesh_sizes
        self.rows, self.width = table_rows.shape
        self.users, self.length = hist_ids.shape
        self.group = lengths.shape[0]
        self.pair = self.group // self.bal
        self.mine = self.pair // self.mp
        self.half = self.length // self.mp
        self.tokens = self.pair * self.half
        self.cap = self.pair * self.length // self.n
        self.heads = pos_bias.shape[0] * self.mp
        self.shift = self.rows.bit_length() - 1


def member(z, plan_ref, dest, slot):
    found = jnp.int32(0)
    for j in range(z.group):
        found = found + jnp.where(plan_ref[dest * z.group + j] == slot, j, 0)
    return found


def slot_of(z, mp_pos, s):
    if s < z.mine:
        return mp_pos * z.mine + s
    return (1 - mp_pos) * z.mine + (s - z.mine)


def token_ids(z, plan_ref, hist_ref, dest, bal_pos, mp_pos):
    parts = []
    for s in range(z.pair):
        slot = bal_pos * z.pair + slot_of(z, mp_pos, s)
        user = dest * z.group + member(z, plan_ref, dest, slot)
        row = hist_ref[pl.ds(user, 1), :]
        parts.append(jnp.where(mp_pos == 0, row[:, : z.half], row[:, z.half :]))
    return jnp.concatenate(parts, axis=1)


def scaled_rows(z, table_ref, scale_ref, rows_ref):
    chunk = 128

    def step(i, carry):
        start = pl.multiple_of(i * chunk, chunk)
        row = scale_ref[pl.ds(i, 1), :]
        column = jnp.broadcast_to(row, (chunk, chunk)).T
        for c in range(z.width // chunk):
            cols = slice(c * chunk, (c + 1) * chunk)
            rows_ref[pl.ds(start, chunk), cols] = (
                table_ref[pl.ds(start, chunk), cols].astype(F32) * column
            ).astype(BF)
        return carry

    lax.fori_loop(0, z.rows // chunk, step, 0)


def two_digits(values):
    row = iota((8, values.shape[1]), 0)
    high = lax.shift_right_logical(values, 7)
    low = values & 127
    return jnp.where(row == 0, high, jnp.where(row == 1, low, 0)).astype(F32).astype(BF)


def column_of(pairs):
    return (pairs[:, 0:1] * 128.0 + pairs[:, 1:2]).astype(jnp.int32)


def triangle(tokens):
    return (iota((tokens, tokens), 0) <= iota((tokens, tokens), 1)).astype(F32).astype(BF)


def send_kernel(z, plan_ref, hist_ref, table_ref, scale_ref, *refs):
    outs, rows_ref = refs[:-1], refs[-1]
    table_pos = lax.axis_index("table")
    bal_pos = lax.axis_index("bal")
    mp_pos = lax.axis_index("mp")
    scaled_rows(z, table_ref, scale_ref, rows_ref)
    tri = triangle(z.tokens)
    for k in range(1, z.n):
        dest = lax.rem(table_pos + k, z.n)
        ids = token_ids(z, plan_ref, hist_ref, dest, bal_pos, mp_pos)
        mine = lax.shift_right_logical(ids, z.shift) == table_pos
        flags = jnp.broadcast_to(mine.astype(F32), (8, z.tokens)).astype(BF)
        rank = dot(flags, tri)[0:1, :].astype(jnp.int32) - 1
        place = jnp.where(mine, rank, -1)
        compact = (iota((z.cap, z.tokens), 0) == place).astype(F32).astype(BF)
        local = column_of(dot_nt(compact, two_digits(ids & (z.rows - 1))))
        pick = (iota((z.cap, z.rows), 1) == local).astype(F32).astype(BF)
        outs[k - 1][...] = dot(pick, rows_ref[...]).astype(BF)


def keep_kernel(z, plan_ref, hist_ref, table_ref, scale_ref, own_ref, route_ref, rows_ref):
    table_pos = lax.axis_index("table")
    bal_pos = lax.axis_index("bal")
    mp_pos = lax.axis_index("mp")
    scaled_rows(z, table_ref, scale_ref, rows_ref)
    tri = triangle(z.tokens)
    ids = token_ids(z, plan_ref, hist_ref, table_pos, bal_pos, mp_pos)
    owner = lax.shift_right_logical(ids, z.shift)
    local = ids & (z.rows - 1)
    eye = (iota((z.tokens, z.tokens), 0) == iota((z.tokens, z.tokens), 1)).astype(F32).astype(BF)
    local_col = column_of(dot_nt(eye, two_digits(jnp.where(owner == table_pos, local, z.rows))))
    pick = (iota((z.tokens, z.rows), 1) == local_col).astype(F32).astype(BF)
    own_ref[...] = dot(pick, rows_ref[...]).astype(BF)
    lanes = max(8, z.n)
    offset = iota((lanes, z.tokens), 0)
    source = table_pos - offset
    source = jnp.where(source < 0, source + z.n, source)
    flags = (owner == source) & (offset >= 1) & (offset < z.n)
    rank = dot(flags.astype(F32).astype(BF), tri).astype(jnp.int32) - 1
    slots = z.n * z.cap
    slot = jnp.sum(
        jnp.where(flags, (offset - 1) * z.cap + rank + 1, 0), axis=0, keepdims=True
    )
    slot = jnp.where(slot == 0, slots, slot - 1)
    slot_col = column_of(dot_nt(eye, two_digits(slot)))
    route_ref[...] = (
        (iota((z.tokens, (z.n - 1) * z.cap), 1) == slot_col).astype(F32).astype(BF)
    )


def place_kernel(z, own_ref, route_ref, *refs):
    got, keep_ref, give_ref = refs[: z.n - 1], refs[-2], refs[-1]
    total = own_ref[...].astype(F32)
    block = max(1, 256 // z.cap)
    for k in range(0, z.n - 1, block):
        group = range(k, min(k + block, z.n - 1))
        rows = [got[g][...] for g in group]
        rows = rows[0] if len(rows) == 1 else jnp.concatenate(rows, axis=0)
        total = total + dot(route_ref[:, k * z.cap : k * z.cap + rows.shape[0]], rows)
    total = total.astype(BF)
    cut = z.tokens // z.mp
    keep_ref[...] = total[:cut]
    give_ref[...] = total[cut:]


def bias_kernel(z, small_ref, plan_ref, lens_ref, time_ref, bias_ref, *, buckets, tbuckets):
    table_pos = lax.axis_index("table")
    bal_pos = lax.axis_index("bal")
    mp_pos = lax.axis_index("mp")
    size = z.length
    number = buckets_of(size, buckets)
    lane = iota((8, size), 1)
    dist = jnp.where(lane == 0, 0, size - lane)
    position = []
    for h in range(z.heads):
        row = jnp.zeros((8, size), F32)
        for b in sorted(set(number)):
            low, high = number.index(b), size - 1 - number[::-1].index(b)
            row = jnp.where((dist >= low) & (dist <= high), small_ref[h, b], row)
        full = jnp.broadcast_to(row[0:1], (size, size))
        position.append(pltpu.roll(full, 0, 1, stride=1, stride_axis=0))
    for h in range(z.heads):
        for u in range(z.mine):
            bias_ref[u, h] = position[h]
    block = 32
    for u in range(z.mine):
        user = member(z, plan_ref, table_pos, bal_pos * z.pair + mp_pos * z.mine + u)
        size_u = lens_ref[user]
        events = time_ref[pl.ds(user, 1), :]
        columns = jnp.broadcast_to(events, (size, size)).T

        for r in range(0, size, block):
            rows = slice(r, r + block)
            diff = jnp.abs(columns[rows] - events)
            column = iota((block, size), 1)
            valid = (column <= iota((block, size), 0) + r) & (column < size_u)
            for h in range(z.heads):
                term = jnp.zeros((block, size), F32)
                for b in range(tbuckets):
                    term = jnp.where(diff == b, small_ref[h, buckets + b], term)
                bias_ref[u, h, rows, :] = jnp.where(valid, bias_ref[u, h, rows, :] + term, FAR)


def silu(s):
    half = 0.5 * s
    return half + half * jnp.tanh(half)


def layer_kernel(
    z, load, n_weights, plan_ref, lens_ref, keep_ref, got_ref, gain_ref, out_gain_ref, bias_hbm, *refs
):
    weights = refs[:n_weights]
    own_out, give_out = refs[n_weights : n_weights + 2]
    (e_ref, w_ref, o_ref, emb_ref, x_ref, xn_ref, act_ref, y_ref, z_ref, bias_ref, sems) = refs[n_weights + 2 :]
    table_pos = lax.axis_index("table")
    bal_pos = lax.axis_index("bal")
    mp_pos = lax.axis_index("mp")
    width = x_ref.shape[1]
    copies = load(weights, e_ref, w_ref, o_ref, sems)
    copies.insert(5, [pltpu.make_async_copy(bias_hbm, bias_ref, sems.at[6])])
    for group in copies:
        for c in group:
            c.start()
    for u in range(z.mine):
        near = pl.multiple_of(u * z.length + mp_pos * z.half, z.half)
        far = pl.multiple_of(u * z.length + (1 - mp_pos) * z.half, z.half)
        rows = slice(u * z.half, (u + 1) * z.half)
        emb_ref[pl.ds(near, z.half), :] = keep_ref[rows, :]
        emb_ref[pl.ds(far, z.half), :] = got_ref[rows, :]
    for c in copies[0]:
        c.wait()
    tokens = z.mine * z.length
    block = 256
    for r in range(0, tokens, block):
        rows = slice(r, r + block)
        x = dot(emb_ref[rows, :], e_ref[...]).astype(BF)
        x_ref[rows, :] = x
        x = x.astype(F32)
        mean = jnp.mean(x, axis=1, keepdims=True)
        centred = x - mean
        var = jnp.mean(centred * centred, axis=1, keepdims=True)
        xn_ref[rows, :] = (centred * lax.rsqrt(var + epsilon) * gain_ref[...]).astype(BF)
    step = 256
    for part in range(4):
        for c in copies[1 + part]:
            c.wait()

        def project(nb, carry):
            cols = pl.ds(pl.multiple_of(nb * step, step), step)
            s = dot(xn_ref[...], w_ref[part, :, cols])
            act_ref[part, :, cols] = silu(s).astype(BF)
            return carry

        lax.fori_loop(0, width // step, project, 0, unroll=True)
    for c in copies[5]:
        c.wait()
    scale = 1.0 / math.sqrt(width // z.heads)
    size = width // z.heads
    for u in range(z.mine):
        user = member(z, plan_ref, table_pos, bal_pos * z.pair + mp_pos * z.mine + u)
        inverse = 1.0 / jnp.full((1, z.length), lens_ref[user], jnp.int32).astype(F32)
        rows = slice(u * z.length, (u + 1) * z.length)

        def attend(h, carry):
            total, square = carry
            cols = pl.ds(pl.multiple_of(h * size, size), size)
            s = dot_nt(act_ref[2, rows, cols], act_ref[3, rows, cols]) * scale + bias_ref[u, h]
            a = (silu(s) * inverse).astype(BF)
            y = dot(a, act_ref[1, rows, cols])
            y_ref[rows, cols] = y
            return (
                total + jnp.sum(y, axis=1, keepdims=True),
                square + jnp.sum(y * y, axis=1, keepdims=True),
            )

        zero = jnp.zeros((z.length, 1), F32)
        total, square = lax.fori_loop(0, z.heads, attend, (zero, zero), unroll=4)
        mean = total / width
        var = square / width - mean * mean
        factor = lax.rsqrt(var + epsilon)
        for h in range(z.heads):
            cols = slice(h * size, (h + 1) * size)
            normed = (y_ref[rows, cols] - mean) * factor * out_gain_ref[h : h + 1, :]
            z_ref[rows, cols] = (normed * act_ref[0, rows, cols].astype(F32)).astype(BF)
    for c in copies[6]:
        c.wait()
    out_cols = width // z.mp
    for which, ref in ((1 - mp_pos, give_out), (mp_pos, own_out)):
        for nb in range(out_cols // step):
            cols = pl.ds(pl.multiple_of(which * out_cols + nb * step, step), step)
            term = dot(z_ref[...], o_ref[:, cols])
            ref[:, nb * step : (nb + 1) * step] = (
                term + x_ref[:, cols].astype(F32)
            ).astype(BF)


def swap(x, axis, size, k=1):
    return lax.ppermute(x, axis, [(i, (i + k) % size) for i in range(size)])


def cross(x, near_first):
    pairs = []
    for i in range(8):
        p, b, m = i // 4, i // 2 % 2, i % 2
        p, b = (p, 1 - b) if (m == 0) == near_first else (1 - p, b)
        pairs.append((i, (p * 2 + b) * 2 + m))
    return lax.ppermute(x, ("parts", "bal", "mp"), pairs)


def corner(x):
    return lax.ppermute(x, ("parts", "bal"), [(i, 3 - i) for i in range(4)])


def pack_kernel(e_ref, w_ref, o_ref, out_ref, sems):
    q = lax.axis_index("parts") * 2 + lax.axis_index("bal")
    m = lax.axis_index("mp")
    share = w_ref.shape[1] // 4
    cols = e_ref.shape[1]
    e_part = e_ref.shape[0] // 16
    o_part = o_ref.shape[0] // 8
    copies = []

    def add(src, dst):
        copies.append(pltpu.make_async_copy(src, dst, sems))

    for c in range(4):
        add(w_ref.at[c, at(q, share), :], out_ref.at[c * share : (c + 1) * share, :])
    first = 4 * share
    for j in range(2):
        lanes = slice(j * cols, (j + 1) * cols)
        add(e_ref.at[at((q * 2 + m) * 2 + j, e_part), :], out_ref.at[first : first + e_part, lanes])
        add(
            o_ref.at[at(q * 2 + j, o_part), :],
            out_ref.at[first + e_part : first + e_part + o_part, lanes],
        )
    for c in copies:
        c.start()
    for c in copies:
        c.wait()


def merge_kernel(*refs):
    out_ref, sem = refs[4:]
    copies = [pltpu.make_async_copy(refs[i], out_ref.at[i], sem) for i in range(4)]
    for c in copies:
        c.start()
    for c in copies:
        c.wait()


def at(x, size):
    return pl.ds(pl.multiple_of(x * size, size), size)


def load_pieces(z):
    def load(refs, e_ref, w_ref, o_ref, sems):
        t, m = lax.axis_index("table"), lax.axis_index("mp")
        p, b = lax.axis_index("parts"), lax.axis_index("bal")
        e_own, w_own, o_own, w_near, o_near = refs[:5]
        deep, cols = w_own.shape[1], w_own.shape[2]
        e_cols = e_own.shape[1]
        o_rows = o_own.shape[0]
        share = deep // 4
        e_part = e_ref.shape[0] // 16
        o_part = o_rows // 8
        first = 4 * share
        along_b, along_p = p * 2 + 1 - b, (1 - p) * 2 + b
        pieces = []
        for k in range(1, z.n):
            source = lax.rem(t + z.n - k, z.n)
            block = refs[PIECES[k - 1] : PIECES[k]]
            if len(block) == 2:
                block = [ref.at[i] for i in range(4) for ref in block]
            for i in range(4):
                for core, ref in ((m, block[2 * i]), (1 - m, block[2 * i + 1])):
                    q = (
                        p * 2 + b,
                        jnp.where(core == 0, along_b, along_p),
                        jnp.where(core == 0, along_p, along_b),
                        (1 - p) * 2 + 1 - b,
                    )[i]
                    pieces.append((ref, source, q, core))
        groups = [[] for _ in range(6)]

        def add(g, src, dst):
            groups[g].append(pltpu.make_async_copy(src, dst, sems.at[g]))

        add(0, e_own, e_ref.at[:, at(t, e_cols)])
        for ref, source, q, core in pieces:
            for j in range(2):
                lanes = slice(j * e_cols, (j + 1) * e_cols)
                rows = at((q * 2 + core) * 2 + j, e_part)
                add(0, ref.at[first : first + e_part, lanes], e_ref.at[rows, at(source, e_cols)])
        for c in range(4):
            for core, w in ((m, w_own), (1 - m, w_near)):
                add(1 + c, w.at[c], w_ref.at[c, at(t, deep), at(core, cols)])
            for ref, source, q, core in pieces:
                add(
                    1 + c,
                    ref.at[c * share : (c + 1) * share, :],
                    w_ref.at[c, at(source * 4 + q, share), at(core, cols)],
                )
        for core, o in ((m, o_own), (1 - m, o_near)):
            add(5, o, o_ref.at[at(core, o_rows), at(t, e_cols)])
        for ref, source, q, core in pieces:
            for j in range(2):
                lanes = slice(j * e_cols, (j + 1) * e_cols)
                rows = at(core * 8 + q * 2 + j, o_part)
                add(
                    5,
                    ref.at[first + e_part : first + e_part + o_part, lanes],
                    o_ref.at[rows, at(source, e_cols)],
                )
        return groups

    return load


def load_whole(refs, e_ref, w_ref, o_ref, sems):
    e, w, o = refs
    groups = [[pltpu.make_async_copy(e, e_ref, sems.at[0])]]
    groups += [[pltpu.make_async_copy(w.at[c], w_ref.at[c], sems.at[1 + c])] for c in range(4)]
    return groups + [[pltpu.make_async_copy(o, o_ref, sems.at[5])]]


def finish_kernel(own_ref, got_ref, out_ref):
    mp_pos = lax.axis_index("mp")
    tokens = own_ref.shape[0]
    out_ref[at(mp_pos, tokens), :] = own_ref[...]
    out_ref[at(1 - mp_pos, tokens), :] = got_ref[...]


PIECES = (5, 7, 9, 17)


def body(
    table_rows,
    row_scale,
    hist_ids,
    lengths,
    plan,
    time_bucket,
    embed_proj,
    in_gain,
    qkvu_proj,
    out_gain,
    out_proj,
    pos_bias,
    time_bias,
):
    axes = tuple(lax.axis_size(a) for a in ("table", "bal", "mp"))
    z = Sizes(axes, table_rows, hist_ids, lengths, pos_bias)
    width = in_gain.shape[0]
    mp_pos = lax.axis_index("mp")
    scale = row_scale.reshape(z.rows // 128, 128)
    send_rows = pl.pallas_call(
        functools.partial(send_kernel, z),
        out_shape=[jax.ShapeDtypeStruct((z.cap, z.width), BF)] * (z.n - 1),
        in_specs=[sspec(), vspec(), vspec(), vspec()],
        out_specs=[vspec()] * (z.n - 1),
        scratch_shapes=[pltpu.VMEM((z.rows, z.width), BF)],
        compiler_params=params(20),
        cost_estimate=cost(7),
        name="send_rows",
    )
    keep_rows = pl.pallas_call(
        functools.partial(keep_kernel, z),
        out_shape=[
            jax.ShapeDtypeStruct((z.tokens, z.width), BF),
            jax.ShapeDtypeStruct((z.tokens, (z.n - 1) * z.cap), BF),
        ],
        in_specs=[sspec(), vspec(), vspec(), vspec()],
        out_specs=[vspec()] * 2,
        scratch_shapes=[pltpu.VMEM((z.rows, z.width), BF)],
        compiler_params=params(20),
        cost_estimate=cost(7),
        name="keep_rows",
    )
    buckets, tbuckets = pos_bias.shape[1], time_bias.shape[1]
    make_bias = pl.pallas_call(
        functools.partial(bias_kernel, z, buckets=buckets, tbuckets=tbuckets),
        out_shape=jax.ShapeDtypeStruct((z.mine, z.heads, z.length, z.length), F32),
        in_specs=[sspec(), sspec(), sspec(), vspec()],
        out_specs=vspec(),
        compiler_params=params(14),
        cost_estimate=cost(7),
        name="bias",
    )
    place_rows = pl.pallas_call(
        functools.partial(place_kernel, z),
        out_shape=[jax.ShapeDtypeStruct((z.tokens // z.mp, z.width), BF)] * 2,
        in_specs=[vspec()] * (z.n + 1),
        out_specs=[vspec()] * 2,
        compiler_params=params(12),
        cost_estimate=cost(3),
        name="place_rows",
    )

    def both(x):
        other = swap(x, "mp", z.mp)
        return jnp.where(
            mp_pos == 0, jnp.concatenate([x, other], 0), jnp.concatenate([other, x], 0)
        )

    def biases(pos_bias, time_bias, out_gain):
        small = jnp.concatenate(
            [pos_bias, time_bias, out_gain.reshape(pos_bias.shape[0], -1)], axis=1
        )
        small = both(small)
        return small[:, : buckets + tbuckets], small[:, buckets + tbuckets :]

    if z.n == 4 and z.bal == 2 and lax.axis_size("parts") == 2:
        near = functools.partial(swap, axis="mp", size=2)
        hop = functools.partial(swap, axis="table", size=z.n)
        rows = qkvu_proj.shape[1] + z.width // 16 + out_proj.shape[0] // 8
        pack = pl.pallas_call(
            pack_kernel,
            out_shape=jax.ShapeDtypeStruct((rows, qkvu_proj.shape[2]), BF),
            in_specs=[pl.BlockSpec(memory_space=pltpu.HBM)] * 3,
            out_specs=vspec(),
            scratch_shapes=[pltpu.SemaphoreType.DMA],
            compiler_params=params(4),
            name="pack",
        )(embed_proj, qkvu_proj, out_proj)
        merge = pl.pallas_call(
            merge_kernel,
            out_shape=jax.ShapeDtypeStruct((4, rows, qkvu_proj.shape[2]), BF),
            in_specs=[pl.BlockSpec(memory_space=pl.ANY)] * 4,
            out_specs=vspec(),
            scratch_shapes=[pltpu.SemaphoreType.DMA],
            compiler_params=params(6),
            cost_estimate=cost(2),
            name="merge",
        )
        r1 = hop(pack)
        sent = send_rows(plan, hist_ids, table_rows, scale)
        w_near, o_near = near(qkvu_proj), near(out_proj)
        sent, small_in = fence(sent, (pos_bias, time_bias, out_gain))
        table, gains = biases(*small_in)
        r1, sent, table, w_near, o_near = fence(r1, sent, table, w_near, o_near)
        b1, a1 = cross(r1, False), cross(r1, True)
        got1 = swap(sent[0], "table", z.n, 1)
        r2 = hop(r1)
        bias = make_bias(table, plan, lengths, time_bucket)
        r1, r2, got1, a1, b1, bias, sent, plan1, gains = fence(
            r1, r2, got1, a1, b1, bias, sent, plan, gains
        )
        b2, a2, d1 = cross(r2, False), cross(r2, True), cross(b1, True)
        got3 = swap(sent[2], "table", z.n, 3)
        r3 = hop(r2)
        own, route = keep_rows(plan1, hist_ids, table_rows, scale)
        r1, a1, b1, d1, r2, r3, a2, b2, got3, own, route, sent = fence(
            r1, a1, b1, d1, r2, r3, a2, b2, got3, own, route, sent
        )
        a3, b3, d2 = cross(r3, True), cross(r3, False), cross(b2, True)
        got2 = swap(sent[1], "table", z.n, 2)
        chunk1 = merge(r1, a1, b1, d1)
        near1 = near(chunk1)
        a3, b3, r2, a2, b2, d2, near1, got2, r3 = fence(a3, b3, r2, a2, b2, d2, near1, got2, r3)
        d3 = cross(b3, True)
        keep, give = place_rows(own, route, got1, got2, got3)
        back = near(give)
        chunk2 = merge(r2, a2, b2, d2)
        near2 = near(chunk2)
        r3n, a3n, b3n = near(r3), near(a3), near(b3)
        weights = [embed_proj, qkvu_proj, out_proj, w_near, o_near, chunk1, near1, chunk2, near2]
        weights += [r3, r3n, a3, a3n, b3, b3n, d3, near(d3)]
        load = load_pieces(z)
    else:
        table, gains = biases(pos_bias, time_bias, out_gain)
        bias = make_bias(table, plan, lengths, time_bucket)
        sent = send_rows(plan, hist_ids, table_rows, scale)
        got = [swap(s, "table", z.n, k + 1) for k, s in enumerate(sent)]
        own, route = keep_rows(plan, hist_ids, table_rows, scale)
        q_full = lax.all_gather(qkvu_proj, "table", axis=1, tiled=True)
        o_full = lax.all_gather(out_proj, "table", axis=1, tiled=True)
        weights = [
            lax.all_gather(embed_proj, "table", axis=1, tiled=True),
            lax.all_gather(q_full, "mp", axis=2, tiled=True),
            lax.all_gather(o_full, "mp", axis=0, tiled=True),
        ]
        load = load_whole
        keep, give = place_rows(own, route, *got)
        back = swap(give, "mp", z.mp)

    tokens = z.mine * z.length
    out_cols = width // z.mp
    out_own, out_give = pl.pallas_call(
        functools.partial(layer_kernel, z, load, len(weights)),
        out_shape=[jax.ShapeDtypeStruct((tokens, out_cols), BF)] * 2,
        in_specs=[sspec(), sspec()]
        + [vspec()] * 4
        + [pl.BlockSpec(memory_space=pl.ANY)] * (1 + len(weights)),
        out_specs=[vspec()] * 2,
        scratch_shapes=[
            pltpu.VMEM((z.width, width), BF),
            pltpu.VMEM((4, width, width), BF),
            pltpu.VMEM((width, width), BF),
            pltpu.VMEM((tokens, z.width), BF),
            pltpu.VMEM((tokens, width), BF),
            pltpu.VMEM((tokens, width), BF),
            pltpu.VMEM((4, tokens, width), BF),
            pltpu.VMEM((tokens, width), F32),
            pltpu.VMEM((tokens, width), BF),
            pltpu.VMEM(bias.shape, F32),
            pltpu.SemaphoreType.DMA((7,)),
        ],
        compiler_params=params(44),
        name="layer",
    )(plan, lengths, keep, back, in_gain.reshape(1, width), gains, bias, *weights)
    out_got = swap(out_give, "mp", z.mp)
    out = pl.pallas_call(
        finish_kernel,
        out_shape=jax.ShapeDtypeStruct((z.mp * tokens, out_cols), BF),
        in_specs=[vspec()] * 2,
        out_specs=vspec(),
        compiler_params=params(8),
        name="finish",
    )(out_own, out_got)
    return out.reshape(z.pair, z.length, out_cols)


def solution(mesh):
    return jax.shard_map(
        body,
        mesh=mesh,
        in_specs=(
            P("table", None),
            P("table"),
            P("parts", None),
            P(("parts", "table")),
            P("parts"),
            P(("parts", "table"), None),
            P(None, "table"),
            P(),
            P(None, "table", "mp"),
            P("mp"),
            P("mp", "table"),
            P("mp", None),
            P("mp", None),
        ),
        out_specs=P(("parts", "table", "bal"), None, "mp"),
        check_vma=False,
    )
```

```python
import functools
import math

import jax
import jax.numpy as jnp
from jax import lax
from jax.experimental import pallas as pl
from jax.experimental.pallas import tpu as pltpu
from jax.sharding import PartitionSpec as P

epsilon = 1e-05
BF = jnp.bfloat16
F32 = jnp.float32
MIB = 1024 * 1024
FAR = -1e30
ROW_BLOCKS = 1


def buckets_of(length, buckets):
    found = []
    for d in range(length):
        b = d if d < 16 else 15 + sum(1 for power in range(4, 20) if d >= 2**power)
        found.append(min(b, buckets - 1))
    return found


def vspec():
    return pl.BlockSpec(memory_space=pltpu.VMEM)


def sspec():
    return pl.BlockSpec(memory_space=pltpu.SMEM)


def params(mib):
    return pltpu.CompilerParams(vmem_limit_bytes=mib * MIB)


def iota(shape, axis):
    return lax.broadcasted_iota(jnp.int32, shape, axis)


def dot(a, b):
    return jnp.dot(a, b, preferred_element_type=F32)


def dot_nt(a, b):
    return lax.dot_general(a, b, (((1,), (1,)), ((), ())), preferred_element_type=F32)


def cost(us):
    return pl.CostEstimate(flops=int(us * 9e8), bytes_accessed=int(us * 2e6), transcendentals=0)


def fence(*values):
    return lax.optimization_barrier(values)


class Sizes:
    def __init__(self, mesh_sizes, table_rows, hist_ids, lengths, pos_bias):
        self.n, self.bal, self.mp = mesh_sizes
        self.rows, self.width = table_rows.shape
        self.users, self.length = hist_ids.shape
        self.group = lengths.shape[0]
        self.pair = self.group // self.bal
        self.mine = self.pair // self.mp
        self.half = self.length // self.mp
        self.tokens = self.pair * self.half
        self.cap = self.pair * self.length // self.n
        self.heads = pos_bias.shape[0] * self.mp
        self.shift = self.rows.bit_length() - 1


def member(z, plan_ref, dest, slot):
    found = jnp.int32(0)
    for j in range(z.group):
        found = found + jnp.where(plan_ref[dest * z.group + j] == slot, j, 0)
    return found


def slot_of(z, mp_pos, s):
    if s < z.mine:
        return mp_pos * z.mine + s
    return (1 - mp_pos) * z.mine + (s - z.mine)


def token_ids(z, plan_ref, hist_ref, dest, bal_pos, mp_pos):
    parts = []
    for s in range(z.pair):
        slot = bal_pos * z.pair + slot_of(z, mp_pos, s)
        user = dest * z.group + member(z, plan_ref, dest, slot)
        row = hist_ref[pl.ds(user, 1), :]
        parts.append(jnp.where(mp_pos == 0, row[:, : z.half], row[:, z.half :]))
    return jnp.concatenate(parts, axis=1)


def scaled_rows(z, table_ref, scale_ref, rows_ref):
    chunk = 128

    def step(i, carry):
        start = pl.multiple_of(i * chunk, chunk)
        row = scale_ref[pl.ds(i, 1), :]
        column = jnp.broadcast_to(row, (chunk, chunk)).T
        for c in range(z.width // chunk):
            cols = slice(c * chunk, (c + 1) * chunk)
            rows_ref[pl.ds(start, chunk), cols] = (
                table_ref[pl.ds(start, chunk), cols].astype(F32) * column
            ).astype(BF)
        return carry

    lax.fori_loop(0, z.rows // chunk, step, 0)


def two_digits(values):
    row = iota((8, values.shape[1]), 0)
    high = lax.shift_right_logical(values, 7)
    low = values & 127
    return jnp.where(row == 0, high, jnp.where(row == 1, low, 0)).astype(F32).astype(BF)


def column_of(pairs):
    return (pairs[:, 0:1] * 128.0 + pairs[:, 1:2]).astype(jnp.int32)


def triangle(tokens):
    return (iota((tokens, tokens), 0) <= iota((tokens, tokens), 1)).astype(F32).astype(BF)


def send_kernel(z, plan_ref, hist_ref, table_ref, scale_ref, *refs):
    outs, rows_ref = refs[:-1], refs[-1]
    table_pos = lax.axis_index("table")
    bal_pos = lax.axis_index("bal")
    mp_pos = lax.axis_index("mp")
    scaled_rows(z, table_ref, scale_ref, rows_ref)
    tri = triangle(z.tokens)
    for k in range(1, z.n):
        dest = lax.rem(table_pos + k, z.n)
        ids = token_ids(z, plan_ref, hist_ref, dest, bal_pos, mp_pos)
        mine = lax.shift_right_logical(ids, z.shift) == table_pos
        flags = jnp.broadcast_to(mine.astype(F32), (8, z.tokens)).astype(BF)
        rank = dot(flags, tri)[0:1, :].astype(jnp.int32) - 1
        place = jnp.where(mine, rank, -1)
        compact = (iota((z.cap, z.tokens), 0) == place).astype(F32).astype(BF)
        local = column_of(dot_nt(compact, two_digits(ids & (z.rows - 1))))
        pick = (iota((z.cap, z.rows), 1) == local).astype(F32).astype(BF)
        outs[k - 1][...] = dot(pick, rows_ref[...]).astype(BF)


def keep_kernel(z, plan_ref, hist_ref, table_ref, scale_ref, own_ref, route_ref, rows_ref):
    table_pos = lax.axis_index("table")
    bal_pos = lax.axis_index("bal")
    mp_pos = lax.axis_index("mp")
    scaled_rows(z, table_ref, scale_ref, rows_ref)
    tri = triangle(z.tokens)
    ids = token_ids(z, plan_ref, hist_ref, table_pos, bal_pos, mp_pos)
    owner = lax.shift_right_logical(ids, z.shift)
    local = ids & (z.rows - 1)
    eye = (iota((z.tokens, z.tokens), 0) == iota((z.tokens, z.tokens), 1)).astype(F32).astype(BF)
    local_col = column_of(dot_nt(eye, two_digits(jnp.where(owner == table_pos, local, z.rows))))
    pick = (iota((z.tokens, z.rows), 1) == local_col).astype(F32).astype(BF)
    own_ref[...] = dot(pick, rows_ref[...]).astype(BF)
    lanes = max(8, z.n)
    offset = iota((lanes, z.tokens), 0)
    source = table_pos - offset
    source = jnp.where(source < 0, source + z.n, source)
    flags = (owner == source) & (offset >= 1) & (offset < z.n)
    rank = dot(flags.astype(F32).astype(BF), tri).astype(jnp.int32) - 1
    slots = z.n * z.cap
    slot = jnp.sum(
        jnp.where(flags, (offset - 1) * z.cap + rank + 1, 0), axis=0, keepdims=True
    )
    slot = jnp.where(slot == 0, slots, slot - 1)
    slot_col = column_of(dot_nt(eye, two_digits(slot)))
    route_ref[...] = (
        (iota((z.tokens, (z.n - 1) * z.cap), 1) == slot_col).astype(F32).astype(BF)
    )


def place_kernel(z, own_ref, route_ref, *refs):
    got, keep_ref, give_ref = refs[: z.n - 1], refs[-2], refs[-1]
    total = own_ref[...].astype(F32)
    block = max(1, 256 // z.cap)
    for k in range(0, z.n - 1, block):
        group = range(k, min(k + block, z.n - 1))
        rows = [got[g][...] for g in group]
        rows = rows[0] if len(rows) == 1 else jnp.concatenate(rows, axis=0)
        total = total + dot(route_ref[:, k * z.cap : k * z.cap + rows.shape[0]], rows)
    total = total.astype(BF)
    cut = z.tokens // z.mp
    keep_ref[...] = total[:cut]
    give_ref[...] = total[cut:]


def bias_kernel(z, small_ref, plan_ref, lens_ref, time_ref, bias_ref, *, buckets, tbuckets):
    table_pos = lax.axis_index("table")
    bal_pos = lax.axis_index("bal")
    mp_pos = lax.axis_index("mp")
    size = z.length
    number = buckets_of(size, buckets)
    lane = iota((8, size), 1)
    dist = jnp.where(lane == 0, 0, size - lane)
    position = []
    for h in range(z.heads):
        row = jnp.zeros((8, size), F32)
        for b in sorted(set(number)):
            low, high = number.index(b), size - 1 - number[::-1].index(b)
            row = jnp.where((dist >= low) & (dist <= high), small_ref[h, b], row)
        full = jnp.broadcast_to(row[0:1], (size, size))
        position.append(pltpu.roll(full, 0, 1, stride=1, stride_axis=0))
    for h in range(z.heads):
        for u in range(z.mine):
            bias_ref[u, h] = position[h]
    block = 32
    for u in range(z.mine):
        user = member(z, plan_ref, table_pos, bal_pos * z.pair + mp_pos * z.mine + u)
        size_u = lens_ref[user]
        events = time_ref[pl.ds(user, 1), :]
        columns = jnp.broadcast_to(events, (size, size)).T

        for r in range(0, size, block):
            rows = slice(r, r + block)
            diff = jnp.abs(columns[rows] - events)
            column = iota((block, size), 1)
            valid = (column <= iota((block, size), 0) + r) & (column < size_u)
            for h in range(z.heads):
                term = jnp.zeros((block, size), F32)
                for b in range(tbuckets):
                    term = jnp.where(diff == b, small_ref[h, buckets + b], term)
                bias_ref[u, h, rows, :] = jnp.where(
                    valid, 0.5 * (bias_ref[u, h, rows, :] + term), FAR
                )


def silu(s):
    half = 0.5 * s
    return half + half * jnp.tanh(half)


def layer_kernel(
    z, load, n_weights, plan_ref, lens_ref, keep_ref, got_ref, gain_ref, out_gain_ref, bias_hbm, *refs
):
    weights = refs[:n_weights]
    own_out, give_out = refs[n_weights : n_weights + 2]
    (e_ref, w_ref, o_ref, emb_ref, x_ref, xn_ref, act_ref, y_ref, z_ref, bias_ref, sems) = refs[n_weights + 2 :]
    table_pos = lax.axis_index("table")
    bal_pos = lax.axis_index("bal")
    mp_pos = lax.axis_index("mp")
    width = x_ref.shape[1]
    copies = load(weights, e_ref, w_ref, o_ref, sems)
    copies.insert(5, [pltpu.make_async_copy(bias_hbm, bias_ref, sems.at[6])])
    for group in copies:
        for c in group:
            c.start()
    for u in range(z.mine):
        near = pl.multiple_of(u * z.length + mp_pos * z.half, z.half)
        far = pl.multiple_of(u * z.length + (1 - mp_pos) * z.half, z.half)
        rows = slice(u * z.half, (u + 1) * z.half)
        emb_ref[pl.ds(near, z.half), :] = keep_ref[rows, :]
        emb_ref[pl.ds(far, z.half), :] = got_ref[rows, :]
    for c in copies[0]:
        c.wait()
    tokens = z.mine * z.length
    block = 256
    for r in range(0, tokens, block):
        rows = slice(r, r + block)
        x = dot(emb_ref[rows, :], e_ref[...]).astype(BF)
        x_ref[rows, :] = x
        x = x.astype(F32)
        mean = jnp.mean(x, axis=1, keepdims=True)
        centred = x - mean
        var = jnp.mean(centred * centred, axis=1, keepdims=True)
        xn_ref[rows, :] = (centred * lax.rsqrt(var + epsilon) * gain_ref[...]).astype(BF)
    step = 256
    for part in range(4):
        for c in copies[1 + part]:
            c.wait()

        def project(nb, carry):
            cols = pl.ds(pl.multiple_of(nb * step, step), step)
            s = dot(xn_ref[...], w_ref[part, :, cols])
            act_ref[part, :, cols] = silu(s).astype(BF)
            return carry

        lax.fori_loop(0, width // step, project, 0, unroll=True)
    for c in copies[5]:
        c.wait()
    scale = 0.5 / math.sqrt(width // z.heads)
    size = width // z.heads
    for u in range(z.mine):
        user = member(z, plan_ref, table_pos, bal_pos * z.pair + mp_pos * z.mine + u)
        inverse = 1.0 / jnp.full((1, z.length), lens_ref[user], jnp.int32).astype(F32)
        rows = slice(u * z.length, (u + 1) * z.length)

        block = z.length // ROW_BLOCKS
        total = [jnp.zeros((block, 1), F32) for _ in range(ROW_BLOCKS)]
        square = [jnp.zeros((block, 1), F32) for _ in range(ROW_BLOCKS)]
        for h in range(z.heads):
            cols = slice(h * size, (h + 1) * size)
            for part in range(ROW_BLOCKS):
                first = u * z.length + part * block
                mine = slice(first, first + block)
                keys = slice(u * z.length, first + block)
                seen = (part + 1) * block
                s = dot_nt(act_ref[2, mine, cols], act_ref[3, keys, cols]) * scale
                s = s + bias_ref[u, h, part * block : seen, :seen]
                a = ((s + s * jnp.tanh(s)) * inverse[:, :seen]).astype(BF)
                y = dot(a, act_ref[1, keys, cols])
                y_ref[mine, cols] = y
                total[part] = total[part] + jnp.sum(y, axis=1, keepdims=True)
                square[part] = square[part] + jnp.sum(y * y, axis=1, keepdims=True)
        total, square = jnp.concatenate(total, 0), jnp.concatenate(square, 0)
        mean = total / width
        var = square / width - mean * mean
        factor = lax.rsqrt(var + epsilon)
        for h in range(z.heads):
            cols = slice(h * size, (h + 1) * size)
            normed = (y_ref[rows, cols] - mean) * factor * out_gain_ref[h : h + 1, :]
            z_ref[rows, cols] = (normed * act_ref[0, rows, cols].astype(F32)).astype(BF)
    for c in copies[6]:
        c.wait()
    out_cols = width // z.mp
    for which, ref in ((1 - mp_pos, give_out), (mp_pos, own_out)):
        for nb in range(out_cols // step):
            cols = pl.ds(pl.multiple_of(which * out_cols + nb * step, step), step)
            term = dot(z_ref[...], o_ref[:, cols])
            ref[:, nb * step : (nb + 1) * step] = (
                term + x_ref[:, cols].astype(F32)
            ).astype(BF)


def swap(x, axis, size, k=1):
    return lax.ppermute(x, axis, [(i, (i + k) % size) for i in range(size)])


def cross(x, near_first):
    pairs = []
    for i in range(8):
        p, b, m = i // 4, i // 2 % 2, i % 2
        p, b = (p, 1 - b) if (m == 0) == near_first else (1 - p, b)
        pairs.append((i, (p * 2 + b) * 2 + m))
    return lax.ppermute(x, ("parts", "bal", "mp"), pairs)


def corner(x):
    return lax.ppermute(x, ("parts", "bal"), [(i, 3 - i) for i in range(4)])


def pack_kernel(e_ref, w_ref, o_ref, out_ref, sems):
    q = lax.axis_index("parts") * 2 + lax.axis_index("bal")
    m = lax.axis_index("mp")
    share = w_ref.shape[1] // 4
    cols = e_ref.shape[1]
    e_part = e_ref.shape[0] // 16
    o_part = o_ref.shape[0] // 8
    copies = []

    def add(src, dst):
        copies.append(pltpu.make_async_copy(src, dst, sems))

    for c in range(4):
        add(w_ref.at[c, at(q, share), :], out_ref.at[c * share : (c + 1) * share, :])
    first = 4 * share
    for j in range(2):
        lanes = slice(j * cols, (j + 1) * cols)
        add(e_ref.at[at((q * 2 + m) * 2 + j, e_part), :], out_ref.at[first : first + e_part, lanes])
        add(
            o_ref.at[at(q * 2 + j, o_part), :],
            out_ref.at[first + e_part : first + e_part + o_part, lanes],
        )
    for c in copies:
        c.start()
    for c in copies:
        c.wait()


def merge_kernel(*refs):
    out_ref, sem = refs[4:]
    copies = [pltpu.make_async_copy(refs[i], out_ref.at[i], sem) for i in range(4)]
    for c in copies:
        c.start()
    for c in copies:
        c.wait()


def at(x, size):
    return pl.ds(pl.multiple_of(x * size, size), size)


def load_pieces(z):
    def load(refs, e_ref, w_ref, o_ref, sems):
        t, m = lax.axis_index("table"), lax.axis_index("mp")
        p, b = lax.axis_index("parts"), lax.axis_index("bal")
        e_own, w_own, o_own, w_near, o_near = refs[:5]
        deep, cols = w_own.shape[1], w_own.shape[2]
        e_cols = e_own.shape[1]
        o_rows = o_own.shape[0]
        share = deep // 4
        e_part = e_ref.shape[0] // 16
        o_part = o_rows // 8
        first = 4 * share
        along_b, along_p = p * 2 + 1 - b, (1 - p) * 2 + b
        pieces = []
        for k in range(1, z.n):
            source = lax.rem(t + z.n - k, z.n)
            block = refs[PIECES[k - 1] : PIECES[k]]
            if len(block) == 2:
                block = [ref.at[i] for i in range(4) for ref in block]
            for i in range(4):
                for core, ref in ((m, block[2 * i]), (1 - m, block[2 * i + 1])):
                    q = (
                        p * 2 + b,
                        jnp.where(core == 0, along_b, along_p),
                        jnp.where(core == 0, along_p, along_b),
                        (1 - p) * 2 + 1 - b,
                    )[i]
                    pieces.append((ref, source, q, core))
        groups = [[] for _ in range(6)]

        def add(g, src, dst):
            groups[g].append(pltpu.make_async_copy(src, dst, sems.at[g]))

        add(0, e_own, e_ref.at[:, at(t, e_cols)])
        for ref, source, q, core in pieces:
            for j in range(2):
                lanes = slice(j * e_cols, (j + 1) * e_cols)
                rows = at((q * 2 + core) * 2 + j, e_part)
                add(0, ref.at[first : first + e_part, lanes], e_ref.at[rows, at(source, e_cols)])
        for c in range(4):
            for core, w in ((m, w_own), (1 - m, w_near)):
                add(1 + c, w.at[c], w_ref.at[c, at(t, deep), at(core, cols)])
            for ref, source, q, core in pieces:
                add(
                    1 + c,
                    ref.at[c * share : (c + 1) * share, :],
                    w_ref.at[c, at(source * 4 + q, share), at(core, cols)],
                )
        for core, o in ((m, o_own), (1 - m, o_near)):
            add(5, o, o_ref.at[at(core, o_rows), at(t, e_cols)])
        for ref, source, q, core in pieces:
            for j in range(2):
                lanes = slice(j * e_cols, (j + 1) * e_cols)
                rows = at(core * 8 + q * 2 + j, o_part)
                add(
                    5,
                    ref.at[first + e_part : first + e_part + o_part, lanes],
                    o_ref.at[rows, at(source, e_cols)],
                )
        return groups

    return load


def load_whole(refs, e_ref, w_ref, o_ref, sems):
    e, w, o = refs
    groups = [[pltpu.make_async_copy(e, e_ref, sems.at[0])]]
    groups += [[pltpu.make_async_copy(w.at[c], w_ref.at[c], sems.at[1 + c])] for c in range(4)]
    return groups + [[pltpu.make_async_copy(o, o_ref, sems.at[5])]]


def finish_kernel(own_ref, got_ref, out_ref):
    mp_pos = lax.axis_index("mp")
    tokens = own_ref.shape[0]
    out_ref[at(mp_pos, tokens), :] = own_ref[...]
    out_ref[at(1 - mp_pos, tokens), :] = got_ref[...]


PIECES = (5, 7, 9, 17)


def body(
    table_rows,
    row_scale,
    hist_ids,
    lengths,
    plan,
    time_bucket,
    embed_proj,
    in_gain,
    qkvu_proj,
    out_gain,
    out_proj,
    pos_bias,
    time_bias,
):
    axes = tuple(lax.axis_size(a) for a in ("table", "bal", "mp"))
    z = Sizes(axes, table_rows, hist_ids, lengths, pos_bias)
    width = in_gain.shape[0]
    mp_pos = lax.axis_index("mp")
    scale = row_scale.reshape(z.rows // 128, 128)
    send_rows = pl.pallas_call(
        functools.partial(send_kernel, z),
        out_shape=[jax.ShapeDtypeStruct((z.cap, z.width), BF)] * (z.n - 1),
        in_specs=[sspec(), vspec(), vspec(), vspec()],
        out_specs=[vspec()] * (z.n - 1),
        scratch_shapes=[pltpu.VMEM((z.rows, z.width), BF)],
        compiler_params=params(20),
        cost_estimate=cost(7),
        name="send_rows",
    )
    keep_rows = pl.pallas_call(
        functools.partial(keep_kernel, z),
        out_shape=[
            jax.ShapeDtypeStruct((z.tokens, z.width), BF),
            jax.ShapeDtypeStruct((z.tokens, (z.n - 1) * z.cap), BF),
        ],
        in_specs=[sspec(), vspec(), vspec(), vspec()],
        out_specs=[vspec()] * 2,
        scratch_shapes=[pltpu.VMEM((z.rows, z.width), BF)],
        compiler_params=params(20),
        cost_estimate=cost(7),
        name="keep_rows",
    )
    buckets, tbuckets = pos_bias.shape[1], time_bias.shape[1]
    make_bias = pl.pallas_call(
        functools.partial(bias_kernel, z, buckets=buckets, tbuckets=tbuckets),
        out_shape=jax.ShapeDtypeStruct((z.mine, z.heads, z.length, z.length), F32),
        in_specs=[sspec(), sspec(), sspec(), vspec()],
        out_specs=vspec(),
        compiler_params=params(14),
        cost_estimate=cost(7),
        name="bias",
    )
    place_rows = pl.pallas_call(
        functools.partial(place_kernel, z),
        out_shape=[jax.ShapeDtypeStruct((z.tokens // z.mp, z.width), BF)] * 2,
        in_specs=[vspec()] * (z.n + 1),
        out_specs=[vspec()] * 2,
        compiler_params=params(12),
        cost_estimate=cost(3),
        name="place_rows",
    )

    def both(x):
        other = swap(x, "mp", z.mp)
        return jnp.where(
            mp_pos == 0, jnp.concatenate([x, other], 0), jnp.concatenate([other, x], 0)
        )

    def biases(pos_bias, time_bias, out_gain):
        small = jnp.concatenate(
            [pos_bias, time_bias, out_gain.reshape(pos_bias.shape[0], -1)], axis=1
        )
        small = both(small)
        return small[:, : buckets + tbuckets], small[:, buckets + tbuckets :]

    if z.n == 4 and z.bal == 2 and lax.axis_size("parts") == 2:
        near = functools.partial(swap, axis="mp", size=2)
        hop = functools.partial(swap, axis="table", size=z.n)
        rows = qkvu_proj.shape[1] + z.width // 16 + out_proj.shape[0] // 8
        pack = pl.pallas_call(
            pack_kernel,
            out_shape=jax.ShapeDtypeStruct((rows, qkvu_proj.shape[2]), BF),
            in_specs=[pl.BlockSpec(memory_space=pltpu.HBM)] * 3,
            out_specs=vspec(),
            scratch_shapes=[pltpu.SemaphoreType.DMA],
            compiler_params=params(60),
            name="pack",
        )(embed_proj, qkvu_proj, out_proj)
        merge = pl.pallas_call(
            merge_kernel,
            out_shape=jax.ShapeDtypeStruct((4, rows, qkvu_proj.shape[2]), BF),
            in_specs=[pl.BlockSpec(memory_space=pl.ANY)] * 4,
            out_specs=vspec(),
            scratch_shapes=[pltpu.SemaphoreType.DMA],
            compiler_params=params(6),
            cost_estimate=cost(2),
            name="merge",
        )
        r1 = hop(pack)
        sent = send_rows(plan, hist_ids, table_rows, scale)
        w_near, o_near = near(qkvu_proj), near(out_proj)
        sent, small_in = fence(sent, (pos_bias, time_bias, out_gain))
        table, gains = biases(*small_in)
        r1, sent, table, w_near, o_near = fence(r1, sent, table, w_near, o_near)
        b1, a1 = cross(r1, False), cross(r1, True)
        got1 = swap(sent[0], "table", z.n, 1)
        r2 = hop(r1)
        bias = make_bias(table, plan, lengths, time_bucket)
        r1, a1, b1, r2, got1, bias, sent, plan1, gains = fence(
            r1, a1, b1, r2, got1, bias, sent, plan, gains
        )
        b2, a2, d1 = cross(r2, False), cross(r2, True), cross(b1, True)
        got3 = swap(sent[2], "table", z.n, 3)
        r3 = hop(r2)
        own, route = keep_rows(plan1, hist_ids, table_rows, scale)
        r1, a1, b1, d1, r2, a2, b2, r3, got3, own, route, sent = fence(
            r1, a1, b1, d1, r2, a2, b2, r3, got3, own, route, sent
        )
        a3, b3, d2 = cross(r3, True), cross(r3, False), cross(b2, True)
        got2 = swap(sent[1], "table", z.n, 2)
        chunk1 = merge(r1, a1, b1, d1)
        near1 = near(chunk1)
        a3, b3, r2, a2, b2, d2, near1, got2, r3 = fence(a3, b3, r2, a2, b2, d2, near1, got2, r3)
        d3 = cross(b3, True)
        keep, give = place_rows(own, route, got1, got2, got3)
        back = near(give)
        chunk2 = merge(r2, a2, b2, d2)
        near2 = near(chunk2)
        r3n, a3n, b3n = near(r3), near(a3), near(b3)
        weights = [embed_proj, qkvu_proj, out_proj, w_near, o_near, chunk1, near1, chunk2, near2]
        weights += [r3, r3n, a3, a3n, b3, b3n, d3, near(d3)]
        load = load_pieces(z)
    else:
        table, gains = biases(pos_bias, time_bias, out_gain)
        bias = make_bias(table, plan, lengths, time_bucket)
        sent = send_rows(plan, hist_ids, table_rows, scale)
        got = [swap(s, "table", z.n, k + 1) for k, s in enumerate(sent)]
        own, route = keep_rows(plan, hist_ids, table_rows, scale)
        q_full = lax.all_gather(qkvu_proj, "table", axis=1, tiled=True)
        o_full = lax.all_gather(out_proj, "table", axis=1, tiled=True)
        weights = [
            lax.all_gather(embed_proj, "table", axis=1, tiled=True),
            lax.all_gather(q_full, "mp", axis=2, tiled=True),
            lax.all_gather(o_full, "mp", axis=0, tiled=True),
        ]
        load = load_whole
        keep, give = place_rows(own, route, *got)
        back = swap(give, "mp", z.mp)

    tokens = z.mine * z.length
    out_cols = width // z.mp
    out_own, out_give = pl.pallas_call(
        functools.partial(layer_kernel, z, load, len(weights)),
        out_shape=[jax.ShapeDtypeStruct((tokens, out_cols), BF)] * 2,
        in_specs=[sspec(), sspec()]
        + [vspec()] * 4
        + [pl.BlockSpec(memory_space=pl.ANY)] * (1 + len(weights)),
        out_specs=[vspec()] * 2,
        scratch_shapes=[
            pltpu.VMEM((z.width, width), BF),
            pltpu.VMEM((4, width, width), BF),
            pltpu.VMEM((width, width), BF),
            pltpu.VMEM((tokens, z.width), BF),
            pltpu.VMEM((tokens, width), BF),
            pltpu.VMEM((tokens, width), BF),
            pltpu.VMEM((4, tokens, width), BF),
            pltpu.VMEM((tokens, width), F32),
            pltpu.VMEM((tokens, width), BF),
            pltpu.VMEM(bias.shape, F32),
            pltpu.SemaphoreType.DMA((7,)),
        ],
        compiler_params=params(36),
        name="layer",
    )(plan, lengths, keep, back, in_gain.reshape(1, width), gains, bias, *weights)
    out_got = swap(out_give, "mp", z.mp)
    out = pl.pallas_call(
        finish_kernel,
        out_shape=jax.ShapeDtypeStruct((z.mp * tokens, out_cols), BF),
        in_specs=[vspec()] * 2,
        out_specs=vspec(),
        compiler_params=params(8),
        name="finish",
    )(out_own, out_got)
    return out.reshape(z.pair, z.length, out_cols)


def solution(mesh):
    return jax.shard_map(
        body,
        mesh=mesh,
        in_specs=(
            P("table", None),
            P("table"),
            P("parts", None),
            P(("parts", "table")),
            P("parts"),
            P(("parts", "table"), None),
            P(None, "table"),
            P(),
            P(None, "table", "mp"),
            P("mp"),
            P("mp", "table"),
            P("mp", None),
            P("mp", None),
        ),
        out_specs=P(("parts", "table", "bal"), None, "mp"),
        check_vma=False,
    )
```

```python
import functools
import math

import jax
import jax.numpy as jnp
from jax import lax
from jax.experimental import pallas as pl
from jax.experimental.pallas import tpu as pltpu
from jax.sharding import PartitionSpec as P

epsilon = 1e-05
BF = jnp.bfloat16
F32 = jnp.float32
MIB = 1024 * 1024
FAR = -1e30
ROW_BLOCKS = 1


def buckets_of(length, buckets):
    found = []
    for d in range(length):
        b = d if d < 16 else 15 + sum(1 for power in range(4, 20) if d >= 2**power)
        found.append(min(b, buckets - 1))
    return found


def vspec():
    return pl.BlockSpec(memory_space=pltpu.VMEM)


def sspec():
    return pl.BlockSpec(memory_space=pltpu.SMEM)


def params(mib):
    return pltpu.CompilerParams(vmem_limit_bytes=mib * MIB)


def iota(shape, axis):
    return lax.broadcasted_iota(jnp.int32, shape, axis)


def dot(a, b):
    return jnp.dot(a, b, preferred_element_type=F32)


def dot_nt(a, b):
    return lax.dot_general(a, b, (((1,), (1,)), ((), ())), preferred_element_type=F32)


def cost(us):
    return pl.CostEstimate(flops=int(us * 9e8), bytes_accessed=int(us * 2e6), transcendentals=0)


def fence(*values):
    return lax.optimization_barrier(values)


class Sizes:
    def __init__(self, mesh_sizes, table_rows, hist_ids, lengths, pos_bias):
        self.n, self.bal, self.mp = mesh_sizes
        self.rows, self.width = table_rows.shape
        self.users, self.length = hist_ids.shape
        self.group = lengths.shape[0]
        self.pair = self.group // self.bal
        self.mine = self.pair // self.mp
        self.half = self.length // self.mp
        self.tokens = self.pair * self.half
        self.cap = self.pair * self.length // self.n
        self.heads = pos_bias.shape[0] * self.mp
        self.shift = self.rows.bit_length() - 1


def member(z, plan_ref, dest, slot):
    found = jnp.int32(0)
    for j in range(z.group):
        found = found + jnp.where(plan_ref[dest * z.group + j] == slot, j, 0)
    return found


def slot_of(z, mp_pos, s):
    if s < z.mine:
        return mp_pos * z.mine + s
    return (1 - mp_pos) * z.mine + (s - z.mine)


def token_ids(z, plan_ref, hist_ref, dest, bal_pos, mp_pos):
    parts = []
    for s in range(z.pair):
        slot = bal_pos * z.pair + slot_of(z, mp_pos, s)
        user = dest * z.group + member(z, plan_ref, dest, slot)
        row = hist_ref[pl.ds(user, 1), :]
        parts.append(jnp.where(mp_pos == 0, row[:, : z.half], row[:, z.half :]))
    return jnp.concatenate(parts, axis=1)


def scaled_rows(z, table_ref, scale_ref, rows_ref):
    chunk = 128

    def step(i, carry):
        start = pl.multiple_of(i * chunk, chunk)
        row = scale_ref[pl.ds(i, 1), :]
        column = jnp.broadcast_to(row, (chunk, chunk)).T
        for c in range(z.width // chunk):
            cols = slice(c * chunk, (c + 1) * chunk)
            rows_ref[pl.ds(start, chunk), cols] = (
                table_ref[pl.ds(start, chunk), cols].astype(F32) * column
            ).astype(BF)
        return carry

    lax.fori_loop(0, z.rows // chunk, step, 0)


def two_digits(values):
    row = iota((8, values.shape[1]), 0)
    high = lax.shift_right_logical(values, 7)
    low = values & 127
    return jnp.where(row == 0, high, jnp.where(row == 1, low, 0)).astype(F32).astype(BF)


def column_of(pairs):
    return (pairs[:, 0:1] * 128.0 + pairs[:, 1:2]).astype(jnp.int32)


def triangle(tokens):
    return (iota((tokens, tokens), 0) <= iota((tokens, tokens), 1)).astype(F32).astype(BF)


def send_kernel(z, plan_ref, hist_ref, table_ref, scale_ref, *refs):
    outs, rows_ref = refs[:-1], refs[-1]
    table_pos = lax.axis_index("table")
    bal_pos = lax.axis_index("bal")
    mp_pos = lax.axis_index("mp")
    scaled_rows(z, table_ref, scale_ref, rows_ref)
    tri = triangle(z.tokens)
    for k in range(1, z.n):
        dest = lax.rem(table_pos + k, z.n)
        ids = token_ids(z, plan_ref, hist_ref, dest, bal_pos, mp_pos)
        mine = lax.shift_right_logical(ids, z.shift) == table_pos
        flags = jnp.broadcast_to(mine.astype(F32), (8, z.tokens)).astype(BF)
        rank = dot(flags, tri)[0:1, :].astype(jnp.int32) - 1
        place = jnp.where(mine, rank, -1)
        compact = (iota((z.cap, z.tokens), 0) == place).astype(F32).astype(BF)
        local = column_of(dot_nt(compact, two_digits(ids & (z.rows - 1))))
        pick = (iota((z.cap, z.rows), 1) == local).astype(F32).astype(BF)
        outs[k - 1][...] = dot(pick, rows_ref[...]).astype(BF)


def keep_kernel(z, plan_ref, hist_ref, table_ref, scale_ref, own_ref, route_ref, rows_ref):
    table_pos = lax.axis_index("table")
    bal_pos = lax.axis_index("bal")
    mp_pos = lax.axis_index("mp")
    scaled_rows(z, table_ref, scale_ref, rows_ref)
    tri = triangle(z.tokens)
    ids = token_ids(z, plan_ref, hist_ref, table_pos, bal_pos, mp_pos)
    owner = lax.shift_right_logical(ids, z.shift)
    local = ids & (z.rows - 1)
    eye = (iota((z.tokens, z.tokens), 0) == iota((z.tokens, z.tokens), 1)).astype(F32).astype(BF)
    local_col = column_of(dot_nt(eye, two_digits(jnp.where(owner == table_pos, local, z.rows))))
    pick = (iota((z.tokens, z.rows), 1) == local_col).astype(F32).astype(BF)
    own_ref[...] = dot(pick, rows_ref[...]).astype(BF)
    lanes = max(8, z.n)
    offset = iota((lanes, z.tokens), 0)
    source = table_pos - offset
    source = jnp.where(source < 0, source + z.n, source)
    flags = (owner == source) & (offset >= 1) & (offset < z.n)
    rank = dot(flags.astype(F32).astype(BF), tri).astype(jnp.int32) - 1
    slots = z.n * z.cap
    slot = jnp.sum(
        jnp.where(flags, (offset - 1) * z.cap + rank + 1, 0), axis=0, keepdims=True
    )
    slot = jnp.where(slot == 0, slots, slot - 1)
    slot_col = column_of(dot_nt(eye, two_digits(slot)))
    route_ref[...] = (
        (iota((z.tokens, (z.n - 1) * z.cap), 1) == slot_col).astype(F32).astype(BF)
    )


def place_kernel(z, own_ref, route_ref, *refs):
    got, keep_ref, give_ref = refs[: z.n - 1], refs[-2], refs[-1]
    total = own_ref[...].astype(F32)
    block = max(1, 256 // z.cap)
    for k in range(0, z.n - 1, block):
        group = range(k, min(k + block, z.n - 1))
        rows = [got[g][...] for g in group]
        rows = rows[0] if len(rows) == 1 else jnp.concatenate(rows, axis=0)
        total = total + dot(route_ref[:, k * z.cap : k * z.cap + rows.shape[0]], rows)
    total = total.astype(BF)
    cut = z.tokens // z.mp
    keep_ref[...] = total[:cut]
    give_ref[...] = total[cut:]


def bias_kernel(z, small_ref, plan_ref, lens_ref, time_ref, bias_ref, *, buckets, tbuckets):
    table_pos = lax.axis_index("table")
    bal_pos = lax.axis_index("bal")
    mp_pos = lax.axis_index("mp")
    size = z.length
    number = buckets_of(size, buckets)
    lane = iota((8, size), 1)
    dist = jnp.where(lane == 0, 0, size - lane)
    position = []
    for h in range(z.heads):
        row = jnp.zeros((8, size), F32)
        for b in sorted(set(number)):
            low, high = number.index(b), size - 1 - number[::-1].index(b)
            row = jnp.where((dist >= low) & (dist <= high), small_ref[h, b], row)
        full = jnp.broadcast_to(row[0:1], (size, size))
        position.append(pltpu.roll(full, 0, 1, stride=1, stride_axis=0))
    for h in range(z.heads):
        for u in range(z.mine):
            bias_ref[u, h] = position[h]
    block = 32
    for u in range(z.mine):
        user = member(z, plan_ref, table_pos, bal_pos * z.pair + mp_pos * z.mine + u)
        size_u = lens_ref[user]
        events = time_ref[pl.ds(user, 1), :]
        columns = jnp.broadcast_to(events, (size, size)).T

        for r in range(0, size, block):
            rows = slice(r, r + block)
            diff = jnp.abs(columns[rows] - events)
            column = iota((block, size), 1)
            valid = (column <= iota((block, size), 0) + r) & (column < size_u)
            for h in range(z.heads):
                term = jnp.zeros((block, size), F32)
                for b in range(tbuckets):
                    term = jnp.where(diff == b, small_ref[h, buckets + b], term)
                bias_ref[u, h, rows, :] = jnp.where(
                    valid, 0.5 * (bias_ref[u, h, rows, :] + term), FAR
                )


def silu(s):
    half = 0.5 * s
    return half + half * jnp.tanh(half)


def arrived(ref, sem):
    pltpu.make_async_copy(ref, ref, sem).wait()


def layer_kernel(
    z, load, group, n_weights, plan_ref, lens_ref, keep_ref, got_ref, gain_ref, out_gain_ref, bias_hbm, *refs
):
    weights = refs[:n_weights]
    own_out, give_out = refs[n_weights : n_weights + 2]
    (e_ref, w_ref, o_ref, emb_ref, x_ref, xn_ref, act_ref, y_ref, z_ref, bias_ref, sems) = refs[n_weights + 2 :]
    table_pos = lax.axis_index("table")
    bal_pos = lax.axis_index("bal")
    mp_pos = lax.axis_index("mp")
    width = x_ref.shape[1]
    copies = load(weights, e_ref, w_ref, o_ref, sems)
    copies.insert(2, [pltpu.make_async_copy(bias_hbm, bias_ref, sems.at[3])])
    for batch in copies:
        for c in batch:
            c.start()
    for u in range(z.mine):
        near = pl.multiple_of(u * z.length + mp_pos * z.half, z.half)
        far = pl.multiple_of(u * z.length + (1 - mp_pos) * z.half, z.half)
        rows = slice(u * z.half, (u + 1) * z.half)
        emb_ref[pl.ds(near, z.half), :] = keep_ref[rows, :]
        emb_ref[pl.ds(far, z.half), :] = got_ref[rows, :]
    arrived(e_ref, sems.at[0])
    tokens = z.mine * z.length
    block = 256
    for r in range(0, tokens, block):
        rows = slice(r, r + block)
        x = []
        for first in range(0, 2 * width, 2 * group):
            e = [e_ref[:, first + j * group : first + (j + 1) * group] for j in range(2)]
            x.append(dot(emb_ref[rows, :], jnp.concatenate(e, axis=0)))
        x = jnp.concatenate(x, axis=1).astype(BF)
        x_ref[rows, :] = x
        x = x.astype(F32)
        mean = jnp.mean(x, axis=1, keepdims=True)
        centred = x - mean
        var = jnp.mean(centred * centred, axis=1, keepdims=True)
        xn_ref[rows, :] = (centred * lax.rsqrt(var + epsilon) * gain_ref[...]).astype(BF)
    step = 256
    arrived(w_ref, sems.at[1])
    share = w_ref.shape[1] // 4
    for part in range(4):

        def project(nb, carry):
            cols = pl.ds(pl.multiple_of(nb * step, step), step)
            w = w_ref[:, part * share : (part + 1) * share, cols].reshape(width, step)
            s = dot(xn_ref[...], w)
            act_ref[part, :, cols] = silu(s).astype(BF)
            return carry

        lax.fori_loop(0, width // step, project, 0, unroll=True)
    arrived(bias_ref, sems.at[3])
    scale = 0.5 / math.sqrt(width // z.heads)
    size = width // z.heads
    for u in range(z.mine):
        user = member(z, plan_ref, table_pos, bal_pos * z.pair + mp_pos * z.mine + u)
        inverse = 1.0 / jnp.full((1, z.length), lens_ref[user], jnp.int32).astype(F32)
        rows = slice(u * z.length, (u + 1) * z.length)

        block = z.length // ROW_BLOCKS
        total = [jnp.zeros((block, 1), F32) for _ in range(ROW_BLOCKS)]
        square = [jnp.zeros((block, 1), F32) for _ in range(ROW_BLOCKS)]
        for h in range(z.heads):
            cols = slice(h * size, (h + 1) * size)
            for part in range(ROW_BLOCKS):
                first = u * z.length + part * block
                mine = slice(first, first + block)
                keys = slice(u * z.length, first + block)
                seen = (part + 1) * block
                s = dot_nt(act_ref[2, mine, cols], act_ref[3, keys, cols]) * scale
                s = s + bias_ref[u, h, part * block : seen, :seen]
                a = ((s + s * jnp.tanh(s)) * inverse[:, :seen]).astype(BF)
                y = dot(a, act_ref[1, keys, cols])
                y_ref[mine, cols] = y
                total[part] = total[part] + jnp.sum(y, axis=1, keepdims=True)
                square[part] = square[part] + jnp.sum(y * y, axis=1, keepdims=True)
        total, square = jnp.concatenate(total, 0), jnp.concatenate(square, 0)
        mean = total / width
        var = square / width - mean * mean
        factor = lax.rsqrt(var + epsilon)
        for h in range(z.heads):
            cols = slice(h * size, (h + 1) * size)
            normed = (y_ref[rows, cols] - mean) * factor * out_gain_ref[h : h + 1, :]
            z_ref[rows, cols] = (normed * act_ref[0, rows, cols].astype(F32)).astype(BF)
    arrived(o_ref, sems.at[2])
    out_cols = width // z.mp
    for which, ref in ((1 - mp_pos, give_out), (mp_pos, own_out)):
        for nb in range(out_cols // step):
            cols = pl.ds(pl.multiple_of(which * out_cols + nb * step, step), step)
            if group <= out_cols:
                first = which * 2 * out_cols + nb * step // group * 2 * group + nb * step % group
            else:
                first = which * out_cols + nb * step
            deep = o_ref.shape[0] // z.mp
            o = []
            for core in range(z.mp):
                for j in range(2):
                    lanes = pl.ds(pl.multiple_of(first + j * group, step), step)
                    o.append(o_ref[core * deep : (core + 1) * deep, lanes])
            term = dot(z_ref[...], jnp.concatenate(o, axis=0))
            ref[:, nb * step : (nb + 1) * step] = (
                term + x_ref[:, cols].astype(F32)
            ).astype(BF)


def swap(x, axis, size, k=1):
    return lax.ppermute(x, axis, [(i, (i + k) % size) for i in range(size)])


def cross(x, near_first):
    pairs = []
    for i in range(8):
        p, b, m = i // 4, i // 2 % 2, i % 2
        p, b = (p, 1 - b) if (m == 0) == near_first else (1 - p, b)
        pairs.append((i, (p * 2 + b) * 2 + m))
    return lax.ppermute(x, ("parts", "bal", "mp"), pairs)


def corner(x):
    return lax.ppermute(x, ("parts", "bal"), [(i, 3 - i) for i in range(4)])


def pack_kernel(e_ref, w_ref, o_ref, out_ref, sems):
    q = lax.axis_index("parts") * 2 + lax.axis_index("bal")
    m = lax.axis_index("mp")
    share = w_ref.shape[1] // 4
    cols = e_ref.shape[1]
    e_part = e_ref.shape[0] // 16
    o_part = o_ref.shape[0] // 8
    copies = []

    def add(src, dst):
        copies.append(pltpu.make_async_copy(src, dst, sems))

    for c in range(4):
        add(w_ref.at[c, at(q, share), :], out_ref.at[c * share : (c + 1) * share, :])
    first = 4 * share
    for j in range(2):
        lanes = slice(j * cols, (j + 1) * cols)
        add(e_ref.at[at(j * 8 + q * 2 + m, e_part), :], out_ref.at[first : first + e_part, lanes])
        add(
            o_ref.at[at(j * 4 + q, o_part), :],
            out_ref.at[first + e_part : first + e_part + o_part, lanes],
        )
    for c in copies:
        c.start()
    for c in copies:
        c.wait()


def merge_kernel(*refs):
    out_ref, sem = refs[4:]
    copies = [pltpu.make_async_copy(refs[i], out_ref.at[i], sem) for i in range(4)]
    for c in copies:
        c.start()
    for c in copies:
        c.wait()


def at(x, size):
    return pl.ds(pl.multiple_of(x * size, size), size)


def load_pieces(z):
    def load(refs, e_ref, w_ref, o_ref, sems):
        t, m = lax.axis_index("table"), lax.axis_index("mp")
        p, b = lax.axis_index("parts"), lax.axis_index("bal")
        e_own, w_own, o_own, w_near, o_near = refs[:5]
        share, cols = w_own.shape[2], w_own.shape[3]
        e_cols = e_own.shape[1]
        o_rows = o_own.shape[0]
        e_part = e_ref.shape[0] // 8
        o_part = o_rows // 8
        first = 4 * share
        along_b, along_p = p * 2 + 1 - b, (1 - p) * 2 + b
        pieces = []
        for k in range(1, z.n):
            source = lax.rem(t + z.n - k, z.n)
            block = refs[PIECES[k - 1] : PIECES[k]]
            if len(block) == 2:
                block = [ref.at[i] for i in range(4) for ref in block]
            for i in range(4):
                for core, ref in ((m, block[2 * i]), (1 - m, block[2 * i + 1])):
                    q = (
                        p * 2 + b,
                        jnp.where(core == 0, along_b, along_p),
                        jnp.where(core == 0, along_p, along_b),
                        (1 - p) * 2 + 1 - b,
                    )[i]
                    pieces.append((ref, source, q, core))
        groups = [[] for _ in range(3)]

        def add(g, src, dst):
            groups[g].append(pltpu.make_async_copy(src, dst, sems.at[g]))

        def half(t, j):
            return at(t * 2 + j, e_cols)

        e_rows, o_deep = e_ref.shape[0], o_rows // 2
        for j in range(2):
            add(0, e_own.at[j * e_rows : (j + 1) * e_rows, :], e_ref.at[:, half(t, j)])
        for ref, source, q, core in pieces:
            rows = at(q * 2 + core, e_part)
            add(0, ref.at[first : first + e_part, :], e_ref.at[rows, at(source, 2 * e_cols)])
        for core, w in ((m, w_own), (1 - m, w_near)):
            for c in range(4):
                rows = slice(c * share, (c + 1) * share)
                add(1, w.at[c], w_ref.at[at(t, 4), rows, at(core, cols)])
        for ref, source, q, core in pieces:
            add(1, ref.at[:first, :], w_ref.at[source * 4 + q, :, at(core, cols)])
        for core, o in ((m, o_own), (1 - m, o_near)):
            for j in range(2):
                rows = slice(j * o_deep, (j + 1) * o_deep)
                add(2, o.at[rows, :], o_ref.at[at(core, o_deep), half(t, j)])
        for ref, source, q, core in pieces:
            last = first + e_part + o_part
            rows = at(core * 4 + q, o_part)
            add(2, ref.at[first + e_part : last, :], o_ref.at[rows, at(source, 2 * e_cols)])
        return groups

    return load


def load_whole(refs, e_ref, w_ref, o_ref, sems):
    e, w, o = refs
    groups = [[], [], []]

    def add(g, src, dst):
        groups[g].append(pltpu.make_async_copy(src, dst, sems.at[g]))

    width, share = w_ref.shape[2], w_ref.shape[1] // 4
    e_rows, o_deep = e_ref.shape[0], o_ref.shape[0] // 2
    for j in range(2):
        lanes = slice(j * width, (j + 1) * width)
        add(0, e.at[j * e_rows : (j + 1) * e_rows, :], e_ref.at[:, lanes])
        for core in range(2):
            rows = slice((core * 2 + j) * o_deep, (core * 2 + j + 1) * o_deep)
            add(2, o.at[rows, :], o_ref.at[core * o_deep : (core + 1) * o_deep, lanes])
    for c in range(4):
        add(1, w.at[c], w_ref.at[:, c * share : (c + 1) * share, :])
    return groups


def blocks(w, count):
    return w.reshape(w.shape[0], count, w.shape[1] // count, w.shape[2])


def finish_kernel(own_ref, got_ref, out_ref):
    mp_pos = lax.axis_index("mp")
    tokens = own_ref.shape[0]
    out_ref[at(mp_pos, tokens), :] = own_ref[...]
    out_ref[at(1 - mp_pos, tokens), :] = got_ref[...]


PIECES = (5, 7, 9, 17)


def body(
    table_rows,
    row_scale,
    hist_ids,
    lengths,
    plan,
    time_bucket,
    embed_proj,
    in_gain,
    qkvu_proj,
    out_gain,
    out_proj,
    pos_bias,
    time_bias,
):
    axes = tuple(lax.axis_size(a) for a in ("table", "bal", "mp"))
    z = Sizes(axes, table_rows, hist_ids, lengths, pos_bias)
    width = in_gain.shape[0]
    mp_pos = lax.axis_index("mp")
    scale = row_scale.reshape(z.rows // 128, 128)
    send_rows = pl.pallas_call(
        functools.partial(send_kernel, z),
        out_shape=[jax.ShapeDtypeStruct((z.cap, z.width), BF)] * (z.n - 1),
        in_specs=[sspec(), vspec(), vspec(), vspec()],
        out_specs=[vspec()] * (z.n - 1),
        scratch_shapes=[pltpu.VMEM((z.rows, z.width), BF)],
        compiler_params=params(20),
        cost_estimate=cost(7),
        name="send_rows",
    )
    keep_rows = pl.pallas_call(
        functools.partial(keep_kernel, z),
        out_shape=[
            jax.ShapeDtypeStruct((z.tokens, z.width), BF),
            jax.ShapeDtypeStruct((z.tokens, (z.n - 1) * z.cap), BF),
        ],
        in_specs=[sspec(), vspec(), vspec(), vspec()],
        out_specs=[vspec()] * 2,
        scratch_shapes=[pltpu.VMEM((z.rows, z.width), BF)],
        compiler_params=params(20),
        cost_estimate=cost(7),
        name="keep_rows",
    )
    buckets, tbuckets = pos_bias.shape[1], time_bias.shape[1]
    make_bias = pl.pallas_call(
        functools.partial(bias_kernel, z, buckets=buckets, tbuckets=tbuckets),
        out_shape=jax.ShapeDtypeStruct((z.mine, z.heads, z.length, z.length), F32),
        in_specs=[sspec(), sspec(), sspec(), vspec()],
        out_specs=vspec(),
        compiler_params=params(14),
        cost_estimate=cost(7),
        name="bias",
    )
    place_rows = pl.pallas_call(
        functools.partial(place_kernel, z),
        out_shape=[jax.ShapeDtypeStruct((z.tokens // z.mp, z.width), BF)] * 2,
        in_specs=[vspec()] * (z.n + 1),
        out_specs=[vspec()] * 2,
        compiler_params=params(12),
        cost_estimate=cost(3),
        name="place_rows",
    )

    def both(x):
        other = swap(x, "mp", z.mp)
        return jnp.where(
            mp_pos == 0, jnp.concatenate([x, other], 0), jnp.concatenate([other, x], 0)
        )

    def biases(pos_bias, time_bias, out_gain):
        small = jnp.concatenate(
            [pos_bias, time_bias, out_gain.reshape(pos_bias.shape[0], -1)], axis=1
        )
        small = both(small)
        return small[:, : buckets + tbuckets], small[:, buckets + tbuckets :]

    if z.n == 4 and z.bal == 2 and lax.axis_size("parts") == 2:
        near = functools.partial(swap, axis="mp", size=2)
        hop = functools.partial(swap, axis="table", size=z.n)
        rows = qkvu_proj.shape[1] + z.width // 16 + out_proj.shape[0] // 8
        pack = pl.pallas_call(
            pack_kernel,
            out_shape=jax.ShapeDtypeStruct((rows, qkvu_proj.shape[2]), BF),
            in_specs=[pl.BlockSpec(memory_space=pltpu.HBM)] * 3,
            out_specs=vspec(),
            scratch_shapes=[pltpu.SemaphoreType.DMA],
            compiler_params=params(60),
            name="pack",
        )(embed_proj, qkvu_proj, out_proj)
        merge = pl.pallas_call(
            merge_kernel,
            out_shape=jax.ShapeDtypeStruct((4, rows, qkvu_proj.shape[2]), BF),
            in_specs=[pl.BlockSpec(memory_space=pl.ANY)] * 4,
            out_specs=vspec(),
            scratch_shapes=[pltpu.SemaphoreType.DMA],
            compiler_params=params(6),
            cost_estimate=cost(2),
            name="merge",
        )
        r1 = hop(pack)
        sent = send_rows(plan, hist_ids, table_rows, scale)
        w_near, o_near = near(qkvu_proj), near(out_proj)
        sent, small_in = fence(sent, (pos_bias, time_bias, out_gain))
        table, gains = biases(*small_in)
        r1, sent, table, w_near, o_near = fence(r1, sent, table, w_near, o_near)
        b1, a1 = cross(r1, False), cross(r1, True)
        got1 = swap(sent[0], "table", z.n, 1)
        r2 = hop(r1)
        bias = make_bias(table, plan, lengths, time_bucket)
        r1, a1, b1, r2, got1, bias, sent, plan1, gains = fence(
            r1, a1, b1, r2, got1, bias, sent, plan, gains
        )
        b2, a2, d1 = cross(r2, False), cross(r2, True), cross(b1, True)
        got3 = swap(sent[2], "table", z.n, 3)
        r3 = hop(r2)
        own, route = keep_rows(plan1, hist_ids, table_rows, scale)
        r1, a1, b1, d1, r2, a2, b2, r3, got3, own, route, sent = fence(
            r1, a1, b1, d1, r2, a2, b2, r3, got3, own, route, sent
        )
        a3, b3, d2 = cross(r3, True), cross(r3, False), cross(b2, True)
        got2 = swap(sent[1], "table", z.n, 2)
        chunk1 = merge(r1, a1, b1, d1)
        near1 = near(chunk1)
        a3, b3, r2, a2, b2, d2, near1, got2, r3 = fence(a3, b3, r2, a2, b2, d2, near1, got2, r3)
        d3 = cross(b3, True)
        keep, give = place_rows(own, route, got1, got2, got3)
        back = near(give)
        chunk2 = merge(r2, a2, b2, d2)
        near2 = near(chunk2)
        r3n, a3n, b3n = near(r3), near(a3), near(b3)
        w_own, w_near = blocks(qkvu_proj, 4), blocks(w_near, 4)
        group = embed_proj.shape[1]
        weights = [embed_proj, w_own, out_proj, w_near, o_near, chunk1, near1, chunk2, near2]
        weights += [r3, r3n, a3, a3n, b3, b3n, d3, near(d3)]
        load = load_pieces(z)
    else:
        table, gains = biases(pos_bias, time_bias, out_gain)
        bias = make_bias(table, plan, lengths, time_bucket)
        sent = send_rows(plan, hist_ids, table_rows, scale)
        got = [swap(s, "table", z.n, k + 1) for k, s in enumerate(sent)]
        own, route = keep_rows(plan, hist_ids, table_rows, scale)
        q_full = lax.all_gather(qkvu_proj, "table", axis=1, tiled=True)
        o_full = lax.all_gather(out_proj, "table", axis=1, tiled=True)
        weights = [
            lax.all_gather(embed_proj, "table", axis=1, tiled=True),
            blocks(lax.all_gather(q_full, "mp", axis=2, tiled=True), 16),
            lax.all_gather(o_full, "mp", axis=0, tiled=True),
        ]
        load, group = load_whole, width
        keep, give = place_rows(own, route, *got)
        back = swap(give, "mp", z.mp)

    tokens = z.mine * z.length
    out_cols = width // z.mp
    out_own, out_give = pl.pallas_call(
        functools.partial(layer_kernel, z, load, group, len(weights)),
        out_shape=[jax.ShapeDtypeStruct((tokens, out_cols), BF)] * 2,
        in_specs=[sspec(), sspec()]
        + [vspec()] * 4
        + [pl.BlockSpec(memory_space=pl.ANY)] * (1 + len(weights)),
        out_specs=[vspec()] * 2,
        scratch_shapes=[
            pltpu.VMEM((z.width // 2, 2 * width), BF),
            pltpu.VMEM((16, width // 4, width), BF),
            pltpu.VMEM((width // 2, 2 * width), BF),
            pltpu.VMEM((tokens, z.width), BF),
            pltpu.VMEM((tokens, width), BF),
            pltpu.VMEM((tokens, width), BF),
            pltpu.VMEM((4, tokens, width), BF),
            pltpu.VMEM((tokens, width), F32),
            pltpu.VMEM((tokens, width), BF),
            pltpu.VMEM(bias.shape, F32),
            pltpu.SemaphoreType.DMA((4,)),
        ],
        compiler_params=params(36),
        name="layer",
    )(plan, lengths, keep, back, in_gain.reshape(1, width), gains, bias, *weights)
    out_got = swap(out_give, "mp", z.mp)
    out = pl.pallas_call(
        finish_kernel,
        out_shape=jax.ShapeDtypeStruct((z.mp * tokens, out_cols), BF),
        in_specs=[vspec()] * 2,
        out_specs=vspec(),
        compiler_params=params(8),
        name="finish",
    )(out_own, out_got)
    return out.reshape(z.pair, z.length, out_cols)


def solution(mesh):
    return jax.shard_map(
        body,
        mesh=mesh,
        in_specs=(
            P("table", None),
            P("table"),
            P("parts", None),
            P(("parts", "table")),
            P("parts"),
            P(("parts", "table"), None),
            P(None, "table"),
            P(),
            P(None, "table", "mp"),
            P("mp"),
            P("mp", "table"),
            P("mp", None),
            P("mp", None),
        ),
        out_specs=P(("parts", "table", "bal"), None, "mp"),
        check_vma=False,
    )
```

```python
import functools
import math

import jax
import jax.numpy as jnp
from jax import lax
from jax.experimental import pallas as pl
from jax.experimental.pallas import tpu as pltpu
from jax.sharding import PartitionSpec as P

epsilon = 1e-05
BF = jnp.bfloat16
F32 = jnp.float32
MIB = 1024 * 1024
FAR = -1e30
ROW_BLOCKS = 1


def buckets_of(length, buckets):
    found = []
    for d in range(length):
        b = d if d < 16 else 15 + sum(1 for power in range(4, 20) if d >= 2**power)
        found.append(min(b, buckets - 1))
    return found


def vspec():
    return pl.BlockSpec(memory_space=pltpu.VMEM)


def sspec():
    return pl.BlockSpec(memory_space=pltpu.SMEM)


def params(mib):
    return pltpu.CompilerParams(vmem_limit_bytes=mib * MIB)


def iota(shape, axis):
    return lax.broadcasted_iota(jnp.int32, shape, axis)


def dot(a, b):
    return jnp.dot(a, b, preferred_element_type=F32)


def dot_nt(a, b):
    return lax.dot_general(a, b, (((1,), (1,)), ((), ())), preferred_element_type=F32)


def cost(us):
    return pl.CostEstimate(flops=int(us * 9e8), bytes_accessed=int(us * 2e6), transcendentals=0)


def fence(*values):
    return lax.optimization_barrier(values)


class Sizes:
    def __init__(self, mesh_sizes, table_rows, hist_ids, lengths, pos_bias):
        self.n, self.bal, self.mp = mesh_sizes
        self.rows, self.width = table_rows.shape
        self.users, self.length = hist_ids.shape
        self.group = lengths.shape[0]
        self.pair = self.group // self.bal
        self.mine = self.pair // self.mp
        self.half = self.length // self.mp
        self.tokens = self.pair * self.half
        self.cap = self.pair * self.length // self.n
        self.heads = pos_bias.shape[0] * self.mp
        self.shift = self.rows.bit_length() - 1


def member(z, plan_ref, dest, slot):
    found = jnp.int32(0)
    for j in range(z.group):
        found = found + jnp.where(plan_ref[dest * z.group + j] == slot, j, 0)
    return found


def slot_of(z, mp_pos, s):
    if s < z.mine:
        return mp_pos * z.mine + s
    return (1 - mp_pos) * z.mine + (s - z.mine)


def token_ids(z, plan_ref, hist_ref, dest, bal_pos, mp_pos):
    parts = []
    for s in range(z.pair):
        slot = bal_pos * z.pair + slot_of(z, mp_pos, s)
        user = dest * z.group + member(z, plan_ref, dest, slot)
        row = hist_ref[pl.ds(user, 1), :]
        parts.append(jnp.where(mp_pos == 0, row[:, : z.half], row[:, z.half :]))
    return jnp.concatenate(parts, axis=1)


def scaled_rows(z, table_ref, scale_ref, rows_ref):
    chunk = 128

    def step(i, carry):
        start = pl.multiple_of(i * chunk, chunk)
        row = scale_ref[pl.ds(i, 1), :]
        column = jnp.broadcast_to(row, (chunk, chunk)).T
        for c in range(z.width // chunk):
            cols = slice(c * chunk, (c + 1) * chunk)
            rows_ref[pl.ds(start, chunk), cols] = (
                table_ref[pl.ds(start, chunk), cols].astype(F32) * column
            ).astype(BF)
        return carry

    lax.fori_loop(0, z.rows // chunk, step, 0)


def two_digits(values):
    row = iota((8, values.shape[1]), 0)
    high = lax.shift_right_logical(values, 7)
    low = values & 127
    return jnp.where(row == 0, high, jnp.where(row == 1, low, 0)).astype(F32).astype(BF)


def column_of(pairs):
    return (pairs[:, 0:1] * 128.0 + pairs[:, 1:2]).astype(jnp.int32)


def triangle(tokens):
    return (iota((tokens, tokens), 0) <= iota((tokens, tokens), 1)).astype(F32).astype(BF)


def send_kernel(z, plan_ref, hist_ref, table_ref, scale_ref, *refs):
    outs, rows_ref = refs[:-1], refs[-1]
    table_pos = lax.axis_index("table")
    bal_pos = lax.axis_index("bal")
    mp_pos = lax.axis_index("mp")
    scaled_rows(z, table_ref, scale_ref, rows_ref)
    tri = triangle(z.tokens)
    for k in range(1, z.n):
        dest = lax.rem(table_pos + k, z.n)
        ids = token_ids(z, plan_ref, hist_ref, dest, bal_pos, mp_pos)
        mine = lax.shift_right_logical(ids, z.shift) == table_pos
        flags = jnp.broadcast_to(mine.astype(F32), (8, z.tokens)).astype(BF)
        rank = dot(flags, tri)[0:1, :].astype(jnp.int32) - 1
        place = jnp.where(mine, rank, -1)
        compact = (iota((z.cap, z.tokens), 0) == place).astype(F32).astype(BF)
        local = column_of(dot_nt(compact, two_digits(ids & (z.rows - 1))))
        pick = (iota((z.cap, z.rows), 1) == local).astype(F32).astype(BF)
        outs[k - 1][...] = dot(pick, rows_ref[...]).astype(BF)


def keep_kernel(z, plan_ref, hist_ref, table_ref, scale_ref, own_ref, route_ref, rows_ref):
    table_pos = lax.axis_index("table")
    bal_pos = lax.axis_index("bal")
    mp_pos = lax.axis_index("mp")
    scaled_rows(z, table_ref, scale_ref, rows_ref)
    tri = triangle(z.tokens)
    ids = token_ids(z, plan_ref, hist_ref, table_pos, bal_pos, mp_pos)
    owner = lax.shift_right_logical(ids, z.shift)
    local = ids & (z.rows - 1)
    eye = (iota((z.tokens, z.tokens), 0) == iota((z.tokens, z.tokens), 1)).astype(F32).astype(BF)
    local_col = column_of(dot_nt(eye, two_digits(jnp.where(owner == table_pos, local, z.rows))))
    pick = (iota((z.tokens, z.rows), 1) == local_col).astype(F32).astype(BF)
    own_ref[...] = dot(pick, rows_ref[...]).astype(BF)
    lanes = max(8, z.n)
    offset = iota((lanes, z.tokens), 0)
    source = table_pos - offset
    source = jnp.where(source < 0, source + z.n, source)
    flags = (owner == source) & (offset >= 1) & (offset < z.n)
    rank = dot(flags.astype(F32).astype(BF), tri).astype(jnp.int32) - 1
    slots = z.n * z.cap
    slot = jnp.sum(
        jnp.where(flags, (offset - 1) * z.cap + rank + 1, 0), axis=0, keepdims=True
    )
    slot = jnp.where(slot == 0, slots, slot - 1)
    slot_col = column_of(dot_nt(eye, two_digits(slot)))
    route_ref[...] = (
        (iota((z.tokens, (z.n - 1) * z.cap), 1) == slot_col).astype(F32).astype(BF)
    )


def place_kernel(z, own_ref, route_ref, *refs):
    got, keep_ref, give_ref = refs[: z.n - 1], refs[-2], refs[-1]
    total = own_ref[...].astype(F32)
    block = max(1, 256 // z.cap)
    for k in range(0, z.n - 1, block):
        group = range(k, min(k + block, z.n - 1))
        rows = [got[g][...] for g in group]
        rows = rows[0] if len(rows) == 1 else jnp.concatenate(rows, axis=0)
        total = total + dot(route_ref[:, k * z.cap : k * z.cap + rows.shape[0]], rows)
    total = total.astype(BF)
    cut = z.tokens // z.mp
    keep_ref[...] = total[:cut]
    give_ref[...] = total[cut:]


def bias_kernel(z, small_ref, plan_ref, lens_ref, time_ref, bias_ref, *, buckets, tbuckets):
    table_pos = lax.axis_index("table")
    bal_pos = lax.axis_index("bal")
    mp_pos = lax.axis_index("mp")
    size = z.length
    number = buckets_of(size, buckets)
    lane = iota((8, size), 1)
    dist = jnp.where(lane == 0, 0, size - lane)
    position = []
    for h in range(z.heads):
        row = jnp.zeros((8, size), F32)
        for b in sorted(set(number)):
            low, high = number.index(b), size - 1 - number[::-1].index(b)
            row = jnp.where((dist >= low) & (dist <= high), small_ref[h, b], row)
        full = jnp.broadcast_to(row[0:1], (size, size))
        position.append(pltpu.roll(full, 0, 1, stride=1, stride_axis=0))
    for h in range(z.heads):
        for u in range(z.mine):
            bias_ref[u, h] = position[h]
    block = 32
    for u in range(z.mine):
        user = member(z, plan_ref, table_pos, bal_pos * z.pair + mp_pos * z.mine + u)
        size_u = lens_ref[user]
        events = time_ref[pl.ds(user, 1), :]
        columns = jnp.broadcast_to(events, (size, size)).T

        for r in range(0, size, block):
            rows = slice(r, r + block)
            diff = jnp.abs(columns[rows] - events)
            column = iota((block, size), 1)
            valid = (column <= iota((block, size), 0) + r) & (column < size_u)
            for h in range(z.heads):
                term = jnp.zeros((block, size), F32)
                for b in range(tbuckets):
                    term = jnp.where(diff == b, small_ref[h, buckets + b], term)
                bias_ref[u, h, rows, :] = jnp.where(
                    valid, 0.5 * (bias_ref[u, h, rows, :] + term), FAR
                )


def silu(s):
    half = 0.5 * s
    return half + half * jnp.tanh(half)


def arrived(ref, sem):
    pltpu.make_async_copy(ref, ref, sem).wait()


def layer_kernel(
    z, load, group, n_weights, plan_ref, lens_ref, keep_ref, got_ref, gain_ref, out_gain_ref, bias_hbm, *refs
):
    weights = refs[:n_weights]
    own_out, give_out = refs[n_weights : n_weights + 2]
    (e_ref, w_ref, o_ref, emb_ref, x_ref, xn_ref, act_ref, y_ref, z_ref, bias_ref, sems) = refs[n_weights + 2 :]
    table_pos = lax.axis_index("table")
    bal_pos = lax.axis_index("bal")
    mp_pos = lax.axis_index("mp")
    width = x_ref.shape[1]
    copies = load(weights, e_ref, w_ref, o_ref, sems)
    copies.insert(2, [pltpu.make_async_copy(bias_hbm, bias_ref, sems.at[3])])
    for batch in copies:
        for c in batch:
            c.start()
    for u in range(z.mine):
        near = pl.multiple_of(u * z.length + mp_pos * z.half, z.half)
        far = pl.multiple_of(u * z.length + (1 - mp_pos) * z.half, z.half)
        rows = slice(u * z.half, (u + 1) * z.half)
        emb_ref[pl.ds(near, z.half), :] = keep_ref[rows, :]
        emb_ref[pl.ds(far, z.half), :] = got_ref[rows, :]
    arrived(e_ref, sems.at[0])
    tokens = z.mine * z.length
    block = 256
    for r in range(0, tokens, block):
        rows = slice(r, r + block)
        x = []
        for first in range(0, 2 * width, 2 * group):
            e = [e_ref[:, first + j * group : first + (j + 1) * group] for j in range(2)]
            x.append(dot(emb_ref[rows, :], jnp.concatenate(e, axis=0)))
        x = jnp.concatenate(x, axis=1).astype(BF)
        x_ref[rows, :] = x
        x = x.astype(F32)
        mean = jnp.mean(x, axis=1, keepdims=True)
        centred = x - mean
        var = jnp.mean(centred * centred, axis=1, keepdims=True)
        xn_ref[rows, :] = (centred * lax.rsqrt(var + epsilon) * gain_ref[...]).astype(BF)
    step = 256
    arrived(w_ref, sems.at[1])
    share = w_ref.shape[1] // 4
    for part in range(4):

        def project(nb, carry):
            cols = pl.ds(pl.multiple_of(nb * step, step), step)
            w = w_ref[:, part * share : (part + 1) * share, cols].reshape(width, step)
            s = dot(xn_ref[...], w)
            act_ref[part, :, cols] = silu(s).astype(BF)
            return carry

        lax.fori_loop(0, width // step, project, 0, unroll=True)
    arrived(bias_ref, sems.at[3])
    scale = 0.5 / math.sqrt(width // z.heads)
    size = width // z.heads
    for u in range(z.mine):
        user = member(z, plan_ref, table_pos, bal_pos * z.pair + mp_pos * z.mine + u)
        inverse = 1.0 / jnp.full((1, z.length), lens_ref[user], jnp.int32).astype(F32)
        rows = slice(u * z.length, (u + 1) * z.length)

        block = z.length // ROW_BLOCKS
        total = [jnp.zeros((block, 1), F32) for _ in range(ROW_BLOCKS)]
        square = [jnp.zeros((block, 1), F32) for _ in range(ROW_BLOCKS)]
        for h in range(z.heads):
            cols = slice(h * size, (h + 1) * size)
            for part in range(ROW_BLOCKS):
                first = u * z.length + part * block
                mine = slice(first, first + block)
                keys = slice(u * z.length, first + block)
                seen = (part + 1) * block
                s = dot_nt(act_ref[2, mine, cols], act_ref[3, keys, cols]) * scale
                s = s + bias_ref[u, h, part * block : seen, :seen]
                a = ((s + s * jnp.tanh(s)) * inverse[:, :seen]).astype(BF)
                y = dot(a, act_ref[1, keys, cols])
                y_ref[mine, cols] = y
                total[part] = total[part] + jnp.sum(y, axis=1, keepdims=True)
                square[part] = square[part] + jnp.sum(y * y, axis=1, keepdims=True)
        total, square = jnp.concatenate(total, 0), jnp.concatenate(square, 0)
        mean = total / width
        var = square / width - mean * mean
        factor = lax.rsqrt(var + epsilon)
        for h in range(z.heads):
            cols = slice(h * size, (h + 1) * size)
            normed = (y_ref[rows, cols] - mean) * factor * out_gain_ref[h : h + 1, :]
            z_ref[rows, cols] = (normed * act_ref[0, rows, cols].astype(F32)).astype(BF)
    arrived(o_ref, sems.at[2])
    out_cols = width // z.mp
    for which, ref in ((1 - mp_pos, give_out), (mp_pos, own_out)):
        for nb in range(out_cols // step):
            cols = pl.ds(pl.multiple_of(which * out_cols + nb * step, step), step)
            if group <= out_cols:
                first = which * 2 * out_cols + nb * step // group * 2 * group + nb * step % group
            else:
                first = which * out_cols + nb * step
            deep = o_ref.shape[0] // z.mp
            o = []
            for core in range(z.mp):
                for j in range(2):
                    lanes = pl.ds(pl.multiple_of(first + j * group, step), step)
                    o.append(o_ref[core * deep : (core + 1) * deep, lanes])
            term = dot(z_ref[...], jnp.concatenate(o, axis=0))
            ref[:, nb * step : (nb + 1) * step] = (
                term + x_ref[:, cols].astype(F32)
            ).astype(BF)


def swap(x, axis, size, k=1):
    return lax.ppermute(x, axis, [(i, (i + k) % size) for i in range(size)])


def cross(x, near_first):
    pairs = []
    for i in range(8):
        p, b, m = i // 4, i // 2 % 2, i % 2
        p, b = (p, 1 - b) if (m == 0) == near_first else (1 - p, b)
        pairs.append((i, (p * 2 + b) * 2 + m))
    return lax.ppermute(x, ("parts", "bal", "mp"), pairs)


def corner(x):
    return lax.ppermute(x, ("parts", "bal"), [(i, 3 - i) for i in range(4)])


def pack_kernel(e_ref, w_ref, o_ref, out_ref, sems):
    q = lax.axis_index("parts") * 2 + lax.axis_index("bal")
    m = lax.axis_index("mp")
    share = w_ref.shape[1] // 4
    cols = e_ref.shape[1]
    e_part = e_ref.shape[0] // 16
    o_part = o_ref.shape[0] // 8
    copies = []

    def add(src, dst):
        copies.append(pltpu.make_async_copy(src, dst, sems))

    for c in range(4):
        add(w_ref.at[c, at(q, share), :], out_ref.at[c * share : (c + 1) * share, :])
    first = 4 * share
    for j in range(2):
        lanes = slice(j * cols, (j + 1) * cols)
        add(e_ref.at[at(j * 8 + q * 2 + m, e_part), :], out_ref.at[first : first + e_part, lanes])
        add(
            o_ref.at[at(j * 4 + q, o_part), :],
            out_ref.at[first + e_part : first + e_part + o_part, lanes],
        )
    for c in copies:
        c.start()
    for c in copies:
        c.wait()


def merge_kernel(*refs):
    out_ref, sem = refs[4:]
    copies = [pltpu.make_async_copy(refs[i], out_ref.at[i], sem) for i in range(4)]
    for c in copies:
        c.start()
    for c in copies:
        c.wait()


def at(x, size):
    return pl.ds(pl.multiple_of(x * size, size), size)


def load_pieces(z):
    def load(refs, e_ref, w_ref, o_ref, sems):
        t, m = lax.axis_index("table"), lax.axis_index("mp")
        p, b = lax.axis_index("parts"), lax.axis_index("bal")
        e_own, w_own, o_own, w_near, o_near = refs[:5]
        share, cols = w_own.shape[2], w_own.shape[3]
        e_cols = e_own.shape[1]
        o_rows = o_own.shape[0]
        e_part = e_ref.shape[0] // 8
        o_part = o_rows // 8
        first = 4 * share
        along_b, along_p = p * 2 + 1 - b, (1 - p) * 2 + b
        pieces = []
        for k in range(1, z.n):
            source = lax.rem(t + z.n - k, z.n)
            block = refs[PIECES[k - 1] : PIECES[k]]
            if len(block) == 2:
                block = [ref.at[i] for i in range(4) for ref in block]
            for i in range(4):
                for core, ref in ((m, block[2 * i]), (1 - m, block[2 * i + 1])):
                    q = (
                        p * 2 + b,
                        jnp.where(core == 0, along_b, along_p),
                        jnp.where(core == 0, along_p, along_b),
                        (1 - p) * 2 + 1 - b,
                    )[i]
                    pieces.append((ref, source, q, core))
        groups = [[] for _ in range(3)]

        def add(g, src, dst):
            groups[g].append(pltpu.make_async_copy(src, dst, sems.at[g]))

        def half(t, j):
            return at(t * 2 + j, e_cols)

        e_rows, o_deep = e_ref.shape[0], o_rows // 2
        for j in range(2):
            add(0, e_own.at[j * e_rows : (j + 1) * e_rows, :], e_ref.at[:, half(t, j)])
        for ref, source, q, core in pieces:
            rows = at(q * 2 + core, e_part)
            add(0, ref.at[first : first + e_part, :], e_ref.at[rows, at(source, 2 * e_cols)])
        for core, w in ((m, w_own), (1 - m, w_near)):
            for c in range(4):
                rows = slice(c * share, (c + 1) * share)
                add(1, w.at[c], w_ref.at[at(t, 4), rows, at(core, cols)])
        for ref, source, q, core in pieces:
            add(1, ref.at[:first, :], w_ref.at[source * 4 + q, :, at(core, cols)])
        for core, o in ((m, o_own), (1 - m, o_near)):
            for j in range(2):
                rows = slice(j * o_deep, (j + 1) * o_deep)
                add(2, o.at[rows, :], o_ref.at[at(core, o_deep), half(t, j)])
        for ref, source, q, core in pieces:
            last = first + e_part + o_part
            rows = at(core * 4 + q, o_part)
            add(2, ref.at[first + e_part : last, :], o_ref.at[rows, at(source, 2 * e_cols)])
        return groups

    return load


def load_whole(refs, e_ref, w_ref, o_ref, sems):
    e, w, o = refs
    groups = [[], [], []]

    def add(g, src, dst):
        groups[g].append(pltpu.make_async_copy(src, dst, sems.at[g]))

    width, share = w_ref.shape[2], w_ref.shape[1] // 4
    e_rows, o_deep = e_ref.shape[0], o_ref.shape[0] // 2
    for j in range(2):
        lanes = slice(j * width, (j + 1) * width)
        add(0, e.at[j * e_rows : (j + 1) * e_rows, :], e_ref.at[:, lanes])
        for core in range(2):
            rows = slice((core * 2 + j) * o_deep, (core * 2 + j + 1) * o_deep)
            add(2, o.at[rows, :], o_ref.at[core * o_deep : (core + 1) * o_deep, lanes])
    for c in range(4):
        add(1, w.at[c], w_ref.at[:, c * share : (c + 1) * share, :])
    return groups


def blocks(w, count):
    return w.reshape(w.shape[0], count, w.shape[1] // count, w.shape[2])


def finish_kernel(own_ref, got_ref, out_ref):
    mp_pos = lax.axis_index("mp")
    tokens = own_ref.shape[0]
    out_ref[at(mp_pos, tokens), :] = own_ref[...]
    out_ref[at(1 - mp_pos, tokens), :] = got_ref[...]


PIECES = (5, 7, 9, 17)


def body(
    table_rows,
    row_scale,
    hist_ids,
    lengths,
    plan,
    time_bucket,
    embed_proj,
    in_gain,
    qkvu_proj,
    out_gain,
    out_proj,
    pos_bias,
    time_bias,
):
    axes = tuple(lax.axis_size(a) for a in ("table", "bal", "mp"))
    z = Sizes(axes, table_rows, hist_ids, lengths, pos_bias)
    width = in_gain.shape[0]
    mp_pos = lax.axis_index("mp")
    scale = row_scale.reshape(z.rows // 128, 128)
    send_rows = pl.pallas_call(
        functools.partial(send_kernel, z),
        out_shape=[jax.ShapeDtypeStruct((z.cap, z.width), BF)] * (z.n - 1),
        in_specs=[sspec(), vspec(), vspec(), vspec()],
        out_specs=[vspec()] * (z.n - 1),
        scratch_shapes=[pltpu.VMEM((z.rows, z.width), BF)],
        compiler_params=params(20),
        cost_estimate=cost(7),
        name="send_rows",
    )
    keep_rows = pl.pallas_call(
        functools.partial(keep_kernel, z),
        out_shape=[
            jax.ShapeDtypeStruct((z.tokens, z.width), BF),
            jax.ShapeDtypeStruct((z.tokens, (z.n - 1) * z.cap), BF),
        ],
        in_specs=[sspec(), vspec(), vspec(), vspec()],
        out_specs=[vspec()] * 2,
        scratch_shapes=[pltpu.VMEM((z.rows, z.width), BF)],
        compiler_params=params(20),
        cost_estimate=cost(7),
        name="keep_rows",
    )
    buckets, tbuckets = pos_bias.shape[1], time_bias.shape[1]
    make_bias = pl.pallas_call(
        functools.partial(bias_kernel, z, buckets=buckets, tbuckets=tbuckets),
        out_shape=jax.ShapeDtypeStruct((z.mine, z.heads, z.length, z.length), F32),
        in_specs=[sspec(), sspec(), sspec(), vspec()],
        out_specs=vspec(),
        compiler_params=params(14),
        cost_estimate=cost(7),
        name="bias",
    )
    place_rows = pl.pallas_call(
        functools.partial(place_kernel, z),
        out_shape=[jax.ShapeDtypeStruct((z.tokens // z.mp, z.width), BF)] * 2,
        in_specs=[vspec()] * (z.n + 1),
        out_specs=[vspec()] * 2,
        compiler_params=params(12),
        cost_estimate=cost(3),
        name="place_rows",
    )

    def both(x):
        other = swap(x, "mp", z.mp)
        return jnp.where(
            mp_pos == 0, jnp.concatenate([x, other], 0), jnp.concatenate([other, x], 0)
        )

    def biases(pos_bias, time_bias, out_gain):
        small = jnp.concatenate(
            [pos_bias, time_bias, out_gain.reshape(pos_bias.shape[0], -1)], axis=1
        )
        small = both(small)
        return small[:, : buckets + tbuckets], small[:, buckets + tbuckets :]

    if z.n == 4 and z.bal == 2 and lax.axis_size("parts") == 2:
        near = functools.partial(swap, axis="mp", size=2)
        hop = functools.partial(swap, axis="table", size=z.n)
        rows = qkvu_proj.shape[1] + z.width // 16 + out_proj.shape[0] // 8
        pack = pl.pallas_call(
            pack_kernel,
            out_shape=jax.ShapeDtypeStruct((rows, qkvu_proj.shape[2]), BF),
            in_specs=[pl.BlockSpec(memory_space=pltpu.HBM)] * 3,
            out_specs=vspec(),
            scratch_shapes=[pltpu.SemaphoreType.DMA],
            compiler_params=params(60),
            name="pack",
        )(embed_proj, qkvu_proj, out_proj)
        merge = pl.pallas_call(
            merge_kernel,
            out_shape=jax.ShapeDtypeStruct((4, rows, qkvu_proj.shape[2]), BF),
            in_specs=[pl.BlockSpec(memory_space=pl.ANY)] * 4,
            out_specs=vspec(),
            scratch_shapes=[pltpu.SemaphoreType.DMA],
            compiler_params=params(6),
            cost_estimate=cost(2),
            name="merge",
        )
        r1 = hop(pack)
        sent = send_rows(plan, hist_ids, table_rows, scale)
        w_near, o_near = near(qkvu_proj), near(out_proj)
        sent, small_in = fence(sent, (pos_bias, time_bias, out_gain))
        table, gains = biases(*small_in)
        r1, sent, table, w_near, o_near = fence(r1, sent, table, w_near, o_near)
        b1, a1 = cross(r1, False), cross(r1, True)
        got1 = swap(sent[0], "table", z.n, 1)
        r2 = hop(r1)
        bias = make_bias(table, plan, lengths, time_bucket)
        r1, a1, b1, r2, got1, bias, sent, plan1, gains = fence(
            r1, a1, b1, r2, got1, bias, sent, plan, gains
        )
        b2, a2, d1 = cross(r2, False), cross(r2, True), cross(b1, True)
        got3 = swap(sent[2], "table", z.n, 3)
        r3 = hop(r2)
        own, route = keep_rows(plan1, hist_ids, table_rows, scale)
        r1, a1, b1, d1, r2, a2, b2, r3, got3, own, route, sent = fence(
            r1, a1, b1, d1, r2, a2, b2, r3, got3, own, route, sent
        )
        a3, b3, d2 = cross(r3, True), cross(r3, False), cross(b2, True)
        got2 = swap(sent[1], "table", z.n, 2)
        chunk1 = merge(r1, a1, b1, d1)
        a3, b3, r2, a2, b2, d2, chunk1, got2, r3 = fence(a3, b3, r2, a2, b2, d2, chunk1, got2, r3)
        near1 = near(chunk1)
        d3 = cross(b3, True)
        keep, give = place_rows(own, route, got1, got2, got3)
        back = near(give)
        chunk2 = merge(r2, a2, b2, d2)
        near2 = near(chunk2)
        r3n, a3n, b3n = near(r3), near(a3), near(b3)
        w_own, w_near = blocks(qkvu_proj, 4), blocks(w_near, 4)
        group = embed_proj.shape[1]
        weights = [embed_proj, w_own, out_proj, w_near, o_near, chunk1, near1, chunk2, near2]
        weights += [r3, r3n, a3, a3n, b3, b3n, d3, near(d3)]
        load = load_pieces(z)
    else:
        table, gains = biases(pos_bias, time_bias, out_gain)
        bias = make_bias(table, plan, lengths, time_bucket)
        sent = send_rows(plan, hist_ids, table_rows, scale)
        got = [swap(s, "table", z.n, k + 1) for k, s in enumerate(sent)]
        own, route = keep_rows(plan, hist_ids, table_rows, scale)
        q_full = lax.all_gather(qkvu_proj, "table", axis=1, tiled=True)
        o_full = lax.all_gather(out_proj, "table", axis=1, tiled=True)
        weights = [
            lax.all_gather(embed_proj, "table", axis=1, tiled=True),
            blocks(lax.all_gather(q_full, "mp", axis=2, tiled=True), 16),
            lax.all_gather(o_full, "mp", axis=0, tiled=True),
        ]
        load, group = load_whole, width
        keep, give = place_rows(own, route, *got)
        back = swap(give, "mp", z.mp)

    tokens = z.mine * z.length
    out_cols = width // z.mp
    out_own, out_give = pl.pallas_call(
        functools.partial(layer_kernel, z, load, group, len(weights)),
        out_shape=[jax.ShapeDtypeStruct((tokens, out_cols), BF)] * 2,
        in_specs=[sspec(), sspec()]
        + [vspec()] * 4
        + [pl.BlockSpec(memory_space=pl.ANY)] * (1 + len(weights)),
        out_specs=[vspec()] * 2,
        scratch_shapes=[
            pltpu.VMEM((z.width // 2, 2 * width), BF),
            pltpu.VMEM((16, width // 4, width), BF),
            pltpu.VMEM((width // 2, 2 * width), BF),
            pltpu.VMEM((tokens, z.width), BF),
            pltpu.VMEM((tokens, width), BF),
            pltpu.VMEM((tokens, width), BF),
            pltpu.VMEM((4, tokens, width), BF),
            pltpu.VMEM((tokens, width), F32),
            pltpu.VMEM((tokens, width), BF),
            pltpu.VMEM(bias.shape, F32),
            pltpu.SemaphoreType.DMA((4,)),
        ],
        compiler_params=params(36),
        name="layer",
    )(plan, lengths, keep, back, in_gain.reshape(1, width), gains, bias, *weights)
    out_got = swap(out_give, "mp", z.mp)
    out = pl.pallas_call(
        finish_kernel,
        out_shape=jax.ShapeDtypeStruct((z.mp * tokens, out_cols), BF),
        in_specs=[vspec()] * 2,
        out_specs=vspec(),
        compiler_params=params(8),
        name="finish",
    )(out_own, out_got)
    return out.reshape(z.pair, z.length, out_cols)


def solution(mesh):
    return jax.shard_map(
        body,
        mesh=mesh,
        in_specs=(
            P("table", None),
            P("table"),
            P("parts", None),
            P(("parts", "table")),
            P("parts"),
            P(("parts", "table"), None),
            P(None, "table"),
            P(),
            P(None, "table", "mp"),
            P("mp"),
            P("mp", "table"),
            P("mp", None),
            P("mp", None),
        ),
        out_specs=P(("parts", "table", "bal"), None, "mp"),
        check_vma=False,
    )
```

```python
import functools
import math

import jax
import jax.numpy as jnp
from jax import lax
from jax.experimental import pallas as pl
from jax.experimental.pallas import tpu as pltpu
from jax.sharding import PartitionSpec as P

epsilon = 1e-05
BF = jnp.bfloat16
F32 = jnp.float32
MIB = 1024 * 1024
FAR = -1e30
ROW_BLOCKS = 1


def buckets_of(length, buckets):
    found = []
    for d in range(length):
        b = d if d < 16 else 15 + sum(1 for power in range(4, 20) if d >= 2**power)
        found.append(min(b, buckets - 1))
    return found


def vspec():
    return pl.BlockSpec(memory_space=pltpu.VMEM)


def sspec():
    return pl.BlockSpec(memory_space=pltpu.SMEM)


def params(mib):
    return pltpu.CompilerParams(vmem_limit_bytes=mib * MIB)


def iota(shape, axis):
    return lax.broadcasted_iota(jnp.int32, shape, axis)


def dot(a, b):
    return jnp.dot(a, b, preferred_element_type=F32)


def dot_nt(a, b):
    return lax.dot_general(a, b, (((1,), (1,)), ((), ())), preferred_element_type=F32)


def cost(us):
    return pl.CostEstimate(flops=int(us * 9e8), bytes_accessed=int(us * 2e6), transcendentals=0)


def fence(*values):
    return lax.optimization_barrier(values)


class Sizes:
    def __init__(self, mesh_sizes, table_rows, hist_ids, lengths, pos_bias):
        self.n, self.bal, self.mp = mesh_sizes
        self.rows, self.width = table_rows.shape
        self.users, self.length = hist_ids.shape
        self.group = lengths.shape[0]
        self.pair = self.group // self.bal
        self.mine = self.pair // self.mp
        self.half = self.length // self.mp
        self.tokens = self.pair * self.half
        self.cap = self.pair * self.length // self.n
        self.heads = pos_bias.shape[0] * self.mp
        self.shift = self.rows.bit_length() - 1


def member(z, plan_ref, dest, slot):
    found = jnp.int32(0)
    for j in range(z.group):
        found = found + jnp.where(plan_ref[dest * z.group + j] == slot, j, 0)
    return found


def slot_of(z, mp_pos, s):
    if s < z.mine:
        return mp_pos * z.mine + s
    return (1 - mp_pos) * z.mine + (s - z.mine)


def token_ids(z, plan_ref, hist_ref, dest, bal_pos, mp_pos):
    parts = []
    for s in range(z.pair):
        slot = bal_pos * z.pair + slot_of(z, mp_pos, s)
        user = dest * z.group + member(z, plan_ref, dest, slot)
        row = hist_ref[pl.ds(user, 1), :]
        parts.append(jnp.where(mp_pos == 0, row[:, : z.half], row[:, z.half :]))
    return jnp.concatenate(parts, axis=1)


def scaled_rows(z, table_ref, scale_ref, rows_ref):
    chunk = 128

    def step(i, carry):
        start = pl.multiple_of(i * chunk, chunk)
        row = scale_ref[pl.ds(i, 1), :]
        column = jnp.broadcast_to(row, (chunk, chunk)).T
        for c in range(z.width // chunk):
            cols = slice(c * chunk, (c + 1) * chunk)
            rows_ref[pl.ds(start, chunk), cols] = (
                table_ref[pl.ds(start, chunk), cols].astype(F32) * column
            ).astype(BF)
        return carry

    lax.fori_loop(0, z.rows // chunk, step, 0)


def two_digits(values):
    row = iota((8, values.shape[1]), 0)
    high = lax.shift_right_logical(values, 7)
    low = values & 127
    return jnp.where(row == 0, high, jnp.where(row == 1, low, 0)).astype(F32).astype(BF)


def column_of(pairs):
    return (pairs[:, 0:1] * 128.0 + pairs[:, 1:2]).astype(jnp.int32)


def triangle(tokens):
    return (iota((tokens, tokens), 0) <= iota((tokens, tokens), 1)).astype(F32).astype(BF)


def send_kernel(z, plan_ref, hist_ref, table_ref, scale_ref, *refs):
    outs, rows_ref = refs[:-1], refs[-1]
    table_pos = lax.axis_index("table")
    bal_pos = lax.axis_index("bal")
    mp_pos = lax.axis_index("mp")
    scaled_rows(z, table_ref, scale_ref, rows_ref)
    tri = triangle(z.tokens)
    for k in range(1, z.n):
        dest = lax.rem(table_pos + k, z.n)
        ids = token_ids(z, plan_ref, hist_ref, dest, bal_pos, mp_pos)
        mine = lax.shift_right_logical(ids, z.shift) == table_pos
        flags = jnp.broadcast_to(mine.astype(F32), (8, z.tokens)).astype(BF)
        rank = dot(flags, tri)[0:1, :].astype(jnp.int32) - 1
        place = jnp.where(mine, rank, -1)
        compact = (iota((z.cap, z.tokens), 0) == place).astype(F32).astype(BF)
        local = column_of(dot_nt(compact, two_digits(ids & (z.rows - 1))))
        pick = (iota((z.cap, z.rows), 1) == local).astype(F32).astype(BF)
        outs[k - 1][...] = dot(pick, rows_ref[...]).astype(BF)


def keep_kernel(z, plan_ref, hist_ref, table_ref, scale_ref, own_ref, route_ref, rows_ref):
    table_pos = lax.axis_index("table")
    bal_pos = lax.axis_index("bal")
    mp_pos = lax.axis_index("mp")
    scaled_rows(z, table_ref, scale_ref, rows_ref)
    tri = triangle(z.tokens)
    ids = token_ids(z, plan_ref, hist_ref, table_pos, bal_pos, mp_pos)
    owner = lax.shift_right_logical(ids, z.shift)
    local = ids & (z.rows - 1)
    eye = (iota((z.tokens, z.tokens), 0) == iota((z.tokens, z.tokens), 1)).astype(F32).astype(BF)
    local_col = column_of(dot_nt(eye, two_digits(jnp.where(owner == table_pos, local, z.rows))))
    pick = (iota((z.tokens, z.rows), 1) == local_col).astype(F32).astype(BF)
    own_ref[...] = dot(pick, rows_ref[...]).astype(BF)
    lanes = max(8, z.n)
    offset = iota((lanes, z.tokens), 0)
    source = table_pos - offset
    source = jnp.where(source < 0, source + z.n, source)
    flags = (owner == source) & (offset >= 1) & (offset < z.n)
    rank = dot(flags.astype(F32).astype(BF), tri).astype(jnp.int32) - 1
    slots = z.n * z.cap
    slot = jnp.sum(
        jnp.where(flags, (offset - 1) * z.cap + rank + 1, 0), axis=0, keepdims=True
    )
    slot = jnp.where(slot == 0, slots, slot - 1)
    slot_col = column_of(dot_nt(eye, two_digits(slot)))
    route_ref[...] = (
        (iota((z.tokens, (z.n - 1) * z.cap), 1) == slot_col).astype(F32).astype(BF)
    )


def place_kernel(z, own_ref, route_ref, *refs):
    got, keep_ref, give_ref = refs[: z.n - 1], refs[-2], refs[-1]
    total = own_ref[...].astype(F32)
    block = max(1, 256 // z.cap)
    for k in range(0, z.n - 1, block):
        group = range(k, min(k + block, z.n - 1))
        rows = [got[g][...] for g in group]
        rows = rows[0] if len(rows) == 1 else jnp.concatenate(rows, axis=0)
        total = total + dot(route_ref[:, k * z.cap : k * z.cap + rows.shape[0]], rows)
    total = total.astype(BF)
    cut = z.tokens // z.mp
    keep_ref[...] = total[:cut]
    give_ref[...] = total[cut:]


def bias_kernel(z, small_ref, plan_ref, lens_ref, time_ref, bias_ref, *, buckets, tbuckets):
    table_pos = lax.axis_index("table")
    bal_pos = lax.axis_index("bal")
    mp_pos = lax.axis_index("mp")
    size = z.length
    number = buckets_of(size, buckets)
    lane = iota((8, size), 1)
    dist = jnp.where(lane == 0, 0, size - lane)
    position = []
    for h in range(z.heads):
        row = jnp.zeros((8, size), F32)
        for b in sorted(set(number)):
            low, high = number.index(b), size - 1 - number[::-1].index(b)
            row = jnp.where((dist >= low) & (dist <= high), small_ref[h, b], row)
        full = jnp.broadcast_to(row[0:1], (size, size))
        position.append(pltpu.roll(full, 0, 1, stride=1, stride_axis=0))
    for h in range(z.heads):
        for u in range(z.mine):
            bias_ref[u, h] = position[h]
    block = 32
    for u in range(z.mine):
        user = member(z, plan_ref, table_pos, bal_pos * z.pair + mp_pos * z.mine + u)
        size_u = lens_ref[user]
        events = time_ref[pl.ds(user, 1), :]
        columns = jnp.broadcast_to(events, (size, size)).T

        for r in range(0, size, block):
            rows = slice(r, r + block)
            diff = jnp.abs(columns[rows] - events)
            column = iota((block, size), 1)
            valid = (column <= iota((block, size), 0) + r) & (column < size_u)
            for h in range(z.heads):
                term = jnp.zeros((block, size), F32)
                for b in range(tbuckets):
                    term = jnp.where(diff == b, small_ref[h, buckets + b], term)
                bias_ref[u, h, rows, :] = jnp.where(
                    valid, 0.5 * (bias_ref[u, h, rows, :] + term), FAR
                )


def silu(s):
    half = 0.5 * s
    return half + half * jnp.tanh(half)


def arrived(ref, sem):
    pltpu.make_async_copy(ref, ref, sem).wait()


def layer_kernel(
    z, load, group, n_weights, plan_ref, lens_ref, keep_ref, got_ref, gain_ref, out_gain_ref, bias_hbm, *refs
):
    weights = refs[:n_weights]
    own_out, give_out = refs[n_weights : n_weights + 2]
    (e_ref, w_ref, o_ref, emb_ref, x_ref, xn_ref, act_ref, y_ref, z_ref, bias_ref, sems) = refs[n_weights + 2 :]
    table_pos = lax.axis_index("table")
    bal_pos = lax.axis_index("bal")
    mp_pos = lax.axis_index("mp")
    width = x_ref.shape[1]
    copies = load(weights, e_ref, w_ref, o_ref, sems)
    copies.insert(2, [pltpu.make_async_copy(bias_hbm, bias_ref, sems.at[3])])
    for batch in copies:
        for c in batch:
            c.start()
    for u in range(z.mine):
        near = pl.multiple_of(u * z.length + mp_pos * z.half, z.half)
        far = pl.multiple_of(u * z.length + (1 - mp_pos) * z.half, z.half)
        rows = slice(u * z.half, (u + 1) * z.half)
        emb_ref[pl.ds(near, z.half), :] = keep_ref[rows, :]
        emb_ref[pl.ds(far, z.half), :] = got_ref[rows, :]
    arrived(e_ref, sems.at[0])
    tokens = z.mine * z.length
    block = 256
    for r in range(0, tokens, block):
        rows = slice(r, r + block)
        x = []
        for first in range(0, 2 * width, 2 * group):
            e = [e_ref[:, first + j * group : first + (j + 1) * group] for j in range(2)]
            x.append(dot(emb_ref[rows, :], jnp.concatenate(e, axis=0)))
        x = jnp.concatenate(x, axis=1).astype(BF)
        x_ref[rows, :] = x
        x = x.astype(F32)
        mean = jnp.mean(x, axis=1, keepdims=True)
        centred = x - mean
        var = jnp.mean(centred * centred, axis=1, keepdims=True)
        xn_ref[rows, :] = (centred * lax.rsqrt(var + epsilon) * gain_ref[...]).astype(BF)
    step = 256
    arrived(w_ref, sems.at[1])
    share = w_ref.shape[1] // 4
    for part in range(4):

        def project(nb, carry):
            cols = pl.ds(pl.multiple_of(nb * step, step), step)
            w = w_ref[:, part * share : (part + 1) * share, cols].reshape(width, step)
            s = dot(xn_ref[...], w)
            act_ref[part, :, cols] = silu(s).astype(BF)
            return carry

        lax.fori_loop(0, width // step, project, 0, unroll=True)
    arrived(bias_ref, sems.at[3])
    scale = 0.5 / math.sqrt(width // z.heads)
    size = width // z.heads
    for u in range(z.mine):
        user = member(z, plan_ref, table_pos, bal_pos * z.pair + mp_pos * z.mine + u)
        inverse = 1.0 / jnp.full((1, z.length), lens_ref[user], jnp.int32).astype(F32)
        rows = slice(u * z.length, (u + 1) * z.length)

        block = z.length // ROW_BLOCKS
        total = [jnp.zeros((block, 1), F32) for _ in range(ROW_BLOCKS)]
        square = [jnp.zeros((block, 1), F32) for _ in range(ROW_BLOCKS)]
        for h in range(z.heads):
            cols = slice(h * size, (h + 1) * size)
            for part in range(ROW_BLOCKS):
                first = u * z.length + part * block
                mine = slice(first, first + block)
                keys = slice(u * z.length, first + block)
                seen = (part + 1) * block
                s = dot_nt(act_ref[2, mine, cols], act_ref[3, keys, cols]) * scale
                s = s + bias_ref[u, h, part * block : seen, :seen]
                a = ((s + s * jnp.tanh(s)) * inverse[:, :seen]).astype(BF)
                y = dot(a, act_ref[1, keys, cols])
                y_ref[mine, cols] = y
                total[part] = total[part] + jnp.sum(y, axis=1, keepdims=True)
                square[part] = square[part] + jnp.sum(y * y, axis=1, keepdims=True)
        total, square = jnp.concatenate(total, 0), jnp.concatenate(square, 0)
        mean = total / width
        var = square / width - mean * mean
        factor = lax.rsqrt(var + epsilon)
        for h in range(z.heads):
            cols = slice(h * size, (h + 1) * size)
            normed = (y_ref[rows, cols] - mean) * factor * out_gain_ref[h : h + 1, :]
            z_ref[rows, cols] = (normed * act_ref[0, rows, cols].astype(F32)).astype(BF)
    arrived(o_ref, sems.at[2])
    out_cols = width // z.mp
    for which, ref in ((1 - mp_pos, give_out), (mp_pos, own_out)):
        for nb in range(out_cols // step):
            cols = pl.ds(pl.multiple_of(which * out_cols + nb * step, step), step)
            if group <= out_cols:
                first = which * 2 * out_cols + nb * step // group * 2 * group + nb * step % group
            else:
                first = which * out_cols + nb * step
            deep = o_ref.shape[0] // z.mp
            o = []
            for core in range(z.mp):
                for j in range(2):
                    lanes = pl.ds(pl.multiple_of(first + j * group, step), step)
                    o.append(o_ref[core * deep : (core + 1) * deep, lanes])
            term = dot(z_ref[...], jnp.concatenate(o, axis=0))
            ref[:, nb * step : (nb + 1) * step] = (
                term + x_ref[:, cols].astype(F32)
            ).astype(BF)


def swap(x, axis, size, k=1):
    return lax.ppermute(x, axis, [(i, (i + k) % size) for i in range(size)])


def cross(x, near_first):
    pairs = []
    for i in range(8):
        p, b, m = i // 4, i // 2 % 2, i % 2
        p, b = (p, 1 - b) if (m == 0) == near_first else (1 - p, b)
        pairs.append((i, (p * 2 + b) * 2 + m))
    return lax.ppermute(x, ("parts", "bal", "mp"), pairs)


def corner(x):
    return lax.ppermute(x, ("parts", "bal"), [(i, 3 - i) for i in range(4)])


def pack_kernel(e_ref, w_ref, o_ref, out_ref, sems):
    q = lax.axis_index("parts") * 2 + lax.axis_index("bal")
    m = lax.axis_index("mp")
    share = w_ref.shape[1] // 4
    cols = e_ref.shape[1]
    e_part = e_ref.shape[0] // 16
    o_part = o_ref.shape[0] // 8
    copies = []

    def add(src, dst):
        copies.append(pltpu.make_async_copy(src, dst, sems))

    for c in range(4):
        add(w_ref.at[c, at(q, share), :], out_ref.at[c * share : (c + 1) * share, :])
    first = 4 * share
    for j in range(2):
        lanes = slice(j * cols, (j + 1) * cols)
        add(e_ref.at[at(j * 8 + q * 2 + m, e_part), :], out_ref.at[first : first + e_part, lanes])
        add(
            o_ref.at[at(j * 4 + q, o_part), :],
            out_ref.at[first + e_part : first + e_part + o_part, lanes],
        )
    for c in copies:
        c.start()
    for c in copies:
        c.wait()


def merge_kernel(*refs):
    out_ref, sem = refs[4:]
    copies = [pltpu.make_async_copy(refs[i], out_ref.at[i], sem) for i in range(4)]
    for c in copies:
        c.start()
    for c in copies:
        c.wait()


def at(x, size):
    return pl.ds(pl.multiple_of(x * size, size), size)


def load_pieces(z):
    def load(refs, e_ref, w_ref, o_ref, sems):
        t, m = lax.axis_index("table"), lax.axis_index("mp")
        p, b = lax.axis_index("parts"), lax.axis_index("bal")
        e_own, w_own, o_own, w_near, o_near = refs[:5]
        share, cols = w_own.shape[2], w_own.shape[3]
        e_cols = e_own.shape[1]
        o_rows = o_own.shape[0]
        e_part = e_ref.shape[0] // 8
        o_part = o_rows // 8
        first = 4 * share
        along_b, along_p = p * 2 + 1 - b, (1 - p) * 2 + b
        one, two, rest = refs[5:7], refs[7:9], refs[9:]
        shards = (
            [ref.at[i] for i in range(4) for ref in one],
            [ref.at[i] for i in range(3) for ref in two] + list(rest[:2]),
            [ref.at[3] for ref in two] + list(rest[2:]),
        )
        pieces = []
        for k in range(1, z.n):
            source = lax.rem(t + z.n - k, z.n)
            block = shards[k - 1]
            for i in range(4):
                for core, ref in ((m, block[2 * i]), (1 - m, block[2 * i + 1])):
                    q = (
                        p * 2 + b,
                        jnp.where(core == 0, along_b, along_p),
                        jnp.where(core == 0, along_p, along_b),
                        (1 - p) * 2 + 1 - b,
                    )[i]
                    pieces.append((ref, source, q, core))
        groups = [[] for _ in range(3)]

        def add(g, src, dst):
            groups[g].append(pltpu.make_async_copy(src, dst, sems.at[g]))

        def half(t, j):
            return at(t * 2 + j, e_cols)

        e_rows, o_deep = e_ref.shape[0], o_rows // 2
        for j in range(2):
            add(0, e_own.at[j * e_rows : (j + 1) * e_rows, :], e_ref.at[:, half(t, j)])
        for ref, source, q, core in pieces:
            rows = at(q * 2 + core, e_part)
            add(0, ref.at[first : first + e_part, :], e_ref.at[rows, at(source, 2 * e_cols)])
        for core, w in ((m, w_own), (1 - m, w_near)):
            for c in range(4):
                rows = slice(c * share, (c + 1) * share)
                add(1, w.at[c], w_ref.at[at(t, 4), rows, at(core, cols)])
        for ref, source, q, core in pieces:
            add(1, ref.at[:first, :], w_ref.at[source * 4 + q, :, at(core, cols)])
        for core, o in ((m, o_own), (1 - m, o_near)):
            for j in range(2):
                rows = slice(j * o_deep, (j + 1) * o_deep)
                add(2, o.at[rows, :], o_ref.at[at(core, o_deep), half(t, j)])
        for ref, source, q, core in pieces:
            last = first + e_part + o_part
            rows = at(core * 4 + q, o_part)
            add(2, ref.at[first + e_part : last, :], o_ref.at[rows, at(source, 2 * e_cols)])
        return groups

    return load


def load_whole(refs, e_ref, w_ref, o_ref, sems):
    e, w, o = refs
    groups = [[], [], []]

    def add(g, src, dst):
        groups[g].append(pltpu.make_async_copy(src, dst, sems.at[g]))

    width, share = w_ref.shape[2], w_ref.shape[1] // 4
    e_rows, o_deep = e_ref.shape[0], o_ref.shape[0] // 2
    for j in range(2):
        lanes = slice(j * width, (j + 1) * width)
        add(0, e.at[j * e_rows : (j + 1) * e_rows, :], e_ref.at[:, lanes])
        for core in range(2):
            rows = slice((core * 2 + j) * o_deep, (core * 2 + j + 1) * o_deep)
            add(2, o.at[rows, :], o_ref.at[core * o_deep : (core + 1) * o_deep, lanes])
    for c in range(4):
        add(1, w.at[c], w_ref.at[:, c * share : (c + 1) * share, :])
    return groups


def blocks(w, count):
    return w.reshape(w.shape[0], count, w.shape[1] // count, w.shape[2])


def finish_kernel(own_ref, got_ref, out_ref):
    mp_pos = lax.axis_index("mp")
    tokens = own_ref.shape[0]
    out_ref[at(mp_pos, tokens), :] = own_ref[...]
    out_ref[at(1 - mp_pos, tokens), :] = got_ref[...]


def body(
    table_rows,
    row_scale,
    hist_ids,
    lengths,
    plan,
    time_bucket,
    embed_proj,
    in_gain,
    qkvu_proj,
    out_gain,
    out_proj,
    pos_bias,
    time_bias,
):
    axes = tuple(lax.axis_size(a) for a in ("table", "bal", "mp"))
    z = Sizes(axes, table_rows, hist_ids, lengths, pos_bias)
    width = in_gain.shape[0]
    mp_pos = lax.axis_index("mp")
    scale = row_scale.reshape(z.rows // 128, 128)
    send_rows = pl.pallas_call(
        functools.partial(send_kernel, z),
        out_shape=[jax.ShapeDtypeStruct((z.cap, z.width), BF)] * (z.n - 1),
        in_specs=[sspec(), vspec(), vspec(), vspec()],
        out_specs=[vspec()] * (z.n - 1),
        scratch_shapes=[pltpu.VMEM((z.rows, z.width), BF)],
        compiler_params=params(20),
        cost_estimate=cost(7),
        name="send_rows",
    )
    keep_rows = pl.pallas_call(
        functools.partial(keep_kernel, z),
        out_shape=[
            jax.ShapeDtypeStruct((z.tokens, z.width), BF),
            jax.ShapeDtypeStruct((z.tokens, (z.n - 1) * z.cap), BF),
        ],
        in_specs=[sspec(), vspec(), vspec(), vspec()],
        out_specs=[vspec()] * 2,
        scratch_shapes=[pltpu.VMEM((z.rows, z.width), BF)],
        compiler_params=params(20),
        cost_estimate=cost(7),
        name="keep_rows",
    )
    buckets, tbuckets = pos_bias.shape[1], time_bias.shape[1]
    make_bias = pl.pallas_call(
        functools.partial(bias_kernel, z, buckets=buckets, tbuckets=tbuckets),
        out_shape=jax.ShapeDtypeStruct((z.mine, z.heads, z.length, z.length), F32),
        in_specs=[sspec(), sspec(), sspec(), vspec()],
        out_specs=vspec(),
        compiler_params=params(14),
        cost_estimate=cost(7),
        name="bias",
    )
    place_rows = pl.pallas_call(
        functools.partial(place_kernel, z),
        out_shape=[jax.ShapeDtypeStruct((z.tokens // z.mp, z.width), BF)] * 2,
        in_specs=[vspec()] * (z.n + 1),
        out_specs=[vspec()] * 2,
        compiler_params=params(12),
        cost_estimate=cost(3),
        name="place_rows",
    )

    def both(x):
        other = swap(x, "mp", z.mp)
        return jnp.where(
            mp_pos == 0, jnp.concatenate([x, other], 0), jnp.concatenate([other, x], 0)
        )

    def biases(pos_bias, time_bias, out_gain):
        small = jnp.concatenate(
            [pos_bias, time_bias, out_gain.reshape(pos_bias.shape[0], -1)], axis=1
        )
        small = both(small)
        return small[:, : buckets + tbuckets], small[:, buckets + tbuckets :]

    if z.n == 4 and z.bal == 2 and lax.axis_size("parts") == 2:
        near = functools.partial(swap, axis="mp", size=2)
        hop = functools.partial(swap, axis="table", size=z.n)
        rows = qkvu_proj.shape[1] + z.width // 16 + out_proj.shape[0] // 8
        pack = pl.pallas_call(
            pack_kernel,
            out_shape=jax.ShapeDtypeStruct((rows, qkvu_proj.shape[2]), BF),
            in_specs=[pl.BlockSpec(memory_space=pltpu.HBM)] * 3,
            out_specs=vspec(),
            scratch_shapes=[pltpu.SemaphoreType.DMA],
            compiler_params=params(60),
            name="pack",
        )(embed_proj, qkvu_proj, out_proj)
        merge = pl.pallas_call(
            merge_kernel,
            out_shape=jax.ShapeDtypeStruct((4, rows, qkvu_proj.shape[2]), BF),
            in_specs=[pl.BlockSpec(memory_space=pl.ANY)] * 4,
            out_specs=vspec(),
            scratch_shapes=[pltpu.SemaphoreType.DMA],
            compiler_params=params(6),
            cost_estimate=cost(2),
            name="merge",
        )
        r1 = hop(pack)
        sent = send_rows(plan, hist_ids, table_rows, scale)
        w_near, o_near = near(qkvu_proj), near(out_proj)
        sent, small_in = fence(sent, (pos_bias, time_bias, out_gain))
        table, gains = biases(*small_in)
        r1, sent, table, w_near, o_near = fence(r1, sent, table, w_near, o_near)
        b1, a1 = cross(r1, False), cross(r1, True)
        got1 = swap(sent[0], "table", z.n, 1)
        r2 = hop(r1)
        bias = make_bias(table, plan, lengths, time_bucket)
        r1, a1, b1, r2, got1, bias, sent, plan1, gains = fence(
            r1, a1, b1, r2, got1, bias, sent, plan, gains
        )
        b2, a2, d1 = cross(r2, False), cross(r2, True), cross(b1, True)
        got3 = swap(sent[2], "table", z.n, 3)
        r3 = hop(r2)
        own, route = keep_rows(plan1, hist_ids, table_rows, scale)
        r1, a1, b1, d1, r2, a2, b2, r3, got3, own, route, sent = fence(
            r1, a1, b1, d1, r2, a2, b2, r3, got3, own, route, sent
        )
        a3, b3, d2 = cross(r3, True), cross(r3, False), cross(b2, True)
        got2 = swap(sent[1], "table", z.n, 2)
        chunk1 = merge(r1, a1, b1, d1)
        chunk2 = merge(r2, a2, b2, r3)
        a3, b3, d2, chunk1, chunk2, got2 = fence(a3, b3, d2, chunk1, chunk2, got2)
        near1 = near(chunk1)
        d3 = cross(b3, True)
        keep, give = place_rows(own, route, got1, got2, got3)
        back = near(give)
        near2 = near(chunk2)
        w_own, w_near = blocks(qkvu_proj, 4), blocks(w_near, 4)
        group = embed_proj.shape[1]
        weights = [embed_proj, w_own, out_proj, w_near, o_near, chunk1, near1, chunk2, near2]
        for v in (d2, a3, b3, d3):
            weights += [v, near(v)]
        load = load_pieces(z)
    else:
        table, gains = biases(pos_bias, time_bias, out_gain)
        bias = make_bias(table, plan, lengths, time_bucket)
        sent = send_rows(plan, hist_ids, table_rows, scale)
        got = [swap(s, "table", z.n, k + 1) for k, s in enumerate(sent)]
        own, route = keep_rows(plan, hist_ids, table_rows, scale)
        q_full = lax.all_gather(qkvu_proj, "table", axis=1, tiled=True)
        o_full = lax.all_gather(out_proj, "table", axis=1, tiled=True)
        weights = [
            lax.all_gather(embed_proj, "table", axis=1, tiled=True),
            blocks(lax.all_gather(q_full, "mp", axis=2, tiled=True), 16),
            lax.all_gather(o_full, "mp", axis=0, tiled=True),
        ]
        load, group = load_whole, width
        keep, give = place_rows(own, route, *got)
        back = swap(give, "mp", z.mp)

    tokens = z.mine * z.length
    out_cols = width // z.mp
    out_own, out_give = pl.pallas_call(
        functools.partial(layer_kernel, z, load, group, len(weights)),
        out_shape=[jax.ShapeDtypeStruct((tokens, out_cols), BF)] * 2,
        in_specs=[sspec(), sspec()]
        + [vspec()] * 4
        + [pl.BlockSpec(memory_space=pl.ANY)] * (1 + len(weights)),
        out_specs=[vspec()] * 2,
        scratch_shapes=[
            pltpu.VMEM((z.width // 2, 2 * width), BF),
            pltpu.VMEM((16, width // 4, width), BF),
            pltpu.VMEM((width // 2, 2 * width), BF),
            pltpu.VMEM((tokens, z.width), BF),
            pltpu.VMEM((tokens, width), BF),
            pltpu.VMEM((tokens, width), BF),
            pltpu.VMEM((4, tokens, width), BF),
            pltpu.VMEM((tokens, width), F32),
            pltpu.VMEM((tokens, width), BF),
            pltpu.VMEM(bias.shape, F32),
            pltpu.SemaphoreType.DMA((4,)),
        ],
        compiler_params=params(36),
        name="layer",
    )(plan, lengths, keep, back, in_gain.reshape(1, width), gains, bias, *weights)
    out_got = swap(out_give, "mp", z.mp)
    out = pl.pallas_call(
        finish_kernel,
        out_shape=jax.ShapeDtypeStruct((z.mp * tokens, out_cols), BF),
        in_specs=[vspec()] * 2,
        out_specs=vspec(),
        compiler_params=params(8),
        name="finish",
    )(out_own, out_got)
    return out.reshape(z.pair, z.length, out_cols)


def solution(mesh):
    return jax.shard_map(
        body,
        mesh=mesh,
        in_specs=(
            P("table", None),
            P("table"),
            P("parts", None),
            P(("parts", "table")),
            P("parts"),
            P(("parts", "table"), None),
            P(None, "table"),
            P(),
            P(None, "table", "mp"),
            P("mp"),
            P("mp", "table"),
            P("mp", None),
            P("mp", None),
        ),
        out_specs=P(("parts", "table", "bal"), None, "mp"),
        check_vma=False,
    )
```
